32 devices in a mesh: grp: 4 (over z), seq: 8 (over y, x, core).
Axes of the slice: x: 2, y: 2, z: 4, core: 2. Of those that a mesh axis runs over, the one named last changes fastest.
Arguments:
- tokens: bfloat16 [2, 4608, 2304], P(None, ('grp', 'seq')), may hold values from -8 to 8
- cotangent: bfloat16 [2, 4608, 2304], P(None, ('grp', 'seq')), may hold values from -6 to 6
- segments: int32 [2, 4608], P(None, 'grp'), may hold values from 0 to 8, as said below
- attn_in: float32 [2304, 4096], P(('grp', 'seq')), may hold values from -0.1388889 to 0.1388889
- attn_out: float32 [2304, 2048], P(('grp', 'seq')), may hold values from -0.125 to 0.125
- ffn_in: float32 [2304, 18432], P(('grp', 'seq')), may hold values from -0.125 to 0.125
- ffn_out: float32 [2304, 9216], P(('grp', 'seq')), may hold values from -0.0625 to 0.0625
- gains: float32 [4, 2304], P(None, ('grp', 'seq')), may hold values from 0.5 to 1.5
- attn_in_mom: float32 [2304, 4096], P(('grp', 'seq')), may hold values from -256 to 256
- attn_out_mom: float32 [2304, 2048], P(('grp', 'seq')), may hold values from -256 to 256
- ffn_in_mom: float32 [2304, 18432], P(('grp', 'seq')), may hold values from -256 to 256
- ffn_out_mom: float32 [2304, 9216], P(('grp', 'seq')), may hold values from -256 to 256
- gains_mom: float32 [4, 2304], P(None, ('grp', 'seq')), may hold values from -512 to 512
- attn_in_avg: float32 [2304, 4096], P(('grp', 'seq')), may hold values from -0.125 to 0.125
- attn_out_avg: float32 [2304, 2048], P(('grp', 'seq')), may hold values from -0.125 to 0.125
- ffn_in_avg: float32 [2304, 18432], P(('grp', 'seq')), may hold values from -0.125 to 0.125
- ffn_out_avg: float32 [2304, 9216], P(('grp', 'seq')), may hold values from -0.0625 to 0.0625
- gains_avg: float32 [4, 2304], P(None, ('grp', 'seq')), may hold values from 0.5 to 1.5
Outputs:
- output: bfloat16 [2, 4608, 2304], P(None, ('grp', 'seq'))
- input_grad: float32 [2, 4608, 2304], P(None, ('grp', 'seq'))
- attn_in_new: float32 [2304, 4096], P(('grp', 'seq'))
- attn_in_mom_new: float32 [2304, 4096], P(('grp', 'seq'))
- attn_in_avg_new: float32 [2304, 4096], P(('grp', 'seq'))
- attn_in_copy: bfloat16 [2304, 4096], P(('grp', 'seq'))
- attn_out_new: float32 [2304, 2048], P(('grp', 'seq'))
- attn_out_mom_new: float32 [2304, 2048], P(('grp', 'seq'))
- attn_out_avg_new: float32 [2304, 2048], P(('grp', 'seq'))
- attn_out_copy: bfloat16 [2304, 2048], P(('grp', 'seq'))
- ffn_in_new: float32 [2304, 18432], P(('grp', 'seq'))
- ffn_in_mom_new: float32 [2304, 18432], P(('grp', 'seq'))
- ffn_in_avg_new: float32 [2304, 18432], P(('grp', 'seq'))
- ffn_in_copy: bfloat16 [2304, 18432], P(('grp', 'seq'))
- ffn_out_new: float32 [2304, 9216], P(('grp', 'seq'))
- ffn_out_mom_new: float32 [2304, 9216], P(('grp', 'seq'))
- ffn_out_avg_new: float32 [2304, 9216], P(('grp', 'seq'))
- ffn_out_copy: bfloat16 [2304, 9216], P(('grp', 'seq'))
- gains_new: float32 [4, 2304], P(None, ('grp', 'seq'))
- gains_mom_new: float32 [4, 2304], P(None, ('grp', 'seq'))
- gains_avg_new: float32 [4, 2304], P(None, ('grp', 'seq'))
- gains_copy: bfloat16 [4, 2304], P(None, ('grp', 'seq'))
The draws below stay inside these ranges and needn't reach their ends.
Inputs may be any that keep to these rules, and one draw needn't show every extreme that they name: `segments`: in each group of 1152 rows the first 1024 rows are 0, the rest are 1 to 8 in rising order, each continuation one or more rows.
All inputs are finite; a program needn't handle non-finite values.
Results may differ from the reference program's by a relative error of at most 0.017.
Values may be sent and summed in bfloat16 or wider, within the bound.
No kernel may reach another device: no remote copies, remote signals or barrier semaphores. Data moves between devices by JAX's collectives and lax.ppermute only.
A program may use at most 384 MiB of HBM per device.

```python
import jax
import jax.numpy as jnp
from jax import lax

D = 2304
HEADS = 8
KV_HEADS = 4
HEAD = 256
FF = 9216
GROUP = 1152
PROMPT = 1024
CONTS = 8
MICRO = 2
CONTTOK = 128
TOKENS = 4608
QW = 2048
QKV = 4096
N_GRP = 4


def shared_direction(key):
    return jnp.clip(jax.random.normal(key, (D,), jnp.float32), -4.0, 4.0)


def draw_tokens(key, part):
    direction = shared_direction(key)
    key = jax.random.fold_in(key, 21)
    noise = jnp.clip(jax.random.normal(key, (MICRO, TOKENS, D), jnp.float32), -4.0, 4.0)
    return (noise + direction[None, None, :]).astype(jnp.bfloat16)


def draw_attn_in(key, part):
    direction = shared_direction(key)
    key = jax.random.fold_in(key, 22)
    noise_key, query_key, value_key, sign_key = jax.random.split(key, 4)
    noise = jnp.clip(jax.random.normal(noise_key, (D, QKV), jnp.float32), -5.0, 5.0) * D ** (-0.5)
    query_strength = jax.random.uniform(query_key, (HEADS,), jnp.float32, 10.0, 20.0)
    kv_strength = jax.random.uniform(value_key, (KV_HEADS,), jnp.float32, 10.0, 20.0)
    signs = (2 * jax.random.randint(sign_key, (KV_HEADS, HEAD), 0, 2) - 1).astype(jnp.float32)
    lanes = jnp.arange(HEAD, dtype=jnp.int32) % (HEAD // 2)
    slowest = (lanes >= HEAD // 2 - 3).astype(jnp.float32)
    pattern = signs * slowest[None, :]
    query_pattern = (query_strength[:, None] * jnp.repeat(pattern, HEADS // KV_HEADS, axis=0)).reshape(HEADS * HEAD)
    key_pattern = (kv_strength[:, None] * pattern).reshape(KV_HEADS * HEAD)
    planted = jnp.concatenate([query_pattern, key_pattern, jnp.zeros((KV_HEADS * HEAD,), jnp.float32)])
    return (noise + direction[:, None] * planted[None, :] / D).astype(jnp.float32)


def draw_segments(key, part):
    key = jax.random.fold_in(key, 11)
    group_count = MICRO * (TOKENS // GROUP)
    group_keys = jax.random.split(key, group_count)

    def one_group(group_key):
        cut_points = jnp.sort(jax.random.permutation(group_key, CONTTOK - 1)[:CONTS - 1].astype(jnp.int32) + 1)
        steps = jnp.arange(CONTTOK, dtype=jnp.int32)
        cont_ids = 1 + jnp.sum((steps[:, None] >= cut_points[None, :]).astype(jnp.int32), axis=1)
        return jnp.concatenate([jnp.zeros((PROMPT,), jnp.int32), cont_ids.astype(jnp.int32)])
    return jax.vmap(one_group)(group_keys).reshape(MICRO, TOKENS).astype(jnp.int32)


def block_levels(own_key, dims, pieces, smallest, top_value):
    level, own = 1.0, jax.random.fold_in(own_key, 6)
    for axis_at, blocks in pieces:
        steps = jnp.exp(jax.random.uniform(jax.random.fold_in(own, axis_at), (blocks,), jnp.float32, smallest / len(pieces), top_value / len(pieces)))
        level = level * jnp.repeat(steps, dims[axis_at] // blocks).reshape([-1 if axis == axis_at else 1 for axis in range(len(dims))])
    return level


def scatter_about(key, dims, deviation, bound, cuts=(), kind=jnp.bfloat16):
    result = deviation * jax.random.normal(key, dims, jnp.float32)
    if cuts:
        result = result * block_levels(key, dims, cuts, -0.22, 0.18)
    return jnp.clip(result, -bound, bound).astype(kind)


def setup_inputs(seed: int = 0) -> dict:
    streams_of = jax.random.split(jax.random.key(seed), 19)
    return {
        "tokens": draw_tokens(jax.random.fold_in(streams_of[18], 71), 0),
        "cotangent": scatter_about(streams_of[1], (MICRO, TOKENS, D), 1.0, 6.0, ((1, 32),)),
        "segments": draw_segments(jax.random.fold_in(streams_of[18], 71), 0),
        "attn_in": draw_attn_in(jax.random.fold_in(streams_of[18], 71), 0),
        "attn_out": scatter_about(streams_of[4], (D, QW), QW ** -0.5, 0.125, ((0, 32),), jnp.float32),
        "ffn_in": scatter_about(streams_of[5], (D, 2 * FF), D ** -0.5, 0.125, ((0, 32),), jnp.float32),
        "ffn_out": scatter_about(streams_of[6], (D, FF), FF ** -0.5, 0.0625, ((0, 32),), jnp.float32),
        "gains": jnp.clip(1.0 + 0.1 * jax.random.normal(streams_of[7], (4, D), jnp.float32), 0.5, 1.5),
        "attn_in_mom": scatter_about(streams_of[8], (D, QKV), (0.5 * (MICRO * TOKENS) ** 0.5), 256.0, ((0, 32),), jnp.float32),
        "attn_out_mom": scatter_about(streams_of[9], (D, QW), (0.5 * (MICRO * TOKENS) ** 0.5), 256.0, ((0, 32),), jnp.float32),
        "ffn_in_mom": scatter_about(streams_of[10], (D, 2 * FF), (0.5 * (MICRO * TOKENS) ** 0.5), 256.0, ((0, 32),), jnp.float32),
        "ffn_out_mom": scatter_about(streams_of[11], (D, FF), (0.5 * (MICRO * TOKENS) ** 0.5), 256.0, ((0, 32),), jnp.float32),
        "gains_mom": scatter_about(streams_of[12], (4, D), ((MICRO * TOKENS) ** 0.5), 512.0, ((1, 32),), jnp.float32),
        "attn_in_avg": scatter_about(streams_of[13], (D, QKV), D ** -0.5, 0.125, ((0, 32),), jnp.float32),
        "attn_out_avg": scatter_about(streams_of[14], (D, QW), QW ** -0.5, 0.125, ((0, 32),), jnp.float32),
        "ffn_in_avg": scatter_about(streams_of[15], (D, 2 * FF), D ** -0.5, 0.125, ((0, 32),), jnp.float32),
        "ffn_out_avg": scatter_about(streams_of[16], (D, FF), FF ** -0.5, 0.0625, ((0, 32),), jnp.float32),
        "gains_avg": jnp.clip(1.0 + 0.1 * jax.random.normal(streams_of[17], (4, D), jnp.float32), 0.5, 1.5),
    }


@jax.custom_vjp
def low(v):
    return lax.optimization_barrier(v.astype(jnp.bfloat16)).astype(jnp.float32)

@jax.custom_vjp
def low_back(v):
    return v

def low_keep(v):
    return (low(v), None)

def low_pass(kept, grad):
    return (grad,)

def back_keep(v):
    return (v, None)

def back_low(kept, grad):
    return (low(grad),)
low.defvjp(low_keep, low_pass)
low_back.defvjp(back_keep, back_low)
eps_norm = 1e-06
soft_cap = 50.0
momentum_decay = 0.5
average_decay = 0.5
weight_rate = 0.03
gain_rate = 0.2
rope_base = 10000.0

def matmul(left, right):
    return jnp.dot(left, right, precision=lax.Precision.HIGHEST, preferred_element_type=jnp.float32)

def matmul_t(left, right):
    return lax.dot_general(left, right, (((1,), (1,)), ((), ())), precision=lax.Precision.HIGHEST, preferred_element_type=jnp.float32)

def scaled(field, gain):
    return field * lax.rsqrt(lax.optimization_barrier(jnp.mean(field * field, axis=-1, keepdims=True)) + eps_norm) * gain

def place_tokens(seg_group, own_segment, row_index):
    levels = jnp.arange(CONTS + 1, dtype=jnp.int32)
    before = lax.optimization_barrier(jnp.sum((seg_group[None, :] < levels[:, None]).astype(jnp.int32), axis=1))
    seg_start = lax.optimization_barrier(jnp.sum(jnp.where(own_segment[:, None] == levels[None, :], before[None, :], 0), axis=1)).astype(jnp.int32)
    return (row_index - seg_start + jnp.where(own_segment > 0, PROMPT, 0)).astype(jnp.int32)

def rotate(field, positions):
    half = field.shape[-1] // 2
    freqs = rope_base ** (-jnp.arange(half, dtype=jnp.float32) * 2.0 / field.shape[-1])
    angles = positions.astype(jnp.float32)[:, None] * freqs[None, :]
    cosine = jnp.cos(angles)[:, None, :]
    sine = jnp.sin(angles)[:, None, :]
    first_half = field[..., :half]
    second_half = field[..., half:]
    return jnp.concatenate([first_half * cosine - second_half * sine, second_half * cosine + first_half * sine], axis=-1)

def glu_part(gate, upper):
    return jax.nn.gelu(gate, approximate=True) * upper

def group_pass(inputs, seg_group, w_qkv, w_o, w_gu, w_d, gain_vals):
    row_index = jnp.arange(GROUP, dtype=jnp.int32)
    positions = place_tokens(seg_group, seg_group, row_index)
    visible = (row_index[None, :] <= row_index[:, None]) & ((seg_group[None, :] == 0) | (seg_group[None, :] == seg_group[:, None]))
    query_width = HEADS * HEAD
    kv_width = KV_HEADS * HEAD
    normed_one = low(scaled(inputs, gain_vals[0]))
    projected = low_back(matmul(normed_one, w_qkv))
    queries = low(rotate(projected[:, :query_width].reshape(GROUP, HEADS, HEAD), positions))
    key_heads = low(rotate(projected[:, query_width:query_width + kv_width].reshape(GROUP, KV_HEADS, HEAD), positions))
    value_heads = low(projected[:, query_width + kv_width:].reshape(GROUP, KV_HEADS, HEAD))
    queries = queries.reshape(GROUP, KV_HEADS, HEADS // KV_HEADS, HEAD)
    raw_scores = low_back(jnp.einsum('tgrd,kgd->grtk', queries, key_heads, precision=lax.Precision.HIGHEST) * HEAD ** (-0.5))
    capped = jnp.where(visible[None, None], soft_cap * jnp.tanh(raw_scores / soft_cap), -1e+30)
    attention = low(jax.nn.softmax(capped, axis=-1))
    mixed_heads = jnp.einsum('grtk,kgd->tgrd', attention, value_heads, precision=lax.Precision.HIGHEST).reshape(GROUP, query_width)
    mixed_heads = low(low_back(mixed_heads))
    branch = low_back(matmul_t(mixed_heads, w_o))
    middle = inputs + scaled(branch, gain_vals[1])
    normed_three = low(scaled(middle, gain_vals[2]))
    gate_up = low_back(matmul(normed_three, w_gu))
    hidden = low(glu_part(gate_up[:, :FF], gate_up[:, FF:]))
    ffn_branch = low_back(matmul_t(hidden, w_d))
    return middle + scaled(ffn_branch, gain_vals[3])

def renew(weight, moment, average, gradient, step_rate):
    moment_new = momentum_decay * moment + gradient
    weight_new = weight - step_rate * (gradient + momentum_decay * moment_new)
    average_new = average_decay * average + (1.0 - average_decay) * weight_new
    return (weight_new, moment_new, average_new, weight_new.astype(jnp.bfloat16))

def reference(tokens, cotangent, segments, attn_in, attn_out, ffn_in, ffn_out, gains, attn_in_mom, attn_out_mom, ffn_in_mom, ffn_out_mom, gains_mom, attn_in_avg, attn_out_avg, ffn_in_avg, ffn_out_avg, gains_avg):
    group_count = MICRO * N_GRP
    inputs = tokens.astype(jnp.float32).reshape(group_count, GROUP, D)
    seg_rows = segments.reshape(group_count, GROUP)

    def forward(layer_in, wa_in, wa_out, wf_in, wf_out, gain_all):
        low_weights = (low(wa_in), low(wa_out), low(wf_in), low(wf_out), low(gain_all))
        group_step = jax.checkpoint(lambda member: group_pass(member[0], member[1], *low_weights))
        return lax.map(group_step, (layer_in, seg_rows))
    outputs, pull_back = jax.vjp(forward, inputs, attn_in, attn_out, ffn_in, ffn_out, gains)
    gradients = pull_back(cotangent.astype(jnp.float32).reshape(group_count, GROUP, D))
    token_total = MICRO * TOKENS
    rate_mat = weight_rate * token_total ** (-0.5)
    rate_gain = gain_rate * token_total ** (-0.5)
    qkv_new, qkv_mom, qkv_avg, qkv_copy = renew(attn_in, attn_in_mom, attn_in_avg, gradients[1], rate_mat)
    out_new, out_mom, out_avg, out_copy = renew(attn_out, attn_out_mom, attn_out_avg, gradients[2], rate_mat)
    gu_new, gu_mom, gu_avg, gu_copy = renew(ffn_in, ffn_in_mom, ffn_in_avg, gradients[3], rate_mat)
    down_new, down_mom, down_avg, down_copy = renew(ffn_out, ffn_out_mom, ffn_out_avg, gradients[4], rate_mat)
    gain_new, gain_mom, gain_avg, gain_copy = renew(gains, gains_mom, gains_avg, gradients[5], rate_gain)
    layer_out = outputs.reshape(MICRO, TOKENS, D).astype(jnp.bfloat16)
    layer_grad = gradients[0].reshape(MICRO, TOKENS, D)
    return (layer_out, layer_grad, qkv_new, qkv_mom, qkv_avg, qkv_copy, out_new, out_mom, out_avg, out_copy, gu_new, gu_mom, gu_avg, gu_copy, down_new, down_mom, down_avg, down_copy, gain_new, gain_mom, gain_avg, gain_copy)
```

```python
import jax
import jax.numpy as jnp
from jax import lax
from jax.sharding import PartitionSpec as P

HEADS = 8
KV_HEADS = 4
HEAD = 256
PROMPT = 1024
CONTS = 8


eps_norm = 1e-06
soft_cap = 50.0
momentum_decay = 0.5
average_decay = 0.5
weight_rate = 0.03
gain_rate = 0.2
rope_base = 10000.0


def scaled(field, gain):
    return field * lax.rsqrt(jnp.mean(field * field, axis=-1, keepdims=True) + eps_norm) * gain


def place_tokens(seg_group, own_segment, row_index):
    levels = jnp.arange(CONTS + 1, dtype=jnp.int32)
    before = jnp.sum((seg_group[None, :] < levels[:, None]).astype(jnp.int32), axis=1)
    seg_start = jnp.sum(
        jnp.where(own_segment[:, None] == levels[None, :], before[None, :], 0), axis=1
    )
    return row_index - seg_start + jnp.where(own_segment > 0, PROMPT, 0)


def rotate(field, positions):
    half = field.shape[-1] // 2
    freqs = rope_base ** (-jnp.arange(half, dtype=jnp.float32) * 2.0 / field.shape[-1])
    angles = positions.astype(jnp.float32)[:, None] * freqs[None, :]
    cosine = jnp.cos(angles)[:, None, :]
    sine = jnp.sin(angles)[:, None, :]
    first_half = field[..., :half]
    second_half = field[..., half:]
    return jnp.concatenate(
        [first_half * cosine - second_half * sine, second_half * cosine + first_half * sine],
        axis=-1,
    )


def glu_part(gate, upper):
    return jax.nn.gelu(gate, approximate=True) * upper


def contract_rows(left, right):
    return lax.dot_general(
        left, right, (((0,), (0,)), ((), ())), preferred_element_type=jnp.float32
    )


def contract_cols(left, right):
    return lax.dot_general(
        left, right, (((1,), (1,)), ((), ())), preferred_element_type=jnp.float32
    )


def renew(weight, moment, average, gradient, step_rate):
    moment_new = momentum_decay * moment + gradient
    weight_new = weight - step_rate * (gradient + momentum_decay * moment_new)
    average_new = average_decay * average + (1.0 - average_decay) * weight_new
    return (weight_new, moment_new, average_new, weight_new.astype(jnp.bfloat16))


def by_rows(
    tokens,
    cotangent,
    segments,
    attn_in,
    attn_out,
    ffn_in,
    ffn_out,
    gains,
    attn_in_mom,
    attn_out_mom,
    ffn_in_mom,
    ffn_out_mom,
    gains_mom,
    attn_in_avg,
    attn_out_avg,
    ffn_in_avg,
    ffn_out_avg,
    gains_avg,
):
    micro_count = tokens.shape[0]
    local_rows = tokens.shape[1]
    all_rows = micro_count * local_rows
    model_width = tokens.shape[2]
    row_offset = lax.axis_index("seq") * local_rows
    row_index = row_offset + jnp.arange(local_rows, dtype=jnp.int32)
    key_index = jnp.arange(segments.shape[1], dtype=jnp.int32)
    query_width = HEADS * HEAD
    kv_width = KV_HEADS * HEAD
    share = HEADS // KV_HEADS
    ffn_width = ffn_out.shape[1]
    own_rows = ffn_in.shape[0]
    score_scale = HEAD ** (-0.5)
    own_segments = lax.dynamic_slice_in_dim(segments, row_offset, local_rows, 1)
    positions = jax.vmap(
        lambda seg_group, own_segment: place_tokens(seg_group, own_segment, row_index)
    )(segments, own_segments).reshape(all_rows)
    visible = (key_index[None, None, :] <= row_index[None, :, None]) & (
        (segments[:, None, :] == 0) | (segments[:, None, :] == own_segments[:, :, None])
    )
    inputs = tokens.astype(jnp.float32).reshape(all_rows, model_width)
    w_qkv, w_o, gain_low = (
        lax.all_gather(attn_in.astype(jnp.bfloat16), ("grp", "seq"), axis=0, tiled=True),
        lax.all_gather(attn_out.astype(jnp.bfloat16), ("grp", "seq"), axis=0, tiled=True),
        lax.all_gather(gains.astype(jnp.bfloat16), ("grp", "seq"), axis=1, tiled=True),
    )
    gain_vals = gain_low.astype(jnp.float32)
    normed_one, norm_one_back = jax.vjp(scaled, inputs, gain_vals[0])
    normed_one = normed_one.astype(jnp.bfloat16)
    projected = jnp.dot(normed_one, w_qkv, preferred_element_type=jnp.float32)
    query_rot, query_back = jax.vjp(
        lambda field: rotate(field, positions),
        projected[:, :query_width].reshape(all_rows, HEADS, HEAD),
    )
    key_rot, key_back = jax.vjp(
        lambda field: rotate(field, positions),
        projected[:, query_width : query_width + kv_width].reshape(all_rows, KV_HEADS, HEAD),
    )
    query_low = query_rot.astype(jnp.bfloat16).reshape(
        micro_count, local_rows, KV_HEADS, share, HEAD
    )
    key_low = key_rot.astype(jnp.bfloat16).reshape(micro_count, local_rows, kv_width)
    value_low = (
        projected[:, query_width + kv_width :]
        .astype(jnp.bfloat16)
        .reshape(micro_count, local_rows, kv_width)
    )
    group_key_rows, group_values = (
        lax.all_gather(key_low, "seq", axis=1, tiled=True),
        lax.all_gather(value_low, "seq", axis=1, tiled=True),
    )
    group_key_rows = group_key_rows.reshape(micro_count, -1, KV_HEADS, HEAD)
    group_values = group_values.reshape(micro_count, -1, KV_HEADS, HEAD)

    def probabilities(raw_scores):
        capped = jnp.where(
            visible[:, None, None], soft_cap * jnp.tanh(raw_scores / soft_cap), -1e30
        )
        return jax.nn.softmax(capped, axis=-1)

    raw_scores = (
        jnp.einsum(
            "mtgrd,mkgd->mgrtk", query_low, group_key_rows, preferred_element_type=jnp.float32
        )
        * score_scale
    )
    attention, attention_back = jax.vjp(probabilities, raw_scores)
    attention_low = attention.astype(jnp.bfloat16)
    mixed_heads = jnp.einsum(
        "mgrtk,mkgd->mtgrd", attention_low, group_values, preferred_element_type=jnp.float32
    )
    mixed_low = mixed_heads.reshape(all_rows, query_width).astype(jnp.bfloat16)
    branch = contract_cols(mixed_low, w_o)
    normed_two, norm_two_back = jax.vjp(scaled, branch, gain_vals[1])
    middle = inputs + normed_two
    normed_three, norm_three_back = jax.vjp(scaled, middle, gain_vals[2])
    normed_three = normed_three.astype(jnp.bfloat16)
    grad_top = cotangent.astype(jnp.float32).reshape(all_rows, model_width)
    seq_count = lax.axis_size("seq")
    grp_count = lax.axis_size("grp")
    slice_width = ffn_width // seq_count
    stacked = jnp.concatenate(
        [
            ffn_in.astype(jnp.bfloat16).reshape(own_rows, 2, seq_count, slice_width),
            ffn_out.astype(jnp.bfloat16).reshape(own_rows, 1, seq_count, slice_width),
        ],
        axis=1,
    )
    spread = jnp.broadcast_to(
        stacked[:, :, None], (own_rows, 3, grp_count, seq_count, slice_width)
    ).reshape(own_rows, 3, grp_count * seq_count, slice_width)
    w_cols = lax.all_to_all(
        spread, ("grp", "seq"), split_axis=2, concat_axis=0, tiled=True
    ).reshape(model_width, 3, slice_width)
    w_gu_cols = w_cols[:, :2].reshape(model_width, 2 * slice_width)
    w_d_cols = w_cols[:, 2]
    norm_rows = lax.all_gather(normed_three, "seq", axis=0, tiled=True)
    gate_up = jnp.dot(norm_rows, w_gu_cols, preferred_element_type=jnp.float32)
    hidden, glu_back = jax.vjp(glu_part, gate_up[:, :slice_width], gate_up[:, slice_width:])
    hidden = hidden.astype(jnp.bfloat16)
    ffn_branch = lax.psum_scatter(
        contract_cols(hidden, w_d_cols), "seq", scatter_dimension=0, tiled=True
    )
    normed_four, norm_four_back = jax.vjp(scaled, ffn_branch, gain_vals[3])
    layer_out = (
        (middle + normed_four).astype(jnp.bfloat16).reshape(micro_count, local_rows, model_width)
    )
    d_ffn, d_gain_four = norm_four_back(grad_top)
    d_ffn_all = lax.all_gather(d_ffn.astype(jnp.bfloat16), "seq", axis=0, tiled=True)
    d_hidden = jnp.dot(d_ffn_all, w_d_cols, preferred_element_type=jnp.float32)
    grad_d_cols = contract_rows(d_ffn_all, hidden)
    d_gate, d_upper = glu_back(d_hidden)
    d_gate_up = jnp.concatenate([d_gate, d_upper], axis=1).astype(jnp.bfloat16)
    grad_gu_cols = contract_rows(norm_rows, d_gate_up)
    d_normed_three = lax.psum_scatter(
        contract_cols(d_gate_up, w_gu_cols), "seq", scatter_dimension=0, tiled=True
    )
    local_grads = jnp.concatenate(
        [grad_gu_cols.reshape(model_width, 2, slice_width), grad_d_cols[:, None, :]], axis=1
    ).reshape(model_width, 3, 1, slice_width)
    returned = lax.all_to_all(
        local_grads.astype(jnp.bfloat16), ("grp", "seq"), split_axis=0, concat_axis=2, tiled=True
    ).astype(local_grads.dtype)
    grad_ffn = jnp.sum(
        returned.reshape(own_rows, 3, grp_count, seq_count, slice_width), axis=2
    ).reshape(own_rows, 3 * ffn_width)
    d_middle_norm, d_gain_three = norm_three_back(d_normed_three)
    d_middle = grad_top + d_middle_norm
    sum_gu = grad_ffn[:, : 2 * ffn_width]
    sum_down = grad_ffn[:, 2 * ffn_width :]
    d_branch, d_gain_two = norm_two_back(d_middle)
    d_branch_low = d_branch.astype(jnp.bfloat16)
    grad_out = contract_rows(d_branch_low, mixed_low)
    d_mixed = jnp.dot(d_branch_low, w_o, preferred_element_type=jnp.float32)
    d_mixed_low = d_mixed.astype(jnp.bfloat16).reshape(
        micro_count, local_rows, KV_HEADS, share, HEAD
    )
    d_attention = jnp.einsum(
        "mtgrd,mkgd->mgrtk", d_mixed_low, group_values, preferred_element_type=jnp.float32
    )
    (d_raw,) = attention_back(d_attention)
    d_raw_low = d_raw.astype(jnp.bfloat16)
    d_query = (
        jnp.einsum(
            "mgrtk,mkgd->mtgrd", d_raw_low, group_key_rows, preferred_element_type=jnp.float32
        )
        * score_scale
    )
    d_group_keys = (
        jnp.einsum("mgrtk,mtgrd->mkgd", d_raw_low, query_low, preferred_element_type=jnp.float32)
        * score_scale
    )
    d_group_values = jnp.einsum(
        "mgrtk,mtgrd->mkgd", attention_low, d_mixed_low, preferred_element_type=jnp.float32
    )
    d_keys, d_values = (
        lax.psum_scatter(
            d_group_keys.reshape(micro_count, -1, kv_width).astype(jnp.bfloat16),
            "seq",
            scatter_dimension=1,
            tiled=True,
        ).astype(jnp.float32),
        lax.psum_scatter(
            d_group_values.reshape(micro_count, -1, kv_width).astype(jnp.bfloat16),
            "seq",
            scatter_dimension=1,
            tiled=True,
        ).astype(jnp.float32),
    )
    (d_query_raw,) = query_back(d_query.reshape(all_rows, HEADS, HEAD))
    (d_key_raw,) = key_back(d_keys.reshape(all_rows, KV_HEADS, HEAD))
    d_projected = jnp.concatenate(
        [
            d_query_raw.reshape(all_rows, query_width),
            d_key_raw.reshape(all_rows, kv_width),
            d_values.reshape(all_rows, kv_width),
        ],
        axis=1,
    ).astype(jnp.bfloat16)
    grad_qkv = contract_rows(normed_one, d_projected)
    d_normed_one = contract_cols(d_projected, w_qkv)
    d_input_norm, d_gain_one = norm_one_back(d_normed_one)
    layer_grad = (d_middle + d_input_norm).reshape(micro_count, local_rows, model_width)
    d_gains = jnp.stack([d_gain_one, d_gain_two, d_gain_three, d_gain_four])
    part_qkv, part_out, part_gain = (
        lax.psum_scatter(
            grad_qkv.astype(jnp.bfloat16), "grp", scatter_dimension=0, tiled=True
        ).astype(jnp.float32),
        lax.psum_scatter(
            grad_out.astype(jnp.bfloat16), "grp", scatter_dimension=0, tiled=True
        ).astype(jnp.float32),
        lax.psum_scatter(
            d_gains.astype(jnp.bfloat16), "grp", scatter_dimension=1, tiled=True
        ).astype(jnp.float32),
    )
    sum_qkv, sum_out, sum_gain = (
        lax.psum_scatter(
            part_qkv.astype(jnp.bfloat16), "seq", scatter_dimension=0, tiled=True
        ).astype(jnp.float32),
        lax.psum_scatter(
            part_out.astype(jnp.bfloat16), "seq", scatter_dimension=0, tiled=True
        ).astype(jnp.float32),
        lax.psum_scatter(
            part_gain.astype(jnp.bfloat16), "seq", scatter_dimension=1, tiled=True
        ).astype(jnp.float32),
    )
    token_total = micro_count * local_rows * lax.axis_size(("grp", "seq"))
    rate_mat = weight_rate * token_total ** (-0.5)
    rate_gain = gain_rate * token_total ** (-0.5)
    qkv_new, qkv_mom, qkv_avg, qkv_copy = renew(
        attn_in, attn_in_mom, attn_in_avg, sum_qkv, rate_mat
    )
    out_new, out_mom, out_avg, out_copy = renew(
        attn_out, attn_out_mom, attn_out_avg, sum_out, rate_mat
    )
    gu_new, gu_mom, gu_avg, gu_copy = renew(ffn_in, ffn_in_mom, ffn_in_avg, sum_gu, rate_mat)
    down_new, down_mom, down_avg, down_copy = renew(
        ffn_out, ffn_out_mom, ffn_out_avg, sum_down, rate_mat
    )
    gain_new, gain_mom, gain_avg, gain_copy = renew(
        gains, gains_mom, gains_avg, sum_gain, rate_gain
    )
    return (
        layer_out,
        layer_grad,
        qkv_new,
        qkv_mom,
        qkv_avg,
        qkv_copy,
        out_new,
        out_mom,
        out_avg,
        out_copy,
        gu_new,
        gu_mom,
        gu_avg,
        gu_copy,
        down_new,
        down_mom,
        down_avg,
        down_copy,
        gain_new,
        gain_mom,
        gain_avg,
        gain_copy,
    )


def permute(field, offset):
    count = lax.axis_size("seq")
    return lax.ppermute(field, "seq", [(i, i ^ offset) for i in range(count)])


def offset_bits():
    return [1 << bit for bit in range(1, lax.axis_size("seq").bit_length() - 1)]


def gather_pieces(field):
    half = field.shape[0] // 2
    bits = offset_bits()
    sides = [({0: field[:half]}, bits), ({0: field[half:]}, bits[::-1])]
    for step in range(len(bits)):
        for have, order in sides:
            bit = order[step]
            have.update({at | bit: permute(block, bit) for at, block in list(have.items())})
    for have, _ in sides:
        have.update({at | 1: permute(block, 1) for at, block in list(have.items())})
    count = lax.axis_size("seq")
    return jnp.concatenate([have[at] for at in range(count) for have, _ in sides], axis=0)


def add_low(left, right):
    return (left.astype(jnp.float32) + right.astype(jnp.float32)).astype(jnp.bfloat16)


def sum_pieces(field):
    count = lax.axis_size("seq")
    rows = field.shape[0] // count
    half = rows // 2
    bits = offset_bits()
    blocks = [field[at * rows : (at + 1) * rows] for at in range(count)]
    pairs = {
        at: add_low(blocks[at], permute(blocks[at | 1], 1)) for at in range(0, count, 2)
    }
    sides = [
        ({at: block[:half] for at, block in pairs.items()}, bits[::-1]),
        ({at: block[half:] for at, block in pairs.items()}, bits),
    ]
    for step in range(len(bits)):
        last = step == len(bits) - 1
        sides = [
            (
                {
                    at: (jnp.add if last else add_low)(
                        *(
                            part.astype(jnp.float32)
                            for part in (block, permute(have[at | order[step]], order[step]))
                        )
                    )
                    for at, block in have.items()
                    if not at & order[step]
                },
                order,
            )
            for have, order in sides
        ]
    return jnp.concatenate([have[0] for have, _ in sides], axis=0)


def swap_order(field):
    count = field.shape[0]
    bits = count.bit_length() - 1
    index = lax.axis_index("seq")
    split = field.reshape((2,) * bits + field.shape[1:])
    for bit in range(bits):
        axis = bits - 1 - bit
        split = jnp.where((index >> bit) & 1 == 1, jnp.flip(split, axis), split)
    return split.reshape(field.shape)


def spread_columns(field):
    rows, _, columns = field.shape
    moved = lax.all_to_all(
        field.astype(jnp.bfloat16).transpose(1, 0, 2), "seq", split_axis=0, concat_axis=0, tiled=True
    )
    return moved.reshape(-1, columns)


def gather_planes(field):
    return lax.all_gather(field, "grp", axis=0, tiled=True)


def sum_planes(field):
    part = lax.psum_scatter(
        field.astype(jnp.bfloat16), "grp", scatter_dimension=0, tiled=True
    )
    count = lax.axis_size("seq")
    moved = lax.all_to_all(
        part.reshape(count, -1, field.shape[1]), "seq", split_axis=0, concat_axis=0, tiled=True
    )
    return moved.transpose(1, 0, 2).astype(jnp.float32)


def by_heads(
    tokens,
    cotangent,
    segments,
    attn_in,
    attn_out,
    ffn_in,
    ffn_out,
    gains,
    attn_in_mom,
    attn_out_mom,
    ffn_in_mom,
    ffn_out_mom,
    gains_mom,
    attn_in_avg,
    attn_out_avg,
    ffn_in_avg,
    ffn_out_avg,
    gains_avg,
):
    micro_count, local_rows, model_width = tokens.shape
    all_rows = micro_count * local_rows
    seq_count = lax.axis_size("seq")
    grp_count = lax.axis_size("grp")
    device_count = seq_count * grp_count
    group_rows = segments.shape[1]
    own_rows = ffn_in.shape[0]
    ffn_width = ffn_out.shape[1]
    slice_width = ffn_width // seq_count
    chunks = 3
    chunk_width = slice_width // chunks
    score_scale = HEAD ** (-0.5)
    core = lax.axis_index("seq") % 2
    key_core = core == 0

    qkv_cols = jnp.concatenate(
        [
            attn_in[:, : HEADS * HEAD].reshape(own_rows, HEADS, HEAD),
            attn_in[:, HEADS * HEAD :]
            .reshape(own_rows, 2, KV_HEADS, HEAD)
            .transpose(0, 2, 1, 3)
            .reshape(own_rows, HEADS, HEAD),
        ],
        axis=2,
    )
    w_qkv = gather_planes(spread_columns(qkv_cols))
    all_gains = lax.all_to_all(
        jnp.broadcast_to(gains.astype(jnp.bfloat16)[None], (device_count,) + gains.shape),
        ("grp", "seq"),
        split_axis=0,
        concat_axis=0,
        tiled=True,
    )
    gain_vals = all_gains.transpose(1, 0, 2).reshape(4, model_width).astype(jnp.float32)
    token_pieces = gather_pieces(tokens.reshape(all_rows, model_width))
    w_o = gather_planes(spread_columns(attn_out.reshape(own_rows, HEADS, HEAD)))
    gu_split = ffn_in.reshape(own_rows, 2, seq_count, chunks, chunk_width)
    w_gu_chunks = [
        gather_planes(
            spread_columns(
                gu_split[:, :, :, at].transpose(0, 2, 1, 3).reshape(own_rows, seq_count, 2 * chunk_width)
            )
        )
        for at in range(chunks)
    ]
    w_d = gather_planes(spread_columns(ffn_out.reshape(own_rows, seq_count, slice_width)))

    row_index = jnp.arange(group_rows, dtype=jnp.int32)
    positions = jax.vmap(lambda seg: place_tokens(seg, seg, row_index))(segments)
    visible = (row_index[None, None, :] <= row_index[None, :, None]) & (
        (segments[:, None, :] == 0) | (segments[:, None, :] == segments[:, :, None])
    )
    flat_positions = positions.reshape(-1)
    kv_positions = jnp.where(key_core, flat_positions, 0)

    def to_groups(field):
        blocks = swap_order(field.reshape(seq_count, all_rows, -1))
        return (
            blocks.reshape(seq_count, micro_count, local_rows, -1)
            .transpose(1, 0, 2, 3)
            .reshape(micro_count * group_rows, -1)
        )

    def from_groups(field):
        blocks = (
            field.reshape(micro_count, seq_count, local_rows, -1)
            .transpose(1, 0, 2, 3)
            .reshape(seq_count, all_rows, -1)
        )
        return swap_order(blocks).reshape(seq_count * all_rows, -1)

    normed_one = scaled(token_pieces.astype(jnp.float32), gain_vals[0]).astype(jnp.bfloat16)
    projected = to_groups(jnp.dot(normed_one, w_qkv, preferred_element_type=jnp.float32))
    query_rot, query_back = jax.vjp(
        lambda field: rotate(field[:, None], flat_positions)[:, 0], projected[:, :HEAD]
    )
    kv_rot, kv_back = jax.vjp(
        lambda field: rotate(field[:, None], kv_positions)[:, 0], projected[:, HEAD:]
    )
    queries = query_rot.astype(jnp.bfloat16).reshape(micro_count, group_rows, HEAD)
    kv_own = kv_rot.astype(jnp.bfloat16)
    kv_other = permute(kv_own, 1)
    keys = jnp.where(key_core, kv_own, kv_other).reshape(micro_count, group_rows, HEAD)
    values = jnp.where(key_core, kv_other, kv_own).reshape(micro_count, group_rows, HEAD)

    def probabilities(raw_scores):
        capped = jnp.where(visible, soft_cap * jnp.tanh(raw_scores / soft_cap), -1e30)
        return jax.nn.softmax(capped, axis=-1)

    raw_scores = (
        jnp.einsum("mtd,mkd->mtk", queries, keys, preferred_element_type=jnp.float32) * score_scale
    )
    attention, attention_back = jax.vjp(probabilities, raw_scores)
    attention_low = attention.astype(jnp.bfloat16)
    mixed = jnp.einsum("mtk,mkd->mtd", attention_low, values, preferred_element_type=jnp.float32)
    mixed_pieces = from_groups(mixed.astype(jnp.bfloat16))
    branch = sum_pieces(contract_cols(mixed_pieces, w_o).astype(jnp.bfloat16))

    inputs = tokens.astype(jnp.float32).reshape(all_rows, model_width)
    grad_top = cotangent.astype(jnp.float32).reshape(all_rows, model_width)
    normed_two, norm_two_back = jax.vjp(scaled, branch, gain_vals[1])
    middle = inputs + normed_two
    normed_three, norm_three_back = jax.vjp(scaled, middle, gain_vals[2])

    norm_rows = gather_pieces(normed_three.astype(jnp.bfloat16))
    gate_ups = [
        jnp.dot(norm_rows, w_gu, preferred_element_type=jnp.float32) for w_gu in w_gu_chunks
    ]
    hiddens, glu_backs = zip(
        *(jax.vjp(glu_part, part[:, :chunk_width], part[:, chunk_width:]) for part in gate_ups)
    )
    hidden = jnp.concatenate([part.astype(jnp.bfloat16) for part in hiddens], axis=1)
    ffn_branch = sum_pieces(contract_cols(hidden, w_d).astype(jnp.bfloat16))
    normed_four, norm_four_back = jax.vjp(scaled, ffn_branch, gain_vals[3])
    layer_out = (middle + normed_four).astype(jnp.bfloat16).reshape(tokens.shape)
    d_ffn, d_gain_four = norm_four_back(grad_top)
    d_ffn_rows = gather_pieces(d_ffn.astype(jnp.bfloat16))
    grad_d = sum_planes(contract_rows(d_ffn_rows, hidden))
    d_hidden = jnp.dot(d_ffn_rows, w_d, preferred_element_type=jnp.float32)
    d_gate_ups = []
    for at in range(chunks):
        d_gate, d_upper = glu_backs[at](d_hidden[:, at * chunk_width : (at + 1) * chunk_width])
        d_gate_ups.append(jnp.concatenate([d_gate, d_upper], axis=1).astype(jnp.bfloat16))
    d_normed_three = sum_pieces(
        contract_cols(
            jnp.concatenate(d_gate_ups, axis=1), jnp.concatenate(w_gu_chunks, axis=1)
        ).astype(jnp.bfloat16)
    )
    grad_gus = [sum_planes(contract_rows(norm_rows, part)) for part in d_gate_ups]
    d_middle_norm, d_gain_three = norm_three_back(d_normed_three)
    d_middle = grad_top + d_middle_norm
    d_branch, d_gain_two = norm_two_back(d_middle)

    d_branch_rows = gather_pieces(d_branch.astype(jnp.bfloat16))
    d_mixed = to_groups(
        jnp.dot(d_branch_rows, w_o, preferred_element_type=jnp.float32).astype(jnp.bfloat16)
    ).reshape(micro_count, group_rows, HEAD)
    d_attention = jnp.einsum("mtd,mkd->mtk", d_mixed, values, preferred_element_type=jnp.float32)
    (d_raw,) = attention_back(d_attention)
    d_raw_low = d_raw.astype(jnp.bfloat16)
    d_query = (
        jnp.einsum("mtk,mkd->mtd", d_raw_low, keys, preferred_element_type=jnp.float32) * score_scale
    ).reshape(-1, HEAD)
    d_keys = (
        jnp.einsum("mtk,mtd->mkd", d_raw_low, queries, preferred_element_type=jnp.float32)
        * score_scale
    ).reshape(-1, HEAD)
    d_values = jnp.einsum(
        "mtk,mtd->mkd", attention_low, d_mixed, preferred_element_type=jnp.float32
    ).reshape(-1, HEAD)
    d_kv = jnp.where(key_core, d_keys, d_values) + permute(
        jnp.where(key_core, d_values, d_keys).astype(jnp.bfloat16), 1
    ).astype(jnp.float32)
    (d_query_raw,) = query_back(d_query)
    (d_kv_raw,) = kv_back(d_kv)
    d_projected = from_groups(
        jnp.concatenate([d_query_raw, d_kv_raw], axis=1).astype(jnp.bfloat16)
    )
    d_normed_one = sum_pieces(contract_cols(d_projected, w_qkv).astype(jnp.bfloat16))
    grad_attn = sum_planes(
        jnp.concatenate(
            [contract_rows(normed_one, d_projected), contract_rows(d_branch_rows, mixed_pieces)],
            axis=1,
        )
    )
    _, norm_one_back = jax.vjp(scaled, inputs, gain_vals[0])
    d_input_norm, d_gain_one = norm_one_back(d_normed_one)
    layer_grad = (d_middle + d_input_norm).reshape(tokens.shape)
    d_gains = jnp.stack([d_gain_one, d_gain_two, d_gain_three, d_gain_four])
    sum_gain = jnp.sum(
        lax.all_to_all(
            d_gains.reshape(4, device_count, -1).transpose(1, 0, 2),
            ("grp", "seq"),
            split_axis=0,
            concat_axis=0,
            tiled=True,
        ),
        axis=0,
    )

    sum_qkv = jnp.concatenate(
        [
            grad_attn[:, :, :HEAD].reshape(own_rows, HEADS * HEAD),
            grad_attn[:, :, HEAD : 2 * HEAD]
            .reshape(own_rows, KV_HEADS, 2, HEAD)
            .transpose(0, 2, 1, 3)
            .reshape(own_rows, 2 * KV_HEADS * HEAD),
        ],
        axis=1,
    )
    sum_out = grad_attn[:, :, 2 * HEAD :].reshape(own_rows, HEADS * HEAD)
    sum_gu = (
        jnp.stack(
            [part.reshape(own_rows, seq_count, 2, chunk_width) for part in grad_gus], axis=3
        )
        .transpose(0, 2, 1, 3, 4)
        .reshape(own_rows, 2 * ffn_width)
    )
    sum_down = grad_d.reshape(own_rows, ffn_width)
    token_total = micro_count * local_rows * device_count
    rate_mat = weight_rate * token_total ** (-0.5)
    rate_gain = gain_rate * token_total ** (-0.5)
    qkv_new, qkv_mom, qkv_avg, qkv_copy = renew(
        attn_in, attn_in_mom, attn_in_avg, sum_qkv, rate_mat
    )
    out_new, out_mom, out_avg, out_copy = renew(
        attn_out, attn_out_mom, attn_out_avg, sum_out, rate_mat
    )
    gu_new, gu_mom, gu_avg, gu_copy = renew(ffn_in, ffn_in_mom, ffn_in_avg, sum_gu, rate_mat)
    down_new, down_mom, down_avg, down_copy = renew(
        ffn_out, ffn_out_mom, ffn_out_avg, sum_down, rate_mat
    )
    gain_new, gain_mom, gain_avg, gain_copy = renew(
        gains, gains_mom, gains_avg, sum_gain, rate_gain
    )
    return (
        layer_out,
        layer_grad,
        qkv_new,
        qkv_mom,
        qkv_avg,
        qkv_copy,
        out_new,
        out_mom,
        out_avg,
        out_copy,
        gu_new,
        gu_mom,
        gu_avg,
        gu_copy,
        down_new,
        down_mom,
        down_avg,
        down_copy,
        gain_new,
        gain_mom,
        gain_avg,
        gain_copy,
    )


def solution(mesh):
    placed = (
        P(None, ("grp", "seq"), None),
        P(None, ("grp", "seq"), None),
        P(None, "grp"),
        P(("grp", "seq"), None),
        P(("grp", "seq"), None),
        P(("grp", "seq"), None),
        P(("grp", "seq"), None),
        P(None, ("grp", "seq")),
        P(("grp", "seq"), None),
        P(("grp", "seq"), None),
        P(("grp", "seq"), None),
        P(("grp", "seq"), None),
        P(None, ("grp", "seq")),
        P(("grp", "seq"), None),
        P(("grp", "seq"), None),
        P(("grp", "seq"), None),
        P(("grp", "seq"), None),
        P(None, ("grp", "seq")),
    )
    heads_fit = mesh.shape["seq"] == HEADS
    return jax.shard_map(
        by_heads if heads_fit else by_rows,
        mesh=mesh,
        in_specs=placed,
        out_specs=(
            P(None, ("grp", "seq"), None),
            P(None, ("grp", "seq"), None),
            P(("grp", "seq"), None),
            P(("grp", "seq"), None),
            P(("grp", "seq"), None),
            P(("grp", "seq"), None),
            P(("grp", "seq"), None),
            P(("grp", "seq"), None),
            P(("grp", "seq"), None),
            P(("grp", "seq"), None),
            P(("grp", "seq"), None),
            P(("grp", "seq"), None),
            P(("grp", "seq"), None),
            P(("grp", "seq"), None),
            P(("grp", "seq"), None),
            P(("grp", "seq"), None),
            P(("grp", "seq"), None),
            P(("grp", "seq"), None),
            P(None, ("grp", "seq")),
            P(None, ("grp", "seq")),
            P(None, ("grp", "seq")),
            P(None, ("grp", "seq")),
        ),
        check_vma=False,
    )
```

```python
import functools

import jax
import jax.numpy as jnp
from jax import lax
from jax.experimental import pallas as pl
from jax.experimental.layout import Layout, with_layout_constraint
from jax.experimental.pallas import tpu as pltpu
from jax.sharding import PartitionSpec as P

HEADS = 8
KV_HEADS = 4
HEAD = 256
PROMPT = 1024
CONTS = 8


eps_norm = 1e-06
soft_cap = 50.0
momentum_decay = 0.5
average_decay = 0.5
weight_rate = 0.03
gain_rate = 0.2
rope_base = 10000.0
GELU_SCALE = (2.0 / 3.141592653589793) ** 0.5


def scaled(field, gain):
    return field * lax.rsqrt(jnp.mean(field * field, axis=-1, keepdims=True) + eps_norm) * gain


def place_tokens(seg_group, own_segment, row_index):
    levels = jnp.arange(CONTS + 1, dtype=jnp.int32)
    before = jnp.sum((seg_group[None, :] < levels[:, None]).astype(jnp.int32), axis=1)
    seg_start = jnp.sum(
        jnp.where(own_segment[:, None] == levels[None, :], before[None, :], 0), axis=1
    )
    return row_index - seg_start + jnp.where(own_segment > 0, PROMPT, 0)


def rotate(field, positions):
    half = field.shape[-1] // 2
    freqs = rope_base ** (-jnp.arange(half, dtype=jnp.float32) * 2.0 / field.shape[-1])
    angles = positions.astype(jnp.float32)[:, None] * freqs[None, :]
    cosine = jnp.cos(angles)[:, None, :]
    sine = jnp.sin(angles)[:, None, :]
    first_half = field[..., :half]
    second_half = field[..., half:]
    return jnp.concatenate(
        [first_half * cosine - second_half * sine, second_half * cosine + first_half * sine],
        axis=-1,
    )


def glu_part(gate, upper):
    return jax.nn.gelu(gate, approximate=True) * upper


def contract_rows(left, right):
    return lax.dot_general(
        left, right, (((0,), (0,)), ((), ())), preferred_element_type=jnp.float32
    )


def contract_cols(left, right):
    return lax.dot_general(
        left, right, (((1,), (1,)), ((), ())), preferred_element_type=jnp.float32
    )


def renew(weight, moment, average, gradient, step_rate):
    moment_new = momentum_decay * moment + gradient
    weight_new = weight - step_rate * (gradient + momentum_decay * moment_new)
    average_new = average_decay * average + (1.0 - average_decay) * weight_new
    return (weight_new, moment_new, average_new, weight_new.astype(jnp.bfloat16))


def by_rows(
    tokens,
    cotangent,
    segments,
    attn_in,
    attn_out,
    ffn_in,
    ffn_out,
    gains,
    attn_in_mom,
    attn_out_mom,
    ffn_in_mom,
    ffn_out_mom,
    gains_mom,
    attn_in_avg,
    attn_out_avg,
    ffn_in_avg,
    ffn_out_avg,
    gains_avg,
):
    micro_count = tokens.shape[0]
    local_rows = tokens.shape[1]
    all_rows = micro_count * local_rows
    model_width = tokens.shape[2]
    row_offset = lax.axis_index("seq") * local_rows
    row_index = row_offset + jnp.arange(local_rows, dtype=jnp.int32)
    key_index = jnp.arange(segments.shape[1], dtype=jnp.int32)
    query_width = HEADS * HEAD
    kv_width = KV_HEADS * HEAD
    share = HEADS // KV_HEADS
    ffn_width = ffn_out.shape[1]
    own_rows = ffn_in.shape[0]
    score_scale = HEAD ** (-0.5)
    own_segments = lax.dynamic_slice_in_dim(segments, row_offset, local_rows, 1)
    positions = jax.vmap(
        lambda seg_group, own_segment: place_tokens(seg_group, own_segment, row_index)
    )(segments, own_segments).reshape(all_rows)
    visible = (key_index[None, None, :] <= row_index[None, :, None]) & (
        (segments[:, None, :] == 0) | (segments[:, None, :] == own_segments[:, :, None])
    )
    inputs = tokens.astype(jnp.float32).reshape(all_rows, model_width)
    w_qkv, w_o, gain_low = (
        lax.all_gather(attn_in.astype(jnp.bfloat16), ("grp", "seq"), axis=0, tiled=True),
        lax.all_gather(attn_out.astype(jnp.bfloat16), ("grp", "seq"), axis=0, tiled=True),
        lax.all_gather(gains.astype(jnp.bfloat16), ("grp", "seq"), axis=1, tiled=True),
    )
    gain_vals = gain_low.astype(jnp.float32)
    normed_one, norm_one_back = jax.vjp(scaled, inputs, gain_vals[0])
    normed_one = normed_one.astype(jnp.bfloat16)
    projected = jnp.dot(normed_one, w_qkv, preferred_element_type=jnp.float32)
    query_rot, query_back = jax.vjp(
        lambda field: rotate(field, positions),
        projected[:, :query_width].reshape(all_rows, HEADS, HEAD),
    )
    key_rot, key_back = jax.vjp(
        lambda field: rotate(field, positions),
        projected[:, query_width : query_width + kv_width].reshape(all_rows, KV_HEADS, HEAD),
    )
    query_low = query_rot.astype(jnp.bfloat16).reshape(
        micro_count, local_rows, KV_HEADS, share, HEAD
    )
    key_low = key_rot.astype(jnp.bfloat16).reshape(micro_count, local_rows, kv_width)
    value_low = (
        projected[:, query_width + kv_width :]
        .astype(jnp.bfloat16)
        .reshape(micro_count, local_rows, kv_width)
    )
    group_key_rows, group_values = (
        lax.all_gather(key_low, "seq", axis=1, tiled=True),
        lax.all_gather(value_low, "seq", axis=1, tiled=True),
    )
    group_key_rows = group_key_rows.reshape(micro_count, -1, KV_HEADS, HEAD)
    group_values = group_values.reshape(micro_count, -1, KV_HEADS, HEAD)

    def probabilities(raw_scores):
        capped = jnp.where(
            visible[:, None, None], soft_cap * jnp.tanh(raw_scores / soft_cap), -1e30
        )
        return jax.nn.softmax(capped, axis=-1)

    raw_scores = (
        jnp.einsum(
            "mtgrd,mkgd->mgrtk", query_low, group_key_rows, preferred_element_type=jnp.float32
        )
        * score_scale
    )
    attention, attention_back = jax.vjp(probabilities, raw_scores)
    attention_low = attention.astype(jnp.bfloat16)
    mixed_heads = jnp.einsum(
        "mgrtk,mkgd->mtgrd", attention_low, group_values, preferred_element_type=jnp.float32
    )
    mixed_low = mixed_heads.reshape(all_rows, query_width).astype(jnp.bfloat16)
    branch = contract_cols(mixed_low, w_o)
    normed_two, norm_two_back = jax.vjp(scaled, branch, gain_vals[1])
    middle = inputs + normed_two
    normed_three, norm_three_back = jax.vjp(scaled, middle, gain_vals[2])
    normed_three = normed_three.astype(jnp.bfloat16)
    grad_top = cotangent.astype(jnp.float32).reshape(all_rows, model_width)
    seq_count = lax.axis_size("seq")
    grp_count = lax.axis_size("grp")
    slice_width = ffn_width // seq_count
    stacked = jnp.concatenate(
        [
            ffn_in.astype(jnp.bfloat16).reshape(own_rows, 2, seq_count, slice_width),
            ffn_out.astype(jnp.bfloat16).reshape(own_rows, 1, seq_count, slice_width),
        ],
        axis=1,
    )
    spread = jnp.broadcast_to(
        stacked[:, :, None], (own_rows, 3, grp_count, seq_count, slice_width)
    ).reshape(own_rows, 3, grp_count * seq_count, slice_width)
    w_cols = lax.all_to_all(
        spread, ("grp", "seq"), split_axis=2, concat_axis=0, tiled=True
    ).reshape(model_width, 3, slice_width)
    w_gu_cols = w_cols[:, :2].reshape(model_width, 2 * slice_width)
    w_d_cols = w_cols[:, 2]
    norm_rows = lax.all_gather(normed_three, "seq", axis=0, tiled=True)
    gate_up = jnp.dot(norm_rows, w_gu_cols, preferred_element_type=jnp.float32)
    hidden, glu_back = jax.vjp(glu_part, gate_up[:, :slice_width], gate_up[:, slice_width:])
    hidden = hidden.astype(jnp.bfloat16)
    ffn_branch = lax.psum_scatter(
        contract_cols(hidden, w_d_cols), "seq", scatter_dimension=0, tiled=True
    )
    normed_four, norm_four_back = jax.vjp(scaled, ffn_branch, gain_vals[3])
    layer_out = (
        (middle + normed_four).astype(jnp.bfloat16).reshape(micro_count, local_rows, model_width)
    )
    d_ffn, d_gain_four = norm_four_back(grad_top)
    d_ffn_all = lax.all_gather(d_ffn.astype(jnp.bfloat16), "seq", axis=0, tiled=True)
    d_hidden = jnp.dot(d_ffn_all, w_d_cols, preferred_element_type=jnp.float32)
    grad_d_cols = contract_rows(d_ffn_all, hidden)
    d_gate, d_upper = glu_back(d_hidden)
    d_gate_up = jnp.concatenate([d_gate, d_upper], axis=1).astype(jnp.bfloat16)
    grad_gu_cols = contract_rows(norm_rows, d_gate_up)
    d_normed_three = lax.psum_scatter(
        contract_cols(d_gate_up, w_gu_cols), "seq", scatter_dimension=0, tiled=True
    )
    local_grads = jnp.concatenate(
        [grad_gu_cols.reshape(model_width, 2, slice_width), grad_d_cols[:, None, :]], axis=1
    ).reshape(model_width, 3, 1, slice_width)
    returned = lax.all_to_all(
        local_grads.astype(jnp.bfloat16), ("grp", "seq"), split_axis=0, concat_axis=2, tiled=True
    ).astype(local_grads.dtype)
    grad_ffn = jnp.sum(
        returned.reshape(own_rows, 3, grp_count, seq_count, slice_width), axis=2
    ).reshape(own_rows, 3 * ffn_width)
    d_middle_norm, d_gain_three = norm_three_back(d_normed_three)
    d_middle = grad_top + d_middle_norm
    sum_gu = grad_ffn[:, : 2 * ffn_width]
    sum_down = grad_ffn[:, 2 * ffn_width :]
    d_branch, d_gain_two = norm_two_back(d_middle)
    d_branch_low = d_branch.astype(jnp.bfloat16)
    grad_out = contract_rows(d_branch_low, mixed_low)
    d_mixed = jnp.dot(d_branch_low, w_o, preferred_element_type=jnp.float32)
    d_mixed_low = d_mixed.astype(jnp.bfloat16).reshape(
        micro_count, local_rows, KV_HEADS, share, HEAD
    )
    d_attention = jnp.einsum(
        "mtgrd,mkgd->mgrtk", d_mixed_low, group_values, preferred_element_type=jnp.float32
    )
    (d_raw,) = attention_back(d_attention)
    d_raw_low = d_raw.astype(jnp.bfloat16)
    d_query = (
        jnp.einsum(
            "mgrtk,mkgd->mtgrd", d_raw_low, group_key_rows, preferred_element_type=jnp.float32
        )
        * score_scale
    )
    d_group_keys = (
        jnp.einsum("mgrtk,mtgrd->mkgd", d_raw_low, query_low, preferred_element_type=jnp.float32)
        * score_scale
    )
    d_group_values = jnp.einsum(
        "mgrtk,mtgrd->mkgd", attention_low, d_mixed_low, preferred_element_type=jnp.float32
    )
    d_keys, d_values = (
        lax.psum_scatter(
            d_group_keys.reshape(micro_count, -1, kv_width).astype(jnp.bfloat16),
            "seq",
            scatter_dimension=1,
            tiled=True,
        ).astype(jnp.float32),
        lax.psum_scatter(
            d_group_values.reshape(micro_count, -1, kv_width).astype(jnp.bfloat16),
            "seq",
            scatter_dimension=1,
            tiled=True,
        ).astype(jnp.float32),
    )
    (d_query_raw,) = query_back(d_query.reshape(all_rows, HEADS, HEAD))
    (d_key_raw,) = key_back(d_keys.reshape(all_rows, KV_HEADS, HEAD))
    d_projected = jnp.concatenate(
        [
            d_query_raw.reshape(all_rows, query_width),
            d_key_raw.reshape(all_rows, kv_width),
            d_values.reshape(all_rows, kv_width),
        ],
        axis=1,
    ).astype(jnp.bfloat16)
    grad_qkv = contract_rows(normed_one, d_projected)
    d_normed_one = contract_cols(d_projected, w_qkv)
    d_input_norm, d_gain_one = norm_one_back(d_normed_one)
    layer_grad = (d_middle + d_input_norm).reshape(micro_count, local_rows, model_width)
    d_gains = jnp.stack([d_gain_one, d_gain_two, d_gain_three, d_gain_four])
    part_qkv, part_out, part_gain = (
        lax.psum_scatter(
            grad_qkv.astype(jnp.bfloat16), "grp", scatter_dimension=0, tiled=True
        ).astype(jnp.float32),
        lax.psum_scatter(
            grad_out.astype(jnp.bfloat16), "grp", scatter_dimension=0, tiled=True
        ).astype(jnp.float32),
        lax.psum_scatter(
            d_gains.astype(jnp.bfloat16), "grp", scatter_dimension=1, tiled=True
        ).astype(jnp.float32),
    )
    sum_qkv, sum_out, sum_gain = (
        lax.psum_scatter(
            part_qkv.astype(jnp.bfloat16), "seq", scatter_dimension=0, tiled=True
        ).astype(jnp.float32),
        lax.psum_scatter(
            part_out.astype(jnp.bfloat16), "seq", scatter_dimension=0, tiled=True
        ).astype(jnp.float32),
        lax.psum_scatter(
            part_gain.astype(jnp.bfloat16), "seq", scatter_dimension=1, tiled=True
        ).astype(jnp.float32),
    )
    token_total = micro_count * local_rows * lax.axis_size(("grp", "seq"))
    rate_mat = weight_rate * token_total ** (-0.5)
    rate_gain = gain_rate * token_total ** (-0.5)
    qkv_new, qkv_mom, qkv_avg, qkv_copy = renew(
        attn_in, attn_in_mom, attn_in_avg, sum_qkv, rate_mat
    )
    out_new, out_mom, out_avg, out_copy = renew(
        attn_out, attn_out_mom, attn_out_avg, sum_out, rate_mat
    )
    gu_new, gu_mom, gu_avg, gu_copy = renew(ffn_in, ffn_in_mom, ffn_in_avg, sum_gu, rate_mat)
    down_new, down_mom, down_avg, down_copy = renew(
        ffn_out, ffn_out_mom, ffn_out_avg, sum_down, rate_mat
    )
    gain_new, gain_mom, gain_avg, gain_copy = renew(
        gains, gains_mom, gains_avg, sum_gain, rate_gain
    )
    return (
        layer_out,
        layer_grad,
        qkv_new,
        qkv_mom,
        qkv_avg,
        qkv_copy,
        out_new,
        out_mom,
        out_avg,
        out_copy,
        gu_new,
        gu_mom,
        gu_avg,
        gu_copy,
        down_new,
        down_mom,
        down_avg,
        down_copy,
        gain_new,
        gain_mom,
        gain_avg,
        gain_copy,
    )


VMEM_LIMIT = 48 * 1024 * 1024


def permute(field, offset):
    count = lax.axis_size("seq")
    return lax.ppermute(field, "seq", [(i, i ^ offset) for i in range(count)])


def gather_near(field):
    return field, permute(field, 2), permute(field, 4)


def gather_mine(field, by_x, by_y):
    half = field.shape[0] // 2
    far = [permute(by_x[:half], 4), permute(by_y[half:], 2)]
    return jnp.concatenate([field, by_x, by_y] + far, axis=0)


def gather_far(field, by_x, by_y):
    mine = gather_mine(field, by_x, by_y)
    return [mine, permute(mine, 1)]


def gather_pieces(field):
    return gather_far(*gather_near(field))


def add_low(left, right):
    return (left.astype(jnp.float32) + right.astype(jnp.float32)).astype(jnp.bfloat16)


def sum_far(own, by_x, by_y, far):
    half = own.shape[0] // 2
    far_x = permute(far[:half], 2)
    far_y = permute(far[half:], 4)
    by_y = jnp.concatenate([add_low(by_y[:half], far_x), by_y[half:]], axis=0)
    by_x = jnp.concatenate([by_x[:half], add_low(by_x[half:], far_y)], axis=0)
    return own, by_x, by_y


def sum_near(own, by_x, by_y):
    return own.astype(jnp.float32) + by_x.astype(jnp.float32) + by_y.astype(jnp.float32)


def sum_pairs(*blocks):
    own, by_x, by_y = sum_far(*blocks)
    return sum_near(own, permute(by_x, 2), permute(by_y, 4))


def pair_products(mine, other, weight):
    rows = mine.shape[0] // 4
    ends = []
    for here in (slice(3 * rows, None), slice(None, 3 * rows)):
        moved = permute(low(contract_cols(other[here], weight)), 1)
        ends.append(add_low(low(contract_cols(mine[here], weight)), moved))
    far, near = ends
    return near[:rows], near[rows : 2 * rows], near[2 * rows :], far


def pair_halves(mine, other, weight):
    moved = permute(low(contract_cols(other, weight)), 1)
    total = add_low(low(contract_cols(mine, weight)), moved)
    rows = total.shape[0] // 4
    return [total[at * rows : (at + 1) * rows] for at in range(4)]


def sum_products(mine, other, weight):
    return sum_pairs(*pair_products(mine, other, weight))


def piece_order(blocks):
    index = lax.axis_index("seq")
    count = blocks.shape[0]
    bits = count.bit_length() - 1
    split = blocks.reshape((2,) * bits + blocks.shape[1:])
    for bit in range(bits):
        axis = bits - 1 - bit
        split = jnp.where((index >> bit) & 1 == 1, jnp.flip(split, axis), split)
    return jnp.swapaxes(split.reshape((count // 2, 2) + blocks.shape[1:]), 0, 1).reshape(blocks.shape)


def qkv_columns(device):
    return [device, HEADS + (device % 2) * KV_HEADS + device // 2]


def out_columns(device):
    return [device]


def spread_kernel(count, blocks, field_ref, out_ref):
    parts = len(blocks(0))
    width = out_ref.shape[2] // parts
    for device in range(count):
        for part, block in enumerate(blocks(device)):
            out_ref[device, :, part * width : (part + 1) * width] = field_ref[
                :, block * width : (block + 1) * width
            ].astype(jnp.bfloat16)


def spread(field, count, blocks):
    rows, columns = field.shape
    return pl.pallas_call(
        functools.partial(spread_kernel, count, blocks),
        out_shape=jax.ShapeDtypeStruct((count, rows, columns // count), jnp.bfloat16),
        cost_estimate=pl.CostEstimate(flops=0, transcendentals=0, bytes_accessed=6 * field.size),
        compiler_params=pltpu.CompilerParams(vmem_limit_bytes=VMEM_LIMIT),
        name="spread",
    )(field)


def row_product(weight, gradient):
    used = weight.astype(jnp.bfloat16).astype(jnp.float32)
    return jnp.sum(used * gradient, axis=1, keepdims=True)


def renew_kernel(rate, w_ref, m_ref, a_ref, g_ref, w_out, m_out, a_out, c_out, product_out):
    gradient = g_ref[0].astype(jnp.float32)
    w_new, m_new, a_new, copy = renew(w_ref[...], m_ref[...], a_ref[...], gradient, rate)
    product_out[...] += row_product(w_ref[...], gradient)
    w_out[...] = w_new
    m_out[...] = m_new
    a_out[...] = a_new
    c_out[...] = copy


def renew_parts_kernel(rate, w_ref, m_ref, a_ref, *refs):
    g_refs, outs = refs[:-5], refs[-5:]

    @pl.when((pl.program_id(0) == 0) & (pl.program_id(1) == 0))
    def _():
        outs[-1][...] = jnp.zeros_like(outs[-1])

    for part, g_ref in enumerate(g_refs):

        @pl.when(pl.program_id(1) == part)
        def _(g_ref=g_ref):
            renew_kernel(rate, w_ref, m_ref, a_ref, g_ref, *outs)


def renew_wide(weight, moment, average, gradients, rate):
    rows, columns = weight.shape
    parts = len(gradients)
    count = gradients[0][0].shape[0]
    width = columns // (count * parts)
    own = pl.BlockSpec((rows, width), lambda d, p: (0, p * count + d))

    def of_block(block):
        return pl.BlockSpec((1, rows, width), lambda d, p: (d, 0, block))

    return pl.pallas_call(
        functools.partial(renew_parts_kernel, rate),
        grid=(count, parts),
        in_specs=[own, own, own] + [of_block(block) for _, block in gradients],
        out_specs=[own, own, own, own, pl.BlockSpec((rows, 1), lambda d, p: (0, 0))],
        out_shape=[jax.ShapeDtypeStruct((rows, columns), jnp.float32)] * 3
        + [
            jax.ShapeDtypeStruct((rows, columns), jnp.bfloat16),
            jax.ShapeDtypeStruct((rows, 1), jnp.float32),
        ],
        cost_estimate=pl.CostEstimate(
            flops=8 * weight.size, transcendentals=0, bytes_accessed=28 * weight.size
        ),
        compiler_params=pltpu.CompilerParams(vmem_limit_bytes=VMEM_LIMIT),
        name="renew",
    )(weight, moment, average, *(array for array, _ in gradients))


def renew_heads_kernel(rate, g_ref, *refs):
    product = jnp.zeros(refs[-1].shape, jnp.float32)
    for device in range(g_ref.shape[0]):
        blocks = [(0, block) for block in qkv_columns(device)] + [(1, device)]
        for part, (which, block) in enumerate(blocks):
            w_ref, m_ref, a_ref = refs[3 * which : 3 * which + 3]
            outs = refs[6 + 4 * which : 10 + 4 * which]
            here = (slice(None), slice(block * HEAD, (block + 1) * HEAD))
            gradient = g_ref[device, :, part * HEAD : (part + 1) * HEAD].astype(jnp.float32)
            results = renew(w_ref[here], m_ref[here], a_ref[here], gradient, rate)
            for out, result in zip(outs, results):
                out[here] = result
            if which == 0:
                product += row_product(w_ref[here], gradient)
    refs[-1][...] = product


def renew_heads(gradient, attn_in, attn_out, rate):
    kinds = (jnp.float32, jnp.float32, jnp.float32, jnp.bfloat16)
    shapes = [
        jax.ShapeDtypeStruct(state[0].shape, kind) for state in (attn_in, attn_out) for kind in kinds
    ]
    size = attn_in[0].size + attn_out[0].size
    results = pl.pallas_call(
        functools.partial(renew_heads_kernel, rate),
        out_shape=shapes + [jax.ShapeDtypeStruct((attn_in[0].shape[0], 1), jnp.float32)],
        cost_estimate=pl.CostEstimate(flops=8 * size, transcendentals=0, bytes_accessed=28 * size),
        compiler_params=pltpu.CompilerParams(vmem_limit_bytes=VMEM_LIMIT),
        name="renew_heads",
    )(gradient, *attn_in, *attn_out)
    return results[:4], results[4:8], results[8]


def glu_back_kernel(left0_ref, left1_ref, w0_ref, w1_ref, gate_up_ref, out_ref):
    width = w0_ref.shape[1]
    d_hidden = jnp.dot(left0_ref[...], w0_ref[...], preferred_element_type=jnp.float32)
    d_hidden += jnp.dot(left1_ref[...], w1_ref[...], preferred_element_type=jnp.float32)
    gate = gate_up_ref[:, :width]
    upper = gate_up_ref[:, width:]
    square = gate * gate
    bent = jnp.tanh(GELU_SCALE * gate * (1.0 + 0.044715 * square))
    rise = 0.5 * (1.0 + bent)
    slope = rise + 0.5 * gate * (1.0 - bent * bent) * GELU_SCALE * (1.0 + 3 * 0.044715 * square)
    out_ref[:, :width] = (d_hidden * upper * slope).astype(jnp.bfloat16)
    out_ref[:, width:] = (d_hidden * gate * rise).astype(jnp.bfloat16)


def glu_back_rows(left0, left1, w0, w1, gate_up):
    rows = left0.shape[0]
    width = w0.shape[1]
    tile = rows // 6
    return pl.pallas_call(
        glu_back_kernel,
        grid=(rows // tile,),
        in_specs=[
            pl.BlockSpec((tile, left0.shape[1]), lambda i: (i, 0)),
            pl.BlockSpec((tile, left1.shape[1]), lambda i: (i, 0)),
            pl.BlockSpec(w0.shape, lambda i: (0, 0)),
            pl.BlockSpec(w1.shape, lambda i: (0, 0)),
            pl.BlockSpec((tile, 2 * width), lambda i: (i, 0)),
        ],
        out_specs=pl.BlockSpec((tile, 2 * width), lambda i: (i, 0)),
        out_shape=jax.ShapeDtypeStruct((rows, 2 * width), jnp.bfloat16),
        cost_estimate=pl.CostEstimate(
            flops=2 * rows * (w0.shape[0] + w1.shape[0]) * width,
            transcendentals=rows * width,
            bytes_accessed=rows * (2 * (left0.shape[1] + left1.shape[1]) + 12 * width),
        ),
        compiler_params=pltpu.CompilerParams(vmem_limit_bytes=VMEM_LIMIT),
        name="glu_back",
    )(left0, left1, w0, w1, gate_up)


def norm_tiles(rows, width, kinds):
    tile = rows // 3
    return [
        pl.BlockSpec((tile, width), lambda i: (i, 0))
        if kind
        else pl.BlockSpec((1, width), lambda i: (0, 0))
        for kind in kinds
    ]


def norm_call(kernel, name, rows, width, fields, gains, outs):
    specs = norm_tiles(rows, width, [1] * len(fields) + [0] * len(gains))
    return pl.pallas_call(
        kernel,
        grid=(3,),
        in_specs=specs,
        out_specs=norm_tiles(rows, width, [out is not None for out in outs]),
        out_shape=[
            jax.ShapeDtypeStruct((rows, width), out)
            if out is not None
            else jax.ShapeDtypeStruct((1, width), jnp.float32)
            for out in outs
        ],
        cost_estimate=pl.CostEstimate(
            flops=20 * rows * width, transcendentals=0, bytes_accessed=20 * rows * width
        ),
        compiler_params=pltpu.CompilerParams(vmem_limit_bytes=VMEM_LIMIT // 2),
        name=name,
    )(*fields, *gains)


def row_inverse(field):
    return lax.rsqrt(jnp.mean(field * field, axis=1, keepdims=True) + eps_norm)


def row_back(field, inverse, top):
    inner = jnp.mean(field * top, axis=1, keepdims=True)
    return inverse * top - field * (inverse * inverse * inverse * inner)


def read_sum(own_ref, by_x_ref, by_y_ref):
    return (
        own_ref[...].astype(jnp.float32)
        + by_x_ref[...].astype(jnp.float32)
        + by_y_ref[...].astype(jnp.float32)
    )


def middle_kernel(own_ref, by_x_ref, by_y_ref, token_ref, g1_ref, g2_ref, branch_ref, middle_ref, out_ref):
    branch = read_sum(own_ref, by_x_ref, by_y_ref)
    branch_ref[...] = branch
    middle = token_ref[...].astype(jnp.float32) + branch * row_inverse(branch) * g1_ref[...]
    middle_ref[...] = middle
    out_ref[...] = (middle * row_inverse(middle) * g2_ref[...]).astype(jnp.bfloat16)


def middle_back_kernel(
    own_ref,
    by_x_ref,
    by_y_ref,
    top_ref,
    branch_ref,
    middle_ref,
    g1_ref,
    g2_ref,
    d_middle_ref,
    d_branch_ref,
    d_gain_ref,
):
    middle, branch = middle_ref[...], branch_ref[...]
    d_normed = read_sum(own_ref, by_x_ref, by_y_ref)
    d_middle = top_ref[...].astype(jnp.float32) + row_back(
        middle, row_inverse(middle), g2_ref[...] * d_normed
    )
    d_middle_ref[...] = d_middle
    inverse = row_inverse(branch)
    d_branch_ref[...] = row_back(branch, inverse, g1_ref[...] * d_middle).astype(jnp.bfloat16)

    @pl.when(pl.program_id(0) == 0)
    def _():
        d_gain_ref[...] = jnp.zeros_like(d_gain_ref)

    d_gain_ref[...] += jnp.sum(d_middle * (branch * inverse), axis=0, keepdims=True)


def input_back_kernel(own_ref, by_x_ref, by_y_ref, token_ref, d_middle_ref, g0_ref, out_ref):
    token = token_ref[...].astype(jnp.float32)
    d_normed = read_sum(own_ref, by_x_ref, by_y_ref)
    out_ref[...] = d_middle_ref[...] + row_back(token, row_inverse(token), g0_ref[...] * d_normed)


def across(left, right):
    return lax.dot_general(
        left, right, (((1,), (1,)), ((), ())), preferred_element_type=jnp.float32
    )


def down(left, right):
    return lax.dot_general(
        left, right, (((0,), (0,)), ((), ())), preferred_element_type=jnp.float32
    )


def capped_scores(q, k, key_ref, query_ref):
    bent = jnp.tanh(across(k, q) * (HEAD ** (-0.5) / soft_cap))
    key, query = key_ref[0][:, :1], query_ref[0]
    seg_k, seg_q = key & 15, query & 15
    seen = ((key >> 4) <= (query >> 4)) & ((seg_k == 0) | (seg_k == seg_q))
    return bent, jnp.where(seen, soft_cap * bent, -1e30)


def attend_kernel(q_ref, k_ref, v_ref, key_ref, query_ref, out_ref, norm_ref):
    _, capped = capped_scores(q_ref[0], k_ref[0], key_ref, query_ref)
    top = jnp.max(capped, axis=0, keepdims=True)
    powers = jnp.exp(capped - top)
    total = jnp.sum(powers, axis=0, keepdims=True)
    weights = (powers * (1.0 / total)).astype(jnp.bfloat16)
    norm_ref[0] = top + jnp.log(total)
    out_ref[0] = down(weights, v_ref[0]).astype(jnp.bfloat16)


def attend_back_kernel(
    q_ref, k_ref, v_ref, key_ref, query_ref, norm_ref, d_out_ref, dq_ref, dk_ref, dv_ref
):
    q, k, v, d_out = q_ref[0], k_ref[0], v_ref[0], d_out_ref[0]
    bent, capped = capped_scores(q, k, key_ref, query_ref)
    weights = jnp.exp(capped - norm_ref[0])
    d_weights = across(v, d_out)
    inner = jnp.sum(weights * d_weights, axis=0, keepdims=True)
    d_raw = (weights * (d_weights - inner) * (1.0 - bent * bent)).astype(jnp.bfloat16)
    scale = HEAD ** (-0.5)

    @pl.when(pl.program_id(1) == 0)
    def _():
        dk_ref[...] = jnp.zeros_like(dk_ref)
        dv_ref[...] = jnp.zeros_like(dv_ref)

    dq_ref[0] = down(d_raw, k) * scale
    dk_ref[0] += jnp.dot(d_raw, q, preferred_element_type=jnp.float32) * scale
    dv_ref[0] += jnp.dot(weights.astype(jnp.bfloat16), d_out, preferred_element_type=jnp.float32)


def attention_cost(micros, rows, products):
    return pl.CostEstimate(
        flops=2 * products * micros * rows * rows * HEAD,
        transcendentals=2 * micros * rows * rows,
        bytes_accessed=4 * products * micros * rows * HEAD,
    )


def attention_specs(rows, tile):
    moving = pl.BlockSpec((1, tile, HEAD), lambda m, i: (m, i, 0))
    whole = pl.BlockSpec((1, rows, HEAD), lambda m, i: (m, 0, 0))
    lane = pl.BlockSpec((1, 1, tile), lambda m, i: (m, 0, i))
    places = [pl.BlockSpec((1, rows, 128), lambda m, i: (m, 0, 0)), lane]
    return moving, whole, lane, places


def attend(q, k, v, places):
    micros, rows, _ = q.shape
    tile = rows // 3
    moving, whole, lane, place_specs = attention_specs(rows, tile)
    return pl.pallas_call(
        attend_kernel,
        grid=(micros, rows // tile),
        in_specs=[moving, whole, whole] + place_specs,
        out_specs=[moving, lane],
        out_shape=[
            jax.ShapeDtypeStruct(q.shape, jnp.bfloat16),
            jax.ShapeDtypeStruct((micros, 1, rows), jnp.float32),
        ],
        cost_estimate=attention_cost(micros, rows, 2),
        compiler_params=pltpu.CompilerParams(vmem_limit_bytes=VMEM_LIMIT),
        name="attend",
    )(q, k, v, *places)


def attend_back(q, k, v, places, norm, d_out):
    micros, rows, _ = q.shape
    tile = rows // 3
    moving, whole, lane, place_specs = attention_specs(rows, tile)
    return pl.pallas_call(
        attend_back_kernel,
        grid=(micros, rows // tile),
        in_specs=[moving, whole, whole] + place_specs + [lane, moving],
        out_specs=[moving, whole, whole],
        out_shape=[jax.ShapeDtypeStruct(q.shape, jnp.float32)] * 3,
        cost_estimate=attention_cost(micros, rows, 5),
        compiler_params=pltpu.CompilerParams(vmem_limit_bytes=VMEM_LIMIT),
        name="attend_back",
    )(q, k, v, *places, norm, d_out)


def exchange(field):
    return lax.all_to_all(field, "seq", split_axis=0, concat_axis=0, tiled=True)


def in_order(step, *operands):
    zeros = jax.eval_shape(step, *operands)
    return lax.cond(
        lax.optimization_barrier(jnp.bool_(True)),
        step,
        lambda *_: jax.tree.map(lambda leaf: jnp.zeros(leaf.shape, leaf.dtype), zeros),
        *operands,
    )


def gather_planes(field):
    return lax.all_gather(field, "grp", axis=0, tiled=True)


def sum_planes(field):
    return lax.psum_scatter(field, "grp", scatter_dimension=0, tiled=True)


def turn(field, cosine, sine):
    half = field.shape[-1] // 2
    first, second = field[..., :half], field[..., half:]
    return jnp.concatenate([first * cosine - second * sine, second * cosine + first * sine], axis=-1)


def low(field):
    return field.astype(jnp.bfloat16)


def dot(left, right):
    return jnp.dot(left, right, preferred_element_type=jnp.float32)


def over_rows(lefts, rights):
    return low(contract_rows(lefts[0], rights[0]) + contract_rows(lefts[1], rights[1]))


def by_heads(
    tokens,
    cotangent,
    segments,
    attn_in,
    attn_out,
    ffn_in,
    ffn_out,
    gains,
    attn_in_mom,
    attn_out_mom,
    ffn_in_mom,
    ffn_out_mom,
    gains_mom,
    attn_in_avg,
    attn_out_avg,
    ffn_in_avg,
    ffn_out_avg,
    gains_avg,
):
    tie = lax.optimization_barrier
    micro_count, local_rows, model_width = tokens.shape
    all_rows = micro_count * local_rows
    seq_count = lax.axis_size("seq")
    grp_count = lax.axis_size("grp")
    device_count = seq_count * grp_count
    group_rows = segments.shape[1]
    own_rows = ffn_in.shape[0]
    plane_rows = own_rows * seq_count
    cut = own_rows * 2 // 3
    slice_width = ffn_out.shape[1] // seq_count
    index = lax.axis_index("seq")
    key_core = index % 2 == 0
    token_total = micro_count * local_rows * device_count
    rate_mat = weight_rate * token_total ** (-0.5)
    rate_gain = gain_rate * token_total ** (-0.5)

    def ffn_columns(device):
        return [device, seq_count + device]

    def by_device(part):
        return exchange(part.reshape(seq_count, own_rows, -1))

    def to_parts(field):
        split = field.reshape(-1, device_count, own_rows)
        return [
            split[:, :, :cut].reshape(field.shape[0], -1),
            split[:, :, cut:].reshape(field.shape[0], -1),
        ]

    def from_parts(parts):
        split = [part.reshape(part.shape[0], device_count, -1) for part in parts]
        return jnp.concatenate(split, axis=2).reshape(-1, model_width)

    def to_groups(field):
        return (
            field.reshape(seq_count, micro_count, local_rows, -1)
            .transpose(1, 0, 2, 3)
            .reshape(micro_count, group_rows, -1)
        )

    def from_groups(field):
        return (
            field.reshape(micro_count, seq_count, local_rows, -1)
            .transpose(1, 0, 2, 3)
            .reshape(seq_count * all_rows, -1)
        )

    def in_two(field):
        return [field[: field.shape[0] // 2], field[field.shape[0] // 2 :]]

    def swap_cores(field):
        first, second = in_two(permute(field, 1))
        return jnp.concatenate([second, first], axis=0)

    heads_moved = exchange(
        jnp.concatenate(
            [spread(attn_in, seq_count, qkv_columns), spread(attn_out, seq_count, out_columns)], axis=2
        )
    ).reshape(plane_rows, 3 * HEAD)
    later_tokens, gains_low, heads_moved = tie((tokens, low(gains), heads_moved))
    w_heads = gather_planes(heads_moved)
    all_gains = lax.all_to_all(
        jnp.broadcast_to(gains_low[None], (device_count,) + gains.shape),
        ("grp", "seq"),
        split_axis=0,
        concat_axis=0,
        tiled=True,
    )
    gain_vals = all_gains.transpose(1, 0, 2).reshape(4, model_width).astype(jnp.float32)
    own_rows_low, by_x, by_y = gather_near(later_tokens.reshape(all_rows, model_width))
    true_rows = jnp.arange(group_rows, dtype=jnp.int32)
    positions = jax.vmap(lambda seg: place_tokens(seg, seg, true_rows))(segments)

    def to_pieces(field):
        return piece_order(field.reshape(micro_count, seq_count, local_rows).transpose(1, 0, 2))

    place = to_pieces(positions).reshape(-1).astype(jnp.float32)
    seg = to_pieces(segments).transpose(1, 0, 2).reshape(micro_count, group_rows)
    row = piece_order(true_rows.reshape(seq_count, local_rows)).reshape(-1)
    freqs = rope_base ** (-jnp.arange(HEAD // 2, dtype=jnp.float32) * 2.0 / HEAD)
    angles = place[:, None] * freqs[None, :]
    cosine, sine = jnp.cos(angles), jnp.sin(angles)
    cosine, sine, kv_cosine, kv_sine, *places = tie(
        (
            cosine,
            sine,
            jnp.where(key_core, cosine, 1.0),
            jnp.where(key_core, sine, 0.0),
            jnp.broadcast_to((16 * row + seg)[:, :, None], seg.shape + (128,)),
            (16 * row + seg)[:, None, :],
        )
    )

    by_x, by_y, later_ffn_in, gain_vals, cosine = tie((by_x, by_y, ffn_in, gain_vals, cosine))
    gu_moved = exchange(spread(later_ffn_in, seq_count, ffn_columns))
    token_rows = gather_far(own_rows_low, by_x, by_y)
    w_gu = gather_planes(gu_moved.reshape(plane_rows, 2 * slice_width))
    down_low = spread(ffn_out, seq_count, out_columns)

    def normed_token_rows(token_rows, inverses):
        return [
            low(part.astype(jnp.float32) * inverse[:, None] * gain_vals[0])
            for part, inverse in zip(token_rows, inverses)
        ]

    def attention(token_rows, w_heads, down_low):
        w_qkv = w_heads[:, : 2 * HEAD]
        down_moved = exchange(down_low)
        inverses = [
            lax.rsqrt(jnp.mean(jnp.square(part.astype(jnp.float32)), axis=1) + eps_norm)
            for part in token_rows
        ]
        projected = jnp.concatenate(
            [dot(part, w_qkv) for part in normed_token_rows(token_rows, inverses)], axis=0
        )
        kv_own = low(turn(projected[:, HEAD:], kv_cosine, kv_sine))
        kv_other = swap_cores(kv_own)
        queries = to_groups(low(turn(projected[:, :HEAD], cosine, sine)))
        keys = to_groups(jnp.where(key_core, kv_own, kv_other))
        values = to_groups(jnp.where(key_core, kv_other, kv_own))
        mixed, norm = attend(queries, keys, values, places)
        mixed, down_moved = tie((mixed, down_moved))
        mixed_rows = in_two(from_groups(mixed))
        down_rows = [
            part.reshape(-1, slice_width) for part in (down_moved[:, :cut], down_moved[:, cut:])
        ]
        return down_rows, inverses, (queries, keys, values, norm), mixed_rows

    down_rows, inverses, state, mixed_rows = in_order(attention, token_rows, w_heads, down_low)
    w_down0, w_down1 = gather_planes(down_rows[0]), gather_planes(down_rows[1])

    def attention_out(mixed_rows, w_heads, tokens, cotangent):
        w_o = w_heads[:, 2 * HEAD :]
        grad_parts = to_parts(cotangent.reshape(all_rows, model_width))
        own, by_x, by_y = sum_far(*pair_products(*mixed_rows, w_o))
        by_x, by_y, *grad_parts = tie((permute(by_x, 2), permute(by_y, 4), *grad_parts))
        branch, middle, normed_three = norm_call(
            middle_kernel,
            "middle",
            all_rows,
            model_width,
            [own, by_x, by_y, tokens.reshape(all_rows, model_width)],
            [gain_vals[1:2], gain_vals[2:3]],
            [jnp.float32, jnp.float32, jnp.bfloat16],
        )
        norm_rows = jnp.concatenate(gather_pieces(normed_three), axis=0)
        return branch, middle, norm_rows, grad_parts

    branch, middle, norm_rows, grad_parts = in_order(
        attention_out, mixed_rows, w_heads, tokens, cotangent
    )
    queries, keys, values, norm = state

    def feed_up(norm_rows, w_gu):
        gate_up = dot(norm_rows, w_gu)
        return gate_up, low(glu_part(gate_up[:, :slice_width], gate_up[:, slice_width:]))

    gate_up, hidden = in_order(feed_up, norm_rows, w_gu)

    def feed_down(hidden, w_down0):
        return sum_products(*in_two(hidden), w_down0)

    ffn0 = in_order(feed_down, hidden, w_down0)
    gain_parts = to_parts(gain_vals[3:])

    def feed_end(hidden, w_down1, ffn0, grad_parts):
        ffn1 = sum_products(*in_two(hidden), w_down1)
        ffns = [ffn0, ffn1]
        squares = sum(jnp.sum(part * part, axis=1, keepdims=True) for part in ffns)
        inverse = lax.rsqrt(squares / model_width + eps_norm)
        tops = [part.astype(jnp.float32) for part in grad_parts]
        scaled_tops = [top * gain for top, gain in zip(tops, gain_parts)]
        inner = sum(
            jnp.sum(top * part, axis=1, keepdims=True) for top, part in zip(scaled_tops, ffns)
        )
        pull = inverse * inverse * inverse * (inner / model_width)
        d_ffns = [low(top * inverse - part * pull) for top, part in zip(scaled_tops, ffns)]
        first = jnp.concatenate(gather_pieces(d_ffns[1]), axis=0)
        return ffn1, inverse, gather_near(d_ffns[0]), first, low(contract_rows(first, hidden))

    ffn1, inverse, second_near, first, grad_down1 = in_order(feed_end, hidden, w_down1, ffn0, grad_parts)

    down_part1 = sum_planes(grad_down1)

    def feed_back(second_near, hidden):
        second = jnp.concatenate(gather_far(*second_near), axis=0)
        return second, low(contract_rows(second, hidden))

    second, grad_down0 = in_order(feed_back, second_near, hidden)
    down_part0 = sum_planes(grad_down0)

    def feed_back_rows(second, first, gate_up, norm_rows, w_down0, w_down1, w_gu, down_part1):
        second, down_part1 = tie((second, down_part1))
        d_gate_up = glu_back_rows(second, first, w_down0, w_down1, gate_up)
        blocks = pair_halves(*in_two(d_gate_up), w_gu)
        grad_gate = low(contract_rows(norm_rows, d_gate_up[:, :slice_width]))
        return d_gate_up, blocks, with_layout_constraint(grad_gate, Layout((0, 1))), down_part1

    d_gate_up, d_norm_blocks, grad_gate, down_part1 = in_order(
        feed_back_rows, second, first, gate_up, norm_rows, w_down0, w_down1, w_gu, down_part1
    )
    gate_part = sum_planes(grad_gate)

    def middle_back(
        d_norm_blocks, d_gate_up, norm_rows, cotangent, branch, middle, down_part0, down_part1
    ):
        d_gate_up, down_part0 = tie((d_gate_up, down_part0))
        down_part = jnp.concatenate(
            [part.reshape(seq_count, -1, slice_width) for part in (down_part0, down_part1)], axis=1
        )
        own, by_x, by_y = sum_far(*d_norm_blocks)
        by_x, by_y, norm_rows = tie((by_x, by_y, norm_rows))
        by_x, by_y = permute(by_x, 2), permute(by_y, 4)
        grad_upper = low(contract_rows(norm_rows, d_gate_up[:, slice_width:]))
        by_x, by_y, grad_upper = tie((by_x, by_y, grad_upper))
        d_middle, d_branch, d_gain_two = norm_call(
            middle_back_kernel,
            "middle_back",
            all_rows,
            model_width,
            [own, by_x, by_y, cotangent.reshape(all_rows, model_width), branch, middle],
            [gain_vals[1:2], gain_vals[2:3]],
            [jnp.float32, jnp.bfloat16, None],
        )
        return grad_upper, d_middle, d_branch, d_gain_two[0], down_part

    grad_upper, d_middle, d_branch, d_gain_two, down_part = in_order(
        middle_back,
        d_norm_blocks,
        d_gate_up,
        norm_rows,
        cotangent,
        branch,
        middle,
        down_part0,
        down_part1,
    )
    upper_part = sum_planes(grad_upper)

    def output_rows(d_branch, middle, ffns, inverse, grad_parts):
        own, by_x, by_y = gather_near(d_branch)
        normeds = [part * inverse for part in ffns]
        d_gain_four = from_parts(
            [
                jnp.sum(top.astype(jnp.float32) * part, axis=0)[None]
                for top, part in zip(grad_parts, normeds)
            ]
        )[0]
        normed_four = from_parts([part * gain for part, gain in zip(normeds, gain_parts)])
        layer_out = low(middle + normed_four).reshape(tokens.shape)
        by_x, by_y, layer_out = tie((by_x, by_y, layer_out))
        return gather_mine(own, by_x, by_y), d_gain_four, layer_out

    d_branch_mine, d_gain_four, layer_out = in_order(
        output_rows, d_branch, middle, [ffn0, ffn1], inverse, grad_parts
    )

    def attention_back(
        d_branch_mine,
        mixed_rows,
        w_heads,
        gate_part,
        down_part,
        token_rows,
        inverses,
        queries,
        keys,
        values,
        norm,
    ):
        gate_grad = by_device(gate_part)
        d_branch_rows = [d_branch_mine, permute(d_branch_mine, 1)]
        d_mixed = to_groups(
            jnp.concatenate([low(dot(part, w_heads[:, 2 * HEAD :])) for part in d_branch_rows], axis=0)
        )
        d_query, d_keys, d_values = attend_back(queries, keys, values, places, norm, d_mixed)
        d_query, d_keys, d_values, gate_grad = tie((d_query, d_keys, d_values, gate_grad))
        d_kv = from_groups(jnp.where(key_core, d_keys, d_values)) + swap_cores(
            from_groups(low(jnp.where(key_core, d_values, d_keys)))
        ).astype(jnp.float32)
        d_projected = in_two(
            low(
                jnp.concatenate(
                    [turn(from_groups(d_query), cosine, -sine), turn(d_kv, kv_cosine, -kv_sine)],
                    axis=1,
                )
            )
        )
        moved = permute(low(contract_cols(d_projected[1], w_heads[:, : 2 * HEAD])), 1)
        down_grad = exchange(down_part)
        grad_out = over_rows(d_branch_rows, mixed_rows)
        grad_qkv = over_rows(normed_token_rows(token_rows, inverses), d_projected)
        grad_heads = jnp.concatenate(
            [with_layout_constraint(grad, Layout((0, 1))) for grad in (grad_qkv, grad_out)], axis=1
        )
        return d_projected[0], moved, grad_heads, gate_grad, down_grad

    d_projected, moved, grad_heads, gate_grad, down_grad = in_order(
        attention_back,
        d_branch_mine,
        mixed_rows,
        w_heads,
        gate_part,
        down_part,
        token_rows,
        inverses,
        queries,
        keys,
        values,
        norm,
    )
    heads_part = sum_planes(grad_heads)

    def update_start(d_projected, moved, w_heads, upper_part):
        upper_grad = by_device(upper_part)
        total = add_low(low(contract_cols(d_projected, w_heads[:, : 2 * HEAD])), moved)
        total, upper_grad = tie((total, upper_grad))
        rows = total.shape[0] // 4
        return sum_far(*(total[at * rows : (at + 1) * rows] for at in range(4))), upper_grad

    (own, by_x, by_y), upper_grad = in_order(
        update_start, d_projected, moved, w_heads, upper_part
    )
    by_x, by_y = permute(by_x, 2), permute(by_y, 4)
    gu_all = renew_wide(
        ffn_in, ffn_in_mom, ffn_in_avg, [(gate_grad, 0), (upper_grad, 0)], rate_mat
    )
    down_all = renew_wide(ffn_out, ffn_out_mom, ffn_out_avg, [(down_grad, 0)], rate_mat)
    gu_all, heads_part = tie((gu_all, heads_part))
    heads_grad = by_device(heads_part)
    heads_grad, d_gain_two = tie((heads_grad, d_gain_two))
    sum_gains = jnp.sum(
        lax.all_to_all(
            jnp.stack([d_gain_two, d_gain_four]).reshape(2, device_count, -1).transpose(1, 0, 2),
            ("grp", "seq"),
            split_axis=0,
            concat_axis=0,
            tiled=True,
        ),
        axis=0,
    )
    (layer_grad,) = norm_call(
        input_back_kernel,
        "input_back",
        all_rows,
        model_width,
        [own, by_x, by_y, tokens.reshape(all_rows, model_width), d_middle],
        [gain_vals[:1]],
        [jnp.float32],
    )
    layer_grad = layer_grad.reshape(tokens.shape)
    qkv_all, out_all, qkv_product = renew_heads(
        heads_grad,
        (attn_in, attn_in_mom, attn_in_avg),
        (attn_out, attn_out_mom, attn_out_avg),
        rate_mat,
    )
    gu_new, gu_mom, gu_avg, gu_copy, gu_product = gu_all
    down_new, down_mom, down_avg, down_copy, _ = down_all
    out_new, out_mom, out_avg, out_copy = out_all
    qkv_new, qkv_mom, qkv_avg, qkv_copy = qkv_all
    own_gains = low(gains).astype(jnp.float32)
    sum_gain = jnp.stack(
        [
            qkv_product[:, 0] / own_gains[0],
            sum_gains[0],
            gu_product[:, 0] / own_gains[2],
            sum_gains[1],
        ]
    )
    gain_new, gain_mom, gain_avg, gain_copy = renew(
        gains, gains_mom, gains_avg, sum_gain, rate_gain
    )
    return (
        layer_out,
        layer_grad,
        qkv_new,
        qkv_mom,
        qkv_avg,
        qkv_copy,
        out_new,
        out_mom,
        out_avg,
        out_copy,
        gu_new,
        gu_mom,
        gu_avg,
        gu_copy,
        down_new,
        down_mom,
        down_avg,
        down_copy,
        gain_new,
        gain_mom,
        gain_avg,
        gain_copy,
    )


def solution(mesh):
    placed = (
        P(None, ("grp", "seq"), None),
        P(None, ("grp", "seq"), None),
        P(None, "grp"),
        P(("grp", "seq"), None),
        P(("grp", "seq"), None),
        P(("grp", "seq"), None),
        P(("grp", "seq"), None),
        P(None, ("grp", "seq")),
        P(("grp", "seq"), None),
        P(("grp", "seq"), None),
        P(("grp", "seq"), None),
        P(("grp", "seq"), None),
        P(None, ("grp", "seq")),
        P(("grp", "seq"), None),
        P(("grp", "seq"), None),
        P(("grp", "seq"), None),
        P(("grp", "seq"), None),
        P(None, ("grp", "seq")),
    )
    heads_fit = mesh.shape["seq"] == HEADS
    return jax.shard_map(
        by_heads if heads_fit else by_rows,
        mesh=mesh,
        in_specs=placed,
        out_specs=(
            P(None, ("grp", "seq"), None),
            P(None, ("grp", "seq"), None),
            P(("grp", "seq"), None),
            P(("grp", "seq"), None),
            P(("grp", "seq"), None),
            P(("grp", "seq"), None),
            P(("grp", "seq"), None),
            P(("grp", "seq"), None),
            P(("grp", "seq"), None),
            P(("grp", "seq"), None),
            P(("grp", "seq"), None),
            P(("grp", "seq"), None),
            P(("grp", "seq"), None),
            P(("grp", "seq"), None),
            P(("grp", "seq"), None),
            P(("grp", "seq"), None),
            P(("grp", "seq"), None),
            P(("grp", "seq"), None),
            P(None, ("grp", "seq")),
            P(None, ("grp", "seq")),
            P(None, ("grp", "seq")),
            P(None, ("grp", "seq")),
        ),
        check_vma=False,
    )
```

```python
import functools

import jax
import jax.numpy as jnp
from jax import lax
from jax.experimental import pallas as pl
from jax.experimental.layout import Layout, with_layout_constraint
from jax.experimental.pallas import tpu as pltpu
from jax.sharding import PartitionSpec as P

HEADS = 8
KV_HEADS = 4
HEAD = 256
PROMPT = 1024
CONTS = 8


eps_norm = 1e-06
soft_cap = 50.0
momentum_decay = 0.5
average_decay = 0.5
weight_rate = 0.03
gain_rate = 0.2
rope_base = 10000.0
GELU_SCALE = (2.0 / 3.141592653589793) ** 0.5


def scaled(field, gain):
    return field * lax.rsqrt(jnp.mean(field * field, axis=-1, keepdims=True) + eps_norm) * gain


def place_tokens(seg_group, own_segment, row_index):
    levels = jnp.arange(CONTS + 1, dtype=jnp.int32)
    before = jnp.sum((seg_group[None, :] < levels[:, None]).astype(jnp.int32), axis=1)
    seg_start = jnp.sum(
        jnp.where(own_segment[:, None] == levels[None, :], before[None, :], 0), axis=1
    )
    return row_index - seg_start + jnp.where(own_segment > 0, PROMPT, 0)


def rotate(field, positions):
    half = field.shape[-1] // 2
    freqs = rope_base ** (-jnp.arange(half, dtype=jnp.float32) * 2.0 / field.shape[-1])
    angles = positions.astype(jnp.float32)[:, None] * freqs[None, :]
    cosine = jnp.cos(angles)[:, None, :]
    sine = jnp.sin(angles)[:, None, :]
    first_half = field[..., :half]
    second_half = field[..., half:]
    return jnp.concatenate(
        [first_half * cosine - second_half * sine, second_half * cosine + first_half * sine],
        axis=-1,
    )


def glu_part(gate, upper):
    return jax.nn.gelu(gate, approximate=True) * upper


def contract_rows(left, right):
    return lax.dot_general(
        left, right, (((0,), (0,)), ((), ())), preferred_element_type=jnp.float32
    )


def contract_cols(left, right):
    return lax.dot_general(
        left, right, (((1,), (1,)), ((), ())), preferred_element_type=jnp.float32
    )


def renew(weight, moment, average, gradient, step_rate):
    moment_new = momentum_decay * moment + gradient
    weight_new = weight - step_rate * (gradient + momentum_decay * moment_new)
    average_new = average_decay * average + (1.0 - average_decay) * weight_new
    return (weight_new, moment_new, average_new, weight_new.astype(jnp.bfloat16))


def by_rows(
    tokens,
    cotangent,
    segments,
    attn_in,
    attn_out,
    ffn_in,
    ffn_out,
    gains,
    attn_in_mom,
    attn_out_mom,
    ffn_in_mom,
    ffn_out_mom,
    gains_mom,
    attn_in_avg,
    attn_out_avg,
    ffn_in_avg,
    ffn_out_avg,
    gains_avg,
):
    micro_count = tokens.shape[0]
    local_rows = tokens.shape[1]
    all_rows = micro_count * local_rows
    model_width = tokens.shape[2]
    row_offset = lax.axis_index("seq") * local_rows
    row_index = row_offset + jnp.arange(local_rows, dtype=jnp.int32)
    key_index = jnp.arange(segments.shape[1], dtype=jnp.int32)
    query_width = HEADS * HEAD
    kv_width = KV_HEADS * HEAD
    share = HEADS // KV_HEADS
    ffn_width = ffn_out.shape[1]
    own_rows = ffn_in.shape[0]
    score_scale = HEAD ** (-0.5)
    own_segments = lax.dynamic_slice_in_dim(segments, row_offset, local_rows, 1)
    positions = jax.vmap(
        lambda seg_group, own_segment: place_tokens(seg_group, own_segment, row_index)
    )(segments, own_segments).reshape(all_rows)
    visible = (key_index[None, None, :] <= row_index[None, :, None]) & (
        (segments[:, None, :] == 0) | (segments[:, None, :] == own_segments[:, :, None])
    )
    inputs = tokens.astype(jnp.float32).reshape(all_rows, model_width)
    w_qkv, w_o, gain_low = (
        lax.all_gather(attn_in.astype(jnp.bfloat16), ("grp", "seq"), axis=0, tiled=True),
        lax.all_gather(attn_out.astype(jnp.bfloat16), ("grp", "seq"), axis=0, tiled=True),
        lax.all_gather(gains.astype(jnp.bfloat16), ("grp", "seq"), axis=1, tiled=True),
    )
    gain_vals = gain_low.astype(jnp.float32)
    normed_one, norm_one_back = jax.vjp(scaled, inputs, gain_vals[0])
    normed_one = normed_one.astype(jnp.bfloat16)
    projected = jnp.dot(normed_one, w_qkv, preferred_element_type=jnp.float32)
    query_rot, query_back = jax.vjp(
        lambda field: rotate(field, positions),
        projected[:, :query_width].reshape(all_rows, HEADS, HEAD),
    )
    key_rot, key_back = jax.vjp(
        lambda field: rotate(field, positions),
        projected[:, query_width : query_width + kv_width].reshape(all_rows, KV_HEADS, HEAD),
    )
    query_low = query_rot.astype(jnp.bfloat16).reshape(
        micro_count, local_rows, KV_HEADS, share, HEAD
    )
    key_low = key_rot.astype(jnp.bfloat16).reshape(micro_count, local_rows, kv_width)
    value_low = (
        projected[:, query_width + kv_width :]
        .astype(jnp.bfloat16)
        .reshape(micro_count, local_rows, kv_width)
    )
    group_key_rows, group_values = (
        lax.all_gather(key_low, "seq", axis=1, tiled=True),
        lax.all_gather(value_low, "seq", axis=1, tiled=True),
    )
    group_key_rows = group_key_rows.reshape(micro_count, -1, KV_HEADS, HEAD)
    group_values = group_values.reshape(micro_count, -1, KV_HEADS, HEAD)

    def probabilities(raw_scores):
        capped = jnp.where(
            visible[:, None, None], soft_cap * jnp.tanh(raw_scores / soft_cap), -1e30
        )
        return jax.nn.softmax(capped, axis=-1)

    raw_scores = (
        jnp.einsum(
            "mtgrd,mkgd->mgrtk", query_low, group_key_rows, preferred_element_type=jnp.float32
        )
        * score_scale
    )
    attention, attention_back = jax.vjp(probabilities, raw_scores)
    attention_low = attention.astype(jnp.bfloat16)
    mixed_heads = jnp.einsum(
        "mgrtk,mkgd->mtgrd", attention_low, group_values, preferred_element_type=jnp.float32
    )
    mixed_low = mixed_heads.reshape(all_rows, query_width).astype(jnp.bfloat16)
    branch = contract_cols(mixed_low, w_o)
    normed_two, norm_two_back = jax.vjp(scaled, branch, gain_vals[1])
    middle = inputs + normed_two
    normed_three, norm_three_back = jax.vjp(scaled, middle, gain_vals[2])
    normed_three = normed_three.astype(jnp.bfloat16)
    grad_top = cotangent.astype(jnp.float32).reshape(all_rows, model_width)
    seq_count = lax.axis_size("seq")
    grp_count = lax.axis_size("grp")
    slice_width = ffn_width // seq_count
    stacked = jnp.concatenate(
        [
            ffn_in.astype(jnp.bfloat16).reshape(own_rows, 2, seq_count, slice_width),
            ffn_out.astype(jnp.bfloat16).reshape(own_rows, 1, seq_count, slice_width),
        ],
        axis=1,
    )
    spread = jnp.broadcast_to(
        stacked[:, :, None], (own_rows, 3, grp_count, seq_count, slice_width)
    ).reshape(own_rows, 3, grp_count * seq_count, slice_width)
    w_cols = lax.all_to_all(
        spread, ("grp", "seq"), split_axis=2, concat_axis=0, tiled=True
    ).reshape(model_width, 3, slice_width)
    w_gu_cols = w_cols[:, :2].reshape(model_width, 2 * slice_width)
    w_d_cols = w_cols[:, 2]
    norm_rows = lax.all_gather(normed_three, "seq", axis=0, tiled=True)
    gate_up = jnp.dot(norm_rows, w_gu_cols, preferred_element_type=jnp.float32)
    hidden, glu_back = jax.vjp(glu_part, gate_up[:, :slice_width], gate_up[:, slice_width:])
    hidden = hidden.astype(jnp.bfloat16)
    ffn_branch = lax.psum_scatter(
        contract_cols(hidden, w_d_cols), "seq", scatter_dimension=0, tiled=True
    )
    normed_four, norm_four_back = jax.vjp(scaled, ffn_branch, gain_vals[3])
    layer_out = (
        (middle + normed_four).astype(jnp.bfloat16).reshape(micro_count, local_rows, model_width)
    )
    d_ffn, d_gain_four = norm_four_back(grad_top)
    d_ffn_all = lax.all_gather(d_ffn.astype(jnp.bfloat16), "seq", axis=0, tiled=True)
    d_hidden = jnp.dot(d_ffn_all, w_d_cols, preferred_element_type=jnp.float32)
    grad_d_cols = contract_rows(d_ffn_all, hidden)
    d_gate, d_upper = glu_back(d_hidden)
    d_gate_up = jnp.concatenate([d_gate, d_upper], axis=1).astype(jnp.bfloat16)
    grad_gu_cols = contract_rows(norm_rows, d_gate_up)
    d_normed_three = lax.psum_scatter(
        contract_cols(d_gate_up, w_gu_cols), "seq", scatter_dimension=0, tiled=True
    )
    local_grads = jnp.concatenate(
        [grad_gu_cols.reshape(model_width, 2, slice_width), grad_d_cols[:, None, :]], axis=1
    ).reshape(model_width, 3, 1, slice_width)
    returned = lax.all_to_all(
        local_grads.astype(jnp.bfloat16), ("grp", "seq"), split_axis=0, concat_axis=2, tiled=True
    ).astype(local_grads.dtype)
    grad_ffn = jnp.sum(
        returned.reshape(own_rows, 3, grp_count, seq_count, slice_width), axis=2
    ).reshape(own_rows, 3 * ffn_width)
    d_middle_norm, d_gain_three = norm_three_back(d_normed_three)
    d_middle = grad_top + d_middle_norm
    sum_gu = grad_ffn[:, : 2 * ffn_width]
    sum_down = grad_ffn[:, 2 * ffn_width :]
    d_branch, d_gain_two = norm_two_back(d_middle)
    d_branch_low = d_branch.astype(jnp.bfloat16)
    grad_out = contract_rows(d_branch_low, mixed_low)
    d_mixed = jnp.dot(d_branch_low, w_o, preferred_element_type=jnp.float32)
    d_mixed_low = d_mixed.astype(jnp.bfloat16).reshape(
        micro_count, local_rows, KV_HEADS, share, HEAD
    )
    d_attention = jnp.einsum(
        "mtgrd,mkgd->mgrtk", d_mixed_low, group_values, preferred_element_type=jnp.float32
    )
    (d_raw,) = attention_back(d_attention)
    d_raw_low = d_raw.astype(jnp.bfloat16)
    d_query = (
        jnp.einsum(
            "mgrtk,mkgd->mtgrd", d_raw_low, group_key_rows, preferred_element_type=jnp.float32
        )
        * score_scale
    )
    d_group_keys = (
        jnp.einsum("mgrtk,mtgrd->mkgd", d_raw_low, query_low, preferred_element_type=jnp.float32)
        * score_scale
    )
    d_group_values = jnp.einsum(
        "mgrtk,mtgrd->mkgd", attention_low, d_mixed_low, preferred_element_type=jnp.float32
    )
    d_keys, d_values = (
        lax.psum_scatter(
            d_group_keys.reshape(micro_count, -1, kv_width).astype(jnp.bfloat16),
            "seq",
            scatter_dimension=1,
            tiled=True,
        ).astype(jnp.float32),
        lax.psum_scatter(
            d_group_values.reshape(micro_count, -1, kv_width).astype(jnp.bfloat16),
            "seq",
            scatter_dimension=1,
            tiled=True,
        ).astype(jnp.float32),
    )
    (d_query_raw,) = query_back(d_query.reshape(all_rows, HEADS, HEAD))
    (d_key_raw,) = key_back(d_keys.reshape(all_rows, KV_HEADS, HEAD))
    d_projected = jnp.concatenate(
        [
            d_query_raw.reshape(all_rows, query_width),
            d_key_raw.reshape(all_rows, kv_width),
            d_values.reshape(all_rows, kv_width),
        ],
        axis=1,
    ).astype(jnp.bfloat16)
    grad_qkv = contract_rows(normed_one, d_projected)
    d_normed_one = contract_cols(d_projected, w_qkv)
    d_input_norm, d_gain_one = norm_one_back(d_normed_one)
    layer_grad = (d_middle + d_input_norm).reshape(micro_count, local_rows, model_width)
    d_gains = jnp.stack([d_gain_one, d_gain_two, d_gain_three, d_gain_four])
    part_qkv, part_out, part_gain = (
        lax.psum_scatter(
            grad_qkv.astype(jnp.bfloat16), "grp", scatter_dimension=0, tiled=True
        ).astype(jnp.float32),
        lax.psum_scatter(
            grad_out.astype(jnp.bfloat16), "grp", scatter_dimension=0, tiled=True
        ).astype(jnp.float32),
        lax.psum_scatter(
            d_gains.astype(jnp.bfloat16), "grp", scatter_dimension=1, tiled=True
        ).astype(jnp.float32),
    )
    sum_qkv, sum_out, sum_gain = (
        lax.psum_scatter(
            part_qkv.astype(jnp.bfloat16), "seq", scatter_dimension=0, tiled=True
        ).astype(jnp.float32),
        lax.psum_scatter(
            part_out.astype(jnp.bfloat16), "seq", scatter_dimension=0, tiled=True
        ).astype(jnp.float32),
        lax.psum_scatter(
            part_gain.astype(jnp.bfloat16), "seq", scatter_dimension=1, tiled=True
        ).astype(jnp.float32),
    )
    token_total = micro_count * local_rows * lax.axis_size(("grp", "seq"))
    rate_mat = weight_rate * token_total ** (-0.5)
    rate_gain = gain_rate * token_total ** (-0.5)
    qkv_new, qkv_mom, qkv_avg, qkv_copy = renew(
        attn_in, attn_in_mom, attn_in_avg, sum_qkv, rate_mat
    )
    out_new, out_mom, out_avg, out_copy = renew(
        attn_out, attn_out_mom, attn_out_avg, sum_out, rate_mat
    )
    gu_new, gu_mom, gu_avg, gu_copy = renew(ffn_in, ffn_in_mom, ffn_in_avg, sum_gu, rate_mat)
    down_new, down_mom, down_avg, down_copy = renew(
        ffn_out, ffn_out_mom, ffn_out_avg, sum_down, rate_mat
    )
    gain_new, gain_mom, gain_avg, gain_copy = renew(
        gains, gains_mom, gains_avg, sum_gain, rate_gain
    )
    return (
        layer_out,
        layer_grad,
        qkv_new,
        qkv_mom,
        qkv_avg,
        qkv_copy,
        out_new,
        out_mom,
        out_avg,
        out_copy,
        gu_new,
        gu_mom,
        gu_avg,
        gu_copy,
        down_new,
        down_mom,
        down_avg,
        down_copy,
        gain_new,
        gain_mom,
        gain_avg,
        gain_copy,
    )


VMEM_LIMIT = 48 * 1024 * 1024


def permute(field, offset):
    count = lax.axis_size("seq")
    return lax.ppermute(field, "seq", [(i, i ^ offset) for i in range(count)])


def gather_near(field):
    return field, permute(field, 2), permute(field, 4)


def gather_mine(field, by_x, by_y):
    half = field.shape[0] // 2
    far = [permute(by_x[:half], 4), permute(by_y[half:], 2)]
    return jnp.concatenate([field, by_x, by_y] + far, axis=0)


def gather_far(field, by_x, by_y):
    mine = gather_mine(field, by_x, by_y)
    return [mine, permute(mine, 1)]


def gather_pieces(field):
    return gather_far(*gather_near(field))


def add_low(left, right):
    return (left.astype(jnp.float32) + right.astype(jnp.float32)).astype(jnp.bfloat16)


def sum_far(own, by_x, by_y, far):
    half = own.shape[0] // 2
    far_x = permute(far[:half], 2)
    far_y = permute(far[half:], 4)
    by_y = jnp.concatenate([add_low(by_y[:half], far_x), by_y[half:]], axis=0)
    by_x = jnp.concatenate([by_x[:half], add_low(by_x[half:], far_y)], axis=0)
    return own, by_x, by_y


def sum_near(own, by_x, by_y):
    return own.astype(jnp.float32) + by_x.astype(jnp.float32) + by_y.astype(jnp.float32)


def sum_pairs(*blocks):
    own, by_x, by_y = sum_far(*blocks)
    return sum_near(own, permute(by_x, 2), permute(by_y, 4))


def pair_products(mine, other, weight):
    rows = mine.shape[0] // 4
    ends = []
    for here in (slice(3 * rows, None), slice(None, 3 * rows)):
        moved = permute(low(contract_cols(other[here], weight)), 1)
        ends.append(add_low(low(contract_cols(mine[here], weight)), moved))
    far, near = ends
    return near[:rows], near[rows : 2 * rows], near[2 * rows :], far


def pair_halves(mine, other, weight):
    moved = permute(low(contract_cols(other, weight)), 1)
    total = add_low(low(contract_cols(mine, weight)), moved)
    rows = total.shape[0] // 4
    return [total[at * rows : (at + 1) * rows] for at in range(4)]


def sum_products(mine, other, weight):
    return sum_pairs(*pair_products(mine, other, weight))


def piece_order(blocks):
    index = lax.axis_index("seq")
    count = blocks.shape[0]
    bits = count.bit_length() - 1
    split = blocks.reshape((2,) * bits + blocks.shape[1:])
    for bit in range(bits):
        axis = bits - 1 - bit
        split = jnp.where((index >> bit) & 1 == 1, jnp.flip(split, axis), split)
    return jnp.swapaxes(split.reshape((count // 2, 2) + blocks.shape[1:]), 0, 1).reshape(blocks.shape)


def qkv_columns(device):
    return [device, HEADS + (device % 2) * KV_HEADS + device // 2]


def out_columns(device):
    return [device]


def spread_kernel(count, blocks, field_ref, out_ref):
    parts = len(blocks(0))
    width = out_ref.shape[2] // parts
    for device in range(count):
        for part, block in enumerate(blocks(device)):
            out_ref[device, :, part * width : (part + 1) * width] = field_ref[
                :, block * width : (block + 1) * width
            ].astype(jnp.bfloat16)


def spread(field, count, blocks):
    rows, columns = field.shape
    return pl.pallas_call(
        functools.partial(spread_kernel, count, blocks),
        out_shape=jax.ShapeDtypeStruct((count, rows, columns // count), jnp.bfloat16),
        cost_estimate=pl.CostEstimate(flops=0, transcendentals=0, bytes_accessed=6 * field.size),
        compiler_params=pltpu.CompilerParams(vmem_limit_bytes=VMEM_LIMIT),
        name="spread",
    )(field)


def row_product(weight, gradient):
    used = weight.astype(jnp.bfloat16).astype(jnp.float32)
    return jnp.sum(used * gradient, axis=1, keepdims=True)


def renew_kernel(rate, w_ref, m_ref, a_ref, g_ref, w_out, m_out, a_out, c_out, product_out):
    gradient = g_ref[0].astype(jnp.float32)
    w_new, m_new, a_new, copy = renew(w_ref[...], m_ref[...], a_ref[...], gradient, rate)
    product_out[...] += row_product(w_ref[...], gradient)
    w_out[...] = w_new
    m_out[...] = m_new
    a_out[...] = a_new
    c_out[...] = copy


def renew_parts_kernel(rate, w_ref, m_ref, a_ref, *refs):
    g_refs, outs = refs[:-5], refs[-5:]

    @pl.when((pl.program_id(0) == 0) & (pl.program_id(1) == 0))
    def _():
        outs[-1][...] = jnp.zeros_like(outs[-1])

    for part, g_ref in enumerate(g_refs):

        @pl.when(pl.program_id(1) == part)
        def _(g_ref=g_ref):
            renew_kernel(rate, w_ref, m_ref, a_ref, g_ref, *outs)


def renew_wide(weight, moment, average, gradients, rate):
    rows, columns = weight.shape
    parts = len(gradients)
    count = gradients[0][0].shape[0]
    width = columns // (count * parts)
    own = pl.BlockSpec((rows, width), lambda d, p: (0, p * count + d))

    def of_block(block):
        return pl.BlockSpec((1, rows, width), lambda d, p: (d, 0, block))

    return pl.pallas_call(
        functools.partial(renew_parts_kernel, rate),
        grid=(count, parts),
        in_specs=[own, own, own] + [of_block(block) for _, block in gradients],
        out_specs=[own, own, own, own, pl.BlockSpec((rows, 1), lambda d, p: (0, 0))],
        out_shape=[jax.ShapeDtypeStruct((rows, columns), jnp.float32)] * 3
        + [
            jax.ShapeDtypeStruct((rows, columns), jnp.bfloat16),
            jax.ShapeDtypeStruct((rows, 1), jnp.float32),
        ],
        cost_estimate=pl.CostEstimate(
            flops=8 * weight.size, transcendentals=0, bytes_accessed=28 * weight.size
        ),
        compiler_params=pltpu.CompilerParams(vmem_limit_bytes=VMEM_LIMIT),
        name="renew",
    )(weight, moment, average, *(array for array, _ in gradients))


def renew_heads_kernel(rate, g_ref, *refs):
    product = jnp.zeros(refs[-1].shape, jnp.float32)
    for device in range(g_ref.shape[0]):
        blocks = [(0, block) for block in qkv_columns(device)] + [(1, device)]
        for part, (which, block) in enumerate(blocks):
            w_ref, m_ref, a_ref = refs[3 * which : 3 * which + 3]
            outs = refs[6 + 4 * which : 10 + 4 * which]
            here = (slice(None), slice(block * HEAD, (block + 1) * HEAD))
            gradient = g_ref[device, : w_ref.shape[0], part * HEAD : (part + 1) * HEAD].astype(
                jnp.float32
            )
            results = renew(w_ref[here], m_ref[here], a_ref[here], gradient, rate)
            for out, result in zip(outs, results):
                out[here] = result
            if which == 0:
                product += row_product(w_ref[here], gradient)
    refs[-1][...] = product


def renew_heads(gradient, attn_in, attn_out, rate):
    kinds = (jnp.float32, jnp.float32, jnp.float32, jnp.bfloat16)
    shapes = [
        jax.ShapeDtypeStruct(state[0].shape, kind) for state in (attn_in, attn_out) for kind in kinds
    ]
    size = attn_in[0].size + attn_out[0].size
    results = pl.pallas_call(
        functools.partial(renew_heads_kernel, rate),
        out_shape=shapes + [jax.ShapeDtypeStruct((attn_in[0].shape[0], 1), jnp.float32)],
        cost_estimate=pl.CostEstimate(flops=8 * size, transcendentals=0, bytes_accessed=28 * size),
        compiler_params=pltpu.CompilerParams(vmem_limit_bytes=VMEM_LIMIT),
        name="renew_heads",
    )(gradient, *attn_in, *attn_out)
    return results[:4], results[4:8], results[8]


def glu_kernel(rows_ref, w_ref, gate_up_ref, hidden_ref):
    width = hidden_ref.shape[1]
    gate_up = jnp.dot(rows_ref[...], w_ref[...], preferred_element_type=jnp.float32)
    gate_up_ref[...] = gate_up
    gate, upper = gate_up[:, :width], gate_up[:, width:]
    bent = jnp.tanh(GELU_SCALE * gate * (1.0 + 0.044715 * gate * gate))
    hidden_ref[...] = (0.5 * gate * (1.0 + bent) * upper).astype(jnp.bfloat16)


def glu_rows(field, weight):
    rows, depth = field.shape
    width = weight.shape[1] // 2
    tile = rows // 6
    return pl.pallas_call(
        glu_kernel,
        grid=(rows // tile,),
        in_specs=[
            pl.BlockSpec((tile, depth), lambda i: (i, 0)),
            pl.BlockSpec(weight.shape, lambda i: (0, 0)),
        ],
        out_specs=[
            pl.BlockSpec((tile, 2 * width), lambda i: (i, 0)),
            pl.BlockSpec((tile, width), lambda i: (i, 0)),
        ],
        out_shape=[
            jax.ShapeDtypeStruct((rows, 2 * width), jnp.float32),
            jax.ShapeDtypeStruct((rows, width), jnp.bfloat16),
        ],
        cost_estimate=pl.CostEstimate(
            flops=4 * rows * depth * width,
            transcendentals=rows * width,
            bytes_accessed=rows * (2 * depth + 10 * width) + 4 * depth * width,
        ),
        compiler_params=pltpu.CompilerParams(vmem_limit_bytes=VMEM_LIMIT),
        name="glu",
    )(field, weight)


def glu_back_kernel(left0_ref, left1_ref, w0_ref, w1_ref, gate_up_ref, out_ref):
    width = w0_ref.shape[1]
    d_hidden = jnp.dot(left0_ref[...], w0_ref[...], preferred_element_type=jnp.float32)
    d_hidden += jnp.dot(left1_ref[...], w1_ref[...], preferred_element_type=jnp.float32)
    gate = gate_up_ref[:, :width]
    upper = gate_up_ref[:, width:]
    square = gate * gate
    bent = jnp.tanh(GELU_SCALE * gate * (1.0 + 0.044715 * square))
    rise = 0.5 * (1.0 + bent)
    slope = rise + 0.5 * gate * (1.0 - bent * bent) * GELU_SCALE * (1.0 + 3 * 0.044715 * square)
    out_ref[:, :width] = (d_hidden * upper * slope).astype(jnp.bfloat16)
    out_ref[:, width:] = (d_hidden * gate * rise).astype(jnp.bfloat16)


def glu_back_rows(left0, left1, w0, w1, gate_up):
    rows = left0.shape[0]
    width = w0.shape[1]
    tile = rows // 6
    return pl.pallas_call(
        glu_back_kernel,
        grid=(rows // tile,),
        in_specs=[
            pl.BlockSpec((tile, left0.shape[1]), lambda i: (i, 0)),
            pl.BlockSpec((tile, left1.shape[1]), lambda i: (i, 0)),
            pl.BlockSpec(w0.shape, lambda i: (0, 0)),
            pl.BlockSpec(w1.shape, lambda i: (0, 0)),
            pl.BlockSpec((tile, 2 * width), lambda i: (i, 0)),
        ],
        out_specs=pl.BlockSpec((tile, 2 * width), lambda i: (i, 0)),
        out_shape=jax.ShapeDtypeStruct((rows, 2 * width), jnp.bfloat16),
        cost_estimate=pl.CostEstimate(
            flops=2 * rows * (w0.shape[0] + w1.shape[0]) * width,
            transcendentals=rows * width,
            bytes_accessed=rows * (2 * (left0.shape[1] + left1.shape[1]) + 12 * width),
        ),
        compiler_params=pltpu.CompilerParams(vmem_limit_bytes=VMEM_LIMIT),
        name="glu_back",
    )(left0, left1, w0, w1, gate_up)


def norm_tiles(rows, width, kinds):
    tile = rows // 3
    return [
        pl.BlockSpec((tile, width), lambda i: (i, 0))
        if kind
        else pl.BlockSpec((1, width), lambda i: (0, 0))
        for kind in kinds
    ]


def norm_call(kernel, name, rows, width, fields, gains, outs):
    specs = norm_tiles(rows, width, [1] * len(fields) + [0] * len(gains))
    return pl.pallas_call(
        kernel,
        grid=(3,),
        in_specs=specs,
        out_specs=norm_tiles(rows, width, [out is not None for out in outs]),
        out_shape=[
            jax.ShapeDtypeStruct((rows, width), out)
            if out is not None
            else jax.ShapeDtypeStruct((1, width), jnp.float32)
            for out in outs
        ],
        cost_estimate=pl.CostEstimate(
            flops=20 * rows * width, transcendentals=0, bytes_accessed=20 * rows * width
        ),
        compiler_params=pltpu.CompilerParams(vmem_limit_bytes=VMEM_LIMIT // 2),
        name=name,
    )(*fields, *gains)


def row_inverse(field):
    return lax.rsqrt(jnp.mean(field * field, axis=1, keepdims=True) + eps_norm)


def row_back(field, inverse, top):
    inner = jnp.mean(field * top, axis=1, keepdims=True)
    return inverse * top - field * (inverse * inverse * inverse * inner)


def read_sum(own_ref, by_x_ref, by_y_ref):
    return (
        own_ref[...].astype(jnp.float32)
        + by_x_ref[...].astype(jnp.float32)
        + by_y_ref[...].astype(jnp.float32)
    )


def middle_kernel(own_ref, by_x_ref, by_y_ref, token_ref, g1_ref, g2_ref, branch_ref, middle_ref, out_ref):
    branch = read_sum(own_ref, by_x_ref, by_y_ref)
    branch_ref[...] = branch
    middle = token_ref[...].astype(jnp.float32) + branch * row_inverse(branch) * g1_ref[...]
    middle_ref[...] = middle
    out_ref[...] = (middle * row_inverse(middle) * g2_ref[...]).astype(jnp.bfloat16)


def middle_back_kernel(
    own_ref,
    by_x_ref,
    by_y_ref,
    top_ref,
    branch_ref,
    middle_ref,
    g1_ref,
    g2_ref,
    d_middle_ref,
    d_branch_ref,
    d_gain_ref,
):
    middle, branch = middle_ref[...], branch_ref[...]
    d_normed = read_sum(own_ref, by_x_ref, by_y_ref)
    d_middle = top_ref[...].astype(jnp.float32) + row_back(
        middle, row_inverse(middle), g2_ref[...] * d_normed
    )
    d_middle_ref[...] = d_middle
    inverse = row_inverse(branch)
    d_branch_ref[...] = row_back(branch, inverse, g1_ref[...] * d_middle).astype(jnp.bfloat16)

    @pl.when(pl.program_id(0) == 0)
    def _():
        d_gain_ref[...] = jnp.zeros_like(d_gain_ref)

    d_gain_ref[...] += jnp.sum(d_middle * (branch * inverse), axis=0, keepdims=True)


def input_back_kernel(own_ref, by_x_ref, by_y_ref, token_ref, d_middle_ref, g0_ref, out_ref):
    token = token_ref[...].astype(jnp.float32)
    d_normed = read_sum(own_ref, by_x_ref, by_y_ref)
    out_ref[...] = d_middle_ref[...] + row_back(token, row_inverse(token), g0_ref[...] * d_normed)


def across(left, right):
    return lax.dot_general(
        left, right, (((1,), (1,)), ((), ())), preferred_element_type=jnp.float32
    )


def down(left, right):
    return lax.dot_general(
        left, right, (((0,), (0,)), ((), ())), preferred_element_type=jnp.float32
    )


def attend_kernel(q_ref, k_ref, v_ref, key_ref, query_ref, out_ref, weights_ref, slopes_ref):
    bent = jnp.tanh(across(k_ref[0], q_ref[0]) * (HEAD ** (-0.5) / soft_cap))
    key, query = key_ref[0][:, :1], query_ref[0]
    seg_k, seg_q = key & 15, query & 15
    seen = ((key >> 4) <= (query >> 4)) & ((seg_k == 0) | (seg_k == seg_q))
    capped = jnp.where(seen, soft_cap * bent, -1e30)
    top = jnp.max(capped, axis=0, keepdims=True)
    powers = jnp.exp(capped - top)
    weights = powers * (1.0 / jnp.sum(powers, axis=0, keepdims=True))
    weights_low = weights.astype(jnp.bfloat16)
    weights_ref[0] = weights_low
    slopes_ref[0] = (weights * (1.0 - bent * bent)).astype(jnp.bfloat16)
    out_ref[0] = down(weights_low, v_ref[0]).astype(jnp.bfloat16)


def attend_back_kernel(
    q_ref,
    k_ref,
    v_ref,
    weights_ref,
    slopes_ref,
    cosine_ref,
    sine_ref,
    core_ref,
    d_out_ref,
    dq_ref,
    keep_ref,
    send_ref,
    dk_sum,
    dv_sum,
):
    q, k, v, d_out = q_ref[0], k_ref[0], v_ref[0], d_out_ref[0]
    weights = weights_ref[0]
    d_weights = across(v, d_out)
    inner = jnp.sum(weights.astype(jnp.float32) * d_weights, axis=0, keepdims=True)
    d_raw = (slopes_ref[0].astype(jnp.float32) * (d_weights - inner)).astype(jnp.bfloat16)
    scale = HEAD ** (-0.5)

    @pl.when(pl.program_id(1) == 0)
    def _():
        dk_sum[...] = jnp.zeros_like(dk_sum)
        dv_sum[...] = jnp.zeros_like(dv_sum)

    dq = down(d_raw, k) * scale
    half = HEAD // 2
    cosine, sine = cosine_ref[0], sine_ref[0]
    first, second = dq[:, :half], dq[:, half:]
    dq_ref[0, :, :half] = (first * cosine + second * sine).astype(jnp.bfloat16)
    dq_ref[0, :, half:] = (second * cosine - first * sine).astype(jnp.bfloat16)
    dk_sum[...] += jnp.dot(d_raw, q, preferred_element_type=jnp.float32)
    dv_sum[...] += jnp.dot(weights, d_out, preferred_element_type=jnp.float32)

    @pl.when(pl.program_id(1) == pl.num_programs(1) - 1)
    def _():
        holds_keys = core_ref[:, :1] == 0
        dk, dv = dk_sum[...] * scale, dv_sum[...]
        keep_ref[0] = jnp.where(holds_keys, dk, dv)
        send_ref[0] = jnp.where(holds_keys, dv, dk).astype(jnp.bfloat16)


def attention_cost(micros, rows, products):
    return pl.CostEstimate(
        flops=2 * products * micros * rows * rows * HEAD,
        transcendentals=2 * micros * rows * rows,
        bytes_accessed=4 * products * micros * rows * HEAD,
    )


def attention_specs(rows, tile):
    moving = pl.BlockSpec((1, tile, HEAD), lambda m, i: (m, i, 0))
    whole = pl.BlockSpec((1, rows, HEAD), lambda m, i: (m, 0, 0))
    scores = pl.BlockSpec((1, rows, tile), lambda m, i: (m, 0, i))
    return moving, whole, scores


def attend(q, k, v, places):
    micros, rows, _ = q.shape
    tile = rows // 3
    moving, whole, scores = attention_specs(rows, tile)
    return pl.pallas_call(
        attend_kernel,
        grid=(micros, rows // tile),
        in_specs=[
            moving,
            whole,
            whole,
            pl.BlockSpec((1, rows, 128), lambda m, i: (m, 0, 0)),
            pl.BlockSpec((1, 1, tile), lambda m, i: (m, 0, i)),
        ],
        out_specs=[moving, scores, scores],
        out_shape=[jax.ShapeDtypeStruct(q.shape, jnp.bfloat16)]
        + [jax.ShapeDtypeStruct((micros, rows, rows), jnp.bfloat16)] * 2,
        cost_estimate=attention_cost(micros, rows, 2),
        compiler_params=pltpu.CompilerParams(vmem_limit_bytes=VMEM_LIMIT),
        name="attend",
    )(q, k, v, *places)


def attend_back(q, k, v, weights, slopes, tables, core, d_out):
    micros, rows, _ = q.shape
    tile = rows // 3
    moving, whole, scores = attention_specs(rows, tile)
    turning = pl.BlockSpec((1, tile, HEAD // 2), lambda m, i: (m, i, 0))
    return pl.pallas_call(
        attend_back_kernel,
        grid=(micros, rows // tile),
        in_specs=[moving, whole, whole, scores, scores, turning, turning]
        + [pl.BlockSpec((1, 128), lambda m, i: (0, 0)), moving],
        out_specs=[moving, whole, whole],
        out_shape=[
            jax.ShapeDtypeStruct(q.shape, jnp.bfloat16),
            jax.ShapeDtypeStruct(q.shape, jnp.float32),
            jax.ShapeDtypeStruct(q.shape, jnp.bfloat16),
        ],
        scratch_shapes=[pltpu.VMEM((rows, HEAD), jnp.float32)] * 2,
        cost_estimate=attention_cost(micros, rows, 4),
        compiler_params=pltpu.CompilerParams(vmem_limit_bytes=VMEM_LIMIT),
        name="attend_back",
    )(q, k, v, weights, slopes, *tables, core, d_out)


def exchange(field):
    return lax.all_to_all(field, "seq", split_axis=0, concat_axis=0, tiled=True)


def in_order(step, *operands):
    zeros = jax.eval_shape(step, *operands)
    return lax.cond(
        lax.optimization_barrier(jnp.bool_(True)),
        step,
        lambda *_: jax.tree.map(lambda leaf: jnp.zeros(leaf.shape, leaf.dtype), zeros),
        *operands,
    )


def gather_planes(field):
    return lax.all_gather(field, "grp", axis=0, tiled=True)


def sum_planes(field):
    return lax.psum_scatter(field, "grp", scatter_dimension=0, tiled=True)


def turn(field, cosine, sine):
    half = field.shape[-1] // 2
    first, second = field[..., :half], field[..., half:]
    return jnp.concatenate([first * cosine - second * sine, second * cosine + first * sine], axis=-1)


def low(field):
    return field.astype(jnp.bfloat16)


def dot(left, right):
    return jnp.dot(left, right, preferred_element_type=jnp.float32)


def over_rows(lefts, rights):
    return low(contract_rows(lefts[0], rights[0]) + contract_rows(lefts[1], rights[1]))


def by_heads(
    tokens,
    cotangent,
    segments,
    attn_in,
    attn_out,
    ffn_in,
    ffn_out,
    gains,
    attn_in_mom,
    attn_out_mom,
    ffn_in_mom,
    ffn_out_mom,
    gains_mom,
    attn_in_avg,
    attn_out_avg,
    ffn_in_avg,
    ffn_out_avg,
    gains_avg,
):
    tie = lax.optimization_barrier
    micro_count, local_rows, model_width = tokens.shape
    all_rows = micro_count * local_rows
    seq_count = lax.axis_size("seq")
    grp_count = lax.axis_size("grp")
    device_count = seq_count * grp_count
    group_rows = segments.shape[1]
    own_rows = ffn_in.shape[0]
    plane_rows = own_rows * seq_count
    cut = own_rows * 2 // 3
    slice_width = ffn_out.shape[1] // seq_count
    index = lax.axis_index("seq")
    key_core = index % 2 == 0
    token_total = micro_count * local_rows * device_count
    rate_mat = weight_rate * token_total ** (-0.5)
    rate_gain = gain_rate * token_total ** (-0.5)

    def ffn_columns(device):
        return [device, seq_count + device]

    def by_device(part):
        return exchange(part.reshape(seq_count, own_rows, -1))

    def to_parts(field):
        split = field.reshape(-1, device_count, own_rows)
        return [
            split[:, :, :cut].reshape(field.shape[0], -1),
            split[:, :, cut:].reshape(field.shape[0], -1),
        ]

    def from_parts(parts):
        split = [part.reshape(part.shape[0], device_count, -1) for part in parts]
        return jnp.concatenate(split, axis=2).reshape(-1, model_width)

    def to_groups(field):
        return (
            field.reshape(seq_count, micro_count, local_rows, -1)
            .transpose(1, 0, 2, 3)
            .reshape(micro_count, group_rows, -1)
        )

    def from_groups(field):
        return (
            field.reshape(micro_count, seq_count, local_rows, -1)
            .transpose(1, 0, 2, 3)
            .reshape(seq_count * all_rows, -1)
        )

    def in_two(field):
        return [field[: field.shape[0] // 2], field[field.shape[0] // 2 :]]

    def swap_cores(field):
        first, second = in_two(permute(field, 1))
        return jnp.concatenate([second, first], axis=0)

    heads_moved = exchange(
        jnp.concatenate(
            [spread(attn_in, seq_count, qkv_columns), spread(attn_out, seq_count, out_columns)], axis=2
        )
    ).reshape(plane_rows, 3 * HEAD)
    later_tokens, gains_low, heads_moved = tie((tokens, low(gains), heads_moved))
    w_heads = gather_planes(heads_moved)
    all_gains = lax.all_to_all(
        jnp.broadcast_to(gains_low[None], (device_count,) + gains.shape),
        ("grp", "seq"),
        split_axis=0,
        concat_axis=0,
        tiled=True,
    )
    gain_vals = all_gains.transpose(1, 0, 2).reshape(4, model_width).astype(jnp.float32)
    own_rows_low, by_x, by_y = gather_near(later_tokens.reshape(all_rows, model_width))
    true_rows = jnp.arange(group_rows, dtype=jnp.int32)
    positions = jax.vmap(lambda seg: place_tokens(seg, seg, true_rows))(segments)

    def to_pieces(field):
        return piece_order(field.reshape(micro_count, seq_count, local_rows).transpose(1, 0, 2))

    place = to_pieces(positions).reshape(-1).astype(jnp.float32)
    seg = to_pieces(segments).transpose(1, 0, 2).reshape(micro_count, group_rows)
    row = piece_order(true_rows.reshape(seq_count, local_rows)).reshape(-1)
    freqs = rope_base ** (-jnp.arange(HEAD // 2, dtype=jnp.float32) * 2.0 / HEAD)
    angles = place[:, None] * freqs[None, :]
    cosine, sine = jnp.cos(angles), jnp.sin(angles)
    cosine, sine, kv_cosine, kv_sine, *places = tie(
        (
            cosine,
            sine,
            jnp.where(key_core, cosine, 1.0),
            jnp.where(key_core, sine, 0.0),
            jnp.broadcast_to((16 * row + seg)[:, :, None], seg.shape + (128,)),
            (16 * row + seg)[:, None, :],
        )
    )

    by_x, by_y, later_ffn_in, gain_vals, cosine = tie((by_x, by_y, ffn_in, gain_vals, cosine))
    gu_moved = exchange(spread(later_ffn_in, seq_count, ffn_columns))
    token_rows = gather_far(own_rows_low, by_x, by_y)
    w_gu = gather_planes(gu_moved.reshape(plane_rows, 2 * slice_width))
    down_low = spread(ffn_out, seq_count, out_columns)

    def normed_token_rows(token_rows, inverses):
        return [
            low(part.astype(jnp.float32) * inverse[:, None] * gain_vals[0])
            for part, inverse in zip(token_rows, inverses)
        ]

    def attention(token_rows, w_heads, down_low):
        w_qkv = w_heads[:, : 2 * HEAD]
        down_moved = exchange(down_low)
        inverses = [
            lax.rsqrt(jnp.mean(jnp.square(part.astype(jnp.float32)), axis=1) + eps_norm)
            for part in token_rows
        ]
        projected = jnp.concatenate(
            [dot(part, w_qkv) for part in normed_token_rows(token_rows, inverses)], axis=0
        )
        kv_own = low(turn(projected[:, HEAD:], kv_cosine, kv_sine))
        kv_other = swap_cores(kv_own)
        queries = to_groups(low(turn(projected[:, :HEAD], cosine, sine)))
        keys = to_groups(jnp.where(key_core, kv_own, kv_other))
        values = to_groups(jnp.where(key_core, kv_other, kv_own))
        mixed, weights, slopes = attend(queries, keys, values, places)
        mixed, down_moved = tie((mixed, down_moved))
        mixed_rows = in_two(from_groups(mixed))
        down_rows = [
            part.reshape(-1, slice_width) for part in (down_moved[:, :cut], down_moved[:, cut:])
        ]
        turn_tables = [to_groups(cosine), to_groups(sine)]
        state = (queries, keys, values, weights, slopes)
        return down_rows, inverses, state, mixed_rows, turn_tables

    down_rows, inverses, state, mixed_rows, turn_tables = in_order(
        attention, token_rows, w_heads, down_low
    )
    w_down0, w_down1 = gather_planes(down_rows[0]), gather_planes(down_rows[1])

    def attention_out(mixed_rows, w_heads, tokens, cotangent):
        w_o = w_heads[:, 2 * HEAD :]
        grad_parts = to_parts(cotangent.reshape(all_rows, model_width))
        own, by_x, by_y = sum_far(*pair_products(*mixed_rows, w_o))
        by_x, by_y, *grad_parts = tie((permute(by_x, 2), permute(by_y, 4), *grad_parts))
        branch, middle, normed_three = norm_call(
            middle_kernel,
            "middle",
            all_rows,
            model_width,
            [own, by_x, by_y, tokens.reshape(all_rows, model_width)],
            [gain_vals[1:2], gain_vals[2:3]],
            [jnp.float32, jnp.float32, jnp.bfloat16],
        )
        norm_rows = jnp.concatenate(gather_pieces(normed_three), axis=0)
        return branch, middle, norm_rows, grad_parts

    branch, middle, norm_rows, grad_parts = in_order(
        attention_out, mixed_rows, w_heads, tokens, cotangent
    )
    queries, keys, values, weights, slopes = state

    def feed_up(norm_rows, w_gu):
        return glu_rows(norm_rows, w_gu)

    gate_up, hidden = in_order(feed_up, norm_rows, w_gu)

    def feed_down(hidden, w_down0):
        return sum_products(*in_two(hidden), w_down0)

    ffn0 = in_order(feed_down, hidden, w_down0)
    gain_parts = to_parts(gain_vals[3:])

    def feed_end(hidden, w_down1, ffn0, grad_parts):
        ffn1 = sum_products(*in_two(hidden), w_down1)
        ffns = [ffn0, ffn1]
        squares = sum(jnp.sum(part * part, axis=1, keepdims=True) for part in ffns)
        inverse = lax.rsqrt(squares / model_width + eps_norm)
        tops = [part.astype(jnp.float32) for part in grad_parts]
        scaled_tops = [top * gain for top, gain in zip(tops, gain_parts)]
        inner = sum(
            jnp.sum(top * part, axis=1, keepdims=True) for top, part in zip(scaled_tops, ffns)
        )
        pull = inverse * inverse * inverse * (inner / model_width)
        d_ffns = [low(top * inverse - part * pull) for top, part in zip(scaled_tops, ffns)]
        first = jnp.concatenate(gather_pieces(d_ffns[1]), axis=0)
        return ffn1, inverse, gather_near(d_ffns[0]), first, low(contract_rows(first, hidden))

    ffn1, inverse, second_near, first, grad_down1 = in_order(feed_end, hidden, w_down1, ffn0, grad_parts)

    down_part1 = sum_planes(grad_down1)

    def feed_back(second_near, hidden):
        second = jnp.concatenate(gather_far(*second_near), axis=0)
        return second, low(contract_rows(second, hidden))

    second, grad_down0 = in_order(feed_back, second_near, hidden)
    down_part0 = sum_planes(grad_down0)

    def feed_back_rows(second, first, gate_up, norm_rows, w_down0, w_down1, w_gu, down_part1):
        second, down_part1 = tie((second, down_part1))
        d_gate_up = glu_back_rows(second, first, w_down0, w_down1, gate_up)
        moved = permute(low(contract_cols(d_gate_up[d_gate_up.shape[0] // 2 :], w_gu)), 1)
        grad_gate = low(contract_rows(norm_rows, d_gate_up[:, :slice_width]))
        return d_gate_up, moved, with_layout_constraint(grad_gate, Layout((0, 1))), down_part1

    d_gate_up, d_norm_moved, grad_gate, down_part1 = in_order(
        feed_back_rows, second, first, gate_up, norm_rows, w_down0, w_down1, w_gu, down_part1
    )
    gate_part = sum_planes(grad_gate)

    def middle_back(
        d_norm_moved,
        d_gate_up,
        norm_rows,
        cotangent,
        branch,
        middle,
        w_heads,
        w_gu,
    ):
        w_qkv = w_heads[:, : 2 * HEAD]
        w_pair = jnp.concatenate([w_qkv, permute(w_qkv, 1)], axis=1)
        total = add_low(
            low(contract_cols(d_gate_up[: d_gate_up.shape[0] // 2], w_gu)), d_norm_moved
        )
        rows = total.shape[0] // 4
        own, by_x, by_y = sum_far(*(total[at * rows : (at + 1) * rows] for at in range(4)))
        by_x, by_y, norm_rows = tie((by_x, by_y, norm_rows))
        by_x, by_y = permute(by_x, 2), permute(by_y, 4)
        grad_upper = low(contract_rows(norm_rows, d_gate_up[:, slice_width:]))
        by_x, by_y, grad_upper, w_pair = tie((by_x, by_y, grad_upper, w_pair))
        d_middle, d_branch, d_gain_two = norm_call(
            middle_back_kernel,
            "middle_back",
            all_rows,
            model_width,
            [own, by_x, by_y, cotangent.reshape(all_rows, model_width), branch, middle],
            [gain_vals[1:2], gain_vals[2:3]],
            [jnp.float32, jnp.bfloat16, None],
        )
        return grad_upper, d_middle, d_branch, d_gain_two[0], w_pair

    grad_upper, d_middle, d_branch, d_gain_two, w_pair = in_order(
        middle_back,
        d_norm_moved,
        d_gate_up,
        norm_rows,
        cotangent,
        branch,
        middle,
        w_heads,
        w_gu,
    )
    upper_part = sum_planes(grad_upper)

    core_row = jnp.broadcast_to(index % 2, (1, 128)).astype(jnp.int32)

    def output_rows(d_branch, d_gain_two, middle, ffns, inverse, grad_parts):
        own, by_x, by_y = gather_near(d_branch)
        normeds = [part * inverse for part in ffns]
        d_gain_four = from_parts(
            [
                jnp.sum(top.astype(jnp.float32) * part, axis=0)[None]
                for top, part in zip(grad_parts, normeds)
            ]
        )[0]
        normed_four = from_parts([part * gain for part, gain in zip(normeds, gain_parts)])
        layer_out = low(middle + normed_four).reshape(tokens.shape)
        gain_rows = jnp.concatenate(
            [low(gain).reshape(grp_count, seq_count, own_rows) for gain in (d_gain_two, d_gain_four)],
            axis=2,
        )
        gain_rows = jnp.pad(gain_rows, ((0, 0), (0, 0), (0, 3 * HEAD - 2 * own_rows)))
        by_x, by_y, layer_out, gain_rows = tie((by_x, by_y, layer_out, gain_rows))
        return gather_mine(own, by_x, by_y), gain_rows, layer_out

    d_branch_mine, gain_rows, layer_out = in_order(
        output_rows, d_branch, d_gain_two, middle, [ffn0, ffn1], inverse, grad_parts
    )

    def attention_back(
        d_branch_mine,
        mixed_rows,
        w_heads,
        gate_part,
        down_parts,
        gain_rows,
        token_rows,
        inverses,
        queries,
        keys,
        values,
        weights,
        slopes,
    ):
        gate_grad = by_device(gate_part)
        d_branch_rows = [d_branch_mine, permute(d_branch_mine, 1)]
        d_mixed = to_groups(
            jnp.concatenate([low(dot(part, w_heads[:, 2 * HEAD :])) for part in d_branch_rows], axis=0)
        )
        d_query, keep, send = attend_back(
            queries, keys, values, weights, slopes, turn_tables, core_row, d_mixed
        )
        d_query, keep, send, gate_grad = tie((d_query, keep, send, gate_grad))
        d_kv = from_groups(keep) + swap_cores(from_groups(send)).astype(jnp.float32)
        d_projected = in_two(
            jnp.concatenate(
                [from_groups(d_query), low(turn(d_kv, kv_cosine, -kv_sine))], axis=1
            )
        )
        moved = permute(d_projected[1], 1)
        down_grad = exchange(
            jnp.concatenate(
                [part.reshape(seq_count, -1, slice_width) for part in down_parts], axis=1
            )
        )
        grad_out = over_rows(d_branch_rows, mixed_rows)
        grad_qkv = over_rows(normed_token_rows(token_rows, inverses), d_projected)
        grad_heads = jnp.concatenate(
            [with_layout_constraint(grad, Layout((0, 1))) for grad in (grad_qkv, grad_out)], axis=1
        )
        grad_heads = jnp.concatenate(
            [grad_heads.reshape(grp_count, plane_rows, 3 * HEAD), gain_rows], axis=1
        ).reshape(-1, 3 * HEAD)
        return d_projected[0], moved, grad_heads, gate_grad, down_grad

    d_projected, moved, grad_heads, gate_grad, down_grad = in_order(
        attention_back,
        d_branch_mine,
        mixed_rows,
        w_heads,
        gate_part,
        [down_part0, down_part1],
        gain_rows,
        token_rows,
        inverses,
        queries,
        keys,
        values,
        weights,
        slopes,
    )
    heads_part = sum_planes(grad_heads)

    def update_start(d_projected, moved, w_pair, upper_part):
        upper_grad = by_device(upper_part)
        total = low(contract_cols(jnp.concatenate([d_projected, moved], axis=1), w_pair))
        total, upper_grad = tie((total, upper_grad))
        rows = total.shape[0] // 4
        return sum_far(*(total[at * rows : (at + 1) * rows] for at in range(4))), upper_grad

    (own, by_x, by_y), upper_grad = in_order(
        update_start, d_projected, moved, w_pair, upper_part
    )
    by_x, by_y = permute(by_x, 2), permute(by_y, 4)
    gu_all = renew_wide(
        ffn_in, ffn_in_mom, ffn_in_avg, [(gate_grad, 0), (upper_grad, 0)], rate_mat
    )
    down_all = renew_wide(ffn_out, ffn_out_mom, ffn_out_avg, [(down_grad, 0)], rate_mat)
    gu_all, heads_part = tie((gu_all, heads_part))
    heads_grad = exchange(
        jnp.concatenate(
            [
                heads_part[:plane_rows].reshape(seq_count, own_rows, 3 * HEAD),
                jnp.pad(heads_part[plane_rows:, None], ((0, 0), (0, 7), (0, 0))),
            ],
            axis=1,
        )
    )
    sum_gains = jnp.sum(heads_grad[:, own_rows, : 2 * own_rows].astype(jnp.float32), axis=0)
    sum_gains = sum_gains.reshape(2, own_rows)
    (layer_grad,) = norm_call(
        input_back_kernel,
        "input_back",
        all_rows,
        model_width,
        [own, by_x, by_y, tokens.reshape(all_rows, model_width), d_middle],
        [gain_vals[:1]],
        [jnp.float32],
    )
    layer_grad = layer_grad.reshape(tokens.shape)
    qkv_all, out_all, qkv_product = renew_heads(
        heads_grad,
        (attn_in, attn_in_mom, attn_in_avg),
        (attn_out, attn_out_mom, attn_out_avg),
        rate_mat,
    )
    gu_new, gu_mom, gu_avg, gu_copy, gu_product = gu_all
    down_new, down_mom, down_avg, down_copy, _ = down_all
    out_new, out_mom, out_avg, out_copy = out_all
    qkv_new, qkv_mom, qkv_avg, qkv_copy = qkv_all
    own_gains = low(gains).astype(jnp.float32)
    sum_gain = jnp.stack(
        [
            qkv_product[:, 0] / own_gains[0],
            sum_gains[0],
            gu_product[:, 0] / own_gains[2],
            sum_gains[1],
        ]
    )
    gain_new, gain_mom, gain_avg, gain_copy = renew(
        gains, gains_mom, gains_avg, sum_gain, rate_gain
    )
    return (
        layer_out,
        layer_grad,
        qkv_new,
        qkv_mom,
        qkv_avg,
        qkv_copy,
        out_new,
        out_mom,
        out_avg,
        out_copy,
        gu_new,
        gu_mom,
        gu_avg,
        gu_copy,
        down_new,
        down_mom,
        down_avg,
        down_copy,
        gain_new,
        gain_mom,
        gain_avg,
        gain_copy,
    )


def solution(mesh):
    placed = (
        P(None, ("grp", "seq"), None),
        P(None, ("grp", "seq"), None),
        P(None, "grp"),
        P(("grp", "seq"), None),
        P(("grp", "seq"), None),
        P(("grp", "seq"), None),
        P(("grp", "seq"), None),
        P(None, ("grp", "seq")),
        P(("grp", "seq"), None),
        P(("grp", "seq"), None),
        P(("grp", "seq"), None),
        P(("grp", "seq"), None),
        P(None, ("grp", "seq")),
        P(("grp", "seq"), None),
        P(("grp", "seq"), None),
        P(("grp", "seq"), None),
        P(("grp", "seq"), None),
        P(None, ("grp", "seq")),
    )
    heads_fit = mesh.shape["seq"] == HEADS
    return jax.shard_map(
        by_heads if heads_fit else by_rows,
        mesh=mesh,
        in_specs=placed,
        out_specs=(
            P(None, ("grp", "seq"), None),
            P(None, ("grp", "seq"), None),
            P(("grp", "seq"), None),
            P(("grp", "seq"), None),
            P(("grp", "seq"), None),
            P(("grp", "seq"), None),
            P(("grp", "seq"), None),
            P(("grp", "seq"), None),
            P(("grp", "seq"), None),
            P(("grp", "seq"), None),
            P(("grp", "seq"), None),
            P(("grp", "seq"), None),
            P(("grp", "seq"), None),
            P(("grp", "seq"), None),
            P(("grp", "seq"), None),
            P(("grp", "seq"), None),
            P(("grp", "seq"), None),
            P(("grp", "seq"), None),
            P(None, ("grp", "seq")),
            P(None, ("grp", "seq")),
            P(None, ("grp", "seq")),
            P(None, ("grp", "seq")),
        ),
        check_vma=False,
    )
```

```python
import functools

import jax
import jax.numpy as jnp
from jax import lax
from jax.experimental import pallas as pl
from jax.experimental.layout import Layout, with_layout_constraint
from jax.experimental.pallas import tpu as pltpu
from jax.sharding import PartitionSpec as P

HEADS = 8
KV_HEADS = 4
HEAD = 256
PROMPT = 1024
CONTS = 8


eps_norm = 1e-06
soft_cap = 50.0
momentum_decay = 0.5
average_decay = 0.5
weight_rate = 0.03
gain_rate = 0.2
rope_base = 10000.0
GELU_SCALE = (2.0 / 3.141592653589793) ** 0.5


def scaled(field, gain):
    return field * lax.rsqrt(jnp.mean(field * field, axis=-1, keepdims=True) + eps_norm) * gain


def place_tokens(seg_group, own_segment, row_index):
    levels = jnp.arange(CONTS + 1, dtype=jnp.int32)
    before = jnp.sum((seg_group[None, :] < levels[:, None]).astype(jnp.int32), axis=1)
    seg_start = jnp.sum(
        jnp.where(own_segment[:, None] == levels[None, :], before[None, :], 0), axis=1
    )
    return row_index - seg_start + jnp.where(own_segment > 0, PROMPT, 0)


def rotate(field, positions):
    half = field.shape[-1] // 2
    freqs = rope_base ** (-jnp.arange(half, dtype=jnp.float32) * 2.0 / field.shape[-1])
    angles = positions.astype(jnp.float32)[:, None] * freqs[None, :]
    cosine = jnp.cos(angles)[:, None, :]
    sine = jnp.sin(angles)[:, None, :]
    first_half = field[..., :half]
    second_half = field[..., half:]
    return jnp.concatenate(
        [first_half * cosine - second_half * sine, second_half * cosine + first_half * sine],
        axis=-1,
    )


def glu_part(gate, upper):
    return jax.nn.gelu(gate, approximate=True) * upper


def contract_rows(left, right):
    return lax.dot_general(
        left, right, (((0,), (0,)), ((), ())), preferred_element_type=jnp.float32
    )


def contract_cols(left, right):
    return lax.dot_general(
        left, right, (((1,), (1,)), ((), ())), preferred_element_type=jnp.float32
    )


def renew(weight, moment, average, gradient, step_rate):
    moment_new = momentum_decay * moment + gradient
    weight_new = weight - step_rate * (gradient + momentum_decay * moment_new)
    average_new = average_decay * average + (1.0 - average_decay) * weight_new
    return (weight_new, moment_new, average_new, weight_new.astype(jnp.bfloat16))


def by_rows(
    tokens,
    cotangent,
    segments,
    attn_in,
    attn_out,
    ffn_in,
    ffn_out,
    gains,
    attn_in_mom,
    attn_out_mom,
    ffn_in_mom,
    ffn_out_mom,
    gains_mom,
    attn_in_avg,
    attn_out_avg,
    ffn_in_avg,
    ffn_out_avg,
    gains_avg,
):
    micro_count = tokens.shape[0]
    local_rows = tokens.shape[1]
    all_rows = micro_count * local_rows
    model_width = tokens.shape[2]
    row_offset = lax.axis_index("seq") * local_rows
    row_index = row_offset + jnp.arange(local_rows, dtype=jnp.int32)
    key_index = jnp.arange(segments.shape[1], dtype=jnp.int32)
    query_width = HEADS * HEAD
    kv_width = KV_HEADS * HEAD
    share = HEADS // KV_HEADS
    ffn_width = ffn_out.shape[1]
    own_rows = ffn_in.shape[0]
    score_scale = HEAD ** (-0.5)
    own_segments = lax.dynamic_slice_in_dim(segments, row_offset, local_rows, 1)
    positions = jax.vmap(
        lambda seg_group, own_segment: place_tokens(seg_group, own_segment, row_index)
    )(segments, own_segments).reshape(all_rows)
    visible = (key_index[None, None, :] <= row_index[None, :, None]) & (
        (segments[:, None, :] == 0) | (segments[:, None, :] == own_segments[:, :, None])
    )
    inputs = tokens.astype(jnp.float32).reshape(all_rows, model_width)
    w_qkv, w_o, gain_low = (
        lax.all_gather(attn_in.astype(jnp.bfloat16), ("grp", "seq"), axis=0, tiled=True),
        lax.all_gather(attn_out.astype(jnp.bfloat16), ("grp", "seq"), axis=0, tiled=True),
        lax.all_gather(gains.astype(jnp.bfloat16), ("grp", "seq"), axis=1, tiled=True),
    )
    gain_vals = gain_low.astype(jnp.float32)
    normed_one, norm_one_back = jax.vjp(scaled, inputs, gain_vals[0])
    normed_one = normed_one.astype(jnp.bfloat16)
    projected = jnp.dot(normed_one, w_qkv, preferred_element_type=jnp.float32)
    query_rot, query_back = jax.vjp(
        lambda field: rotate(field, positions),
        projected[:, :query_width].reshape(all_rows, HEADS, HEAD),
    )
    key_rot, key_back = jax.vjp(
        lambda field: rotate(field, positions),
        projected[:, query_width : query_width + kv_width].reshape(all_rows, KV_HEADS, HEAD),
    )
    query_low = query_rot.astype(jnp.bfloat16).reshape(
        micro_count, local_rows, KV_HEADS, share, HEAD
    )
    key_low = key_rot.astype(jnp.bfloat16).reshape(micro_count, local_rows, kv_width)
    value_low = (
        projected[:, query_width + kv_width :]
        .astype(jnp.bfloat16)
        .reshape(micro_count, local_rows, kv_width)
    )
    group_key_rows, group_values = (
        lax.all_gather(key_low, "seq", axis=1, tiled=True),
        lax.all_gather(value_low, "seq", axis=1, tiled=True),
    )
    group_key_rows = group_key_rows.reshape(micro_count, -1, KV_HEADS, HEAD)
    group_values = group_values.reshape(micro_count, -1, KV_HEADS, HEAD)

    def probabilities(raw_scores):
        capped = jnp.where(
            visible[:, None, None], soft_cap * jnp.tanh(raw_scores / soft_cap), -1e30
        )
        return jax.nn.softmax(capped, axis=-1)

    raw_scores = (
        jnp.einsum(
            "mtgrd,mkgd->mgrtk", query_low, group_key_rows, preferred_element_type=jnp.float32
        )
        * score_scale
    )
    attention, attention_back = jax.vjp(probabilities, raw_scores)
    attention_low = attention.astype(jnp.bfloat16)
    mixed_heads = jnp.einsum(
        "mgrtk,mkgd->mtgrd", attention_low, group_values, preferred_element_type=jnp.float32
    )
    mixed_low = mixed_heads.reshape(all_rows, query_width).astype(jnp.bfloat16)
    branch = contract_cols(mixed_low, w_o)
    normed_two, norm_two_back = jax.vjp(scaled, branch, gain_vals[1])
    middle = inputs + normed_two
    normed_three, norm_three_back = jax.vjp(scaled, middle, gain_vals[2])
    normed_three = normed_three.astype(jnp.bfloat16)
    grad_top = cotangent.astype(jnp.float32).reshape(all_rows, model_width)
    seq_count = lax.axis_size("seq")
    grp_count = lax.axis_size("grp")
    slice_width = ffn_width // seq_count
    stacked = jnp.concatenate(
        [
            ffn_in.astype(jnp.bfloat16).reshape(own_rows, 2, seq_count, slice_width),
            ffn_out.astype(jnp.bfloat16).reshape(own_rows, 1, seq_count, slice_width),
        ],
        axis=1,
    )
    spread = jnp.broadcast_to(
        stacked[:, :, None], (own_rows, 3, grp_count, seq_count, slice_width)
    ).reshape(own_rows, 3, grp_count * seq_count, slice_width)
    w_cols = lax.all_to_all(
        spread, ("grp", "seq"), split_axis=2, concat_axis=0, tiled=True
    ).reshape(model_width, 3, slice_width)
    w_gu_cols = w_cols[:, :2].reshape(model_width, 2 * slice_width)
    w_d_cols = w_cols[:, 2]
    norm_rows = lax.all_gather(normed_three, "seq", axis=0, tiled=True)
    gate_up = jnp.dot(norm_rows, w_gu_cols, preferred_element_type=jnp.float32)
    hidden, glu_back = jax.vjp(glu_part, gate_up[:, :slice_width], gate_up[:, slice_width:])
    hidden = hidden.astype(jnp.bfloat16)
    ffn_branch = lax.psum_scatter(
        contract_cols(hidden, w_d_cols), "seq", scatter_dimension=0, tiled=True
    )
    normed_four, norm_four_back = jax.vjp(scaled, ffn_branch, gain_vals[3])
    layer_out = (
        (middle + normed_four).astype(jnp.bfloat16).reshape(micro_count, local_rows, model_width)
    )
    d_ffn, d_gain_four = norm_four_back(grad_top)
    d_ffn_all = lax.all_gather(d_ffn.astype(jnp.bfloat16), "seq", axis=0, tiled=True)
    d_hidden = jnp.dot(d_ffn_all, w_d_cols, preferred_element_type=jnp.float32)
    grad_d_cols = contract_rows(d_ffn_all, hidden)
    d_gate, d_upper = glu_back(d_hidden)
    d_gate_up = jnp.concatenate([d_gate, d_upper], axis=1).astype(jnp.bfloat16)
    grad_gu_cols = contract_rows(norm_rows, d_gate_up)
    d_normed_three = lax.psum_scatter(
        contract_cols(d_gate_up, w_gu_cols), "seq", scatter_dimension=0, tiled=True
    )
    local_grads = jnp.concatenate(
        [grad_gu_cols.reshape(model_width, 2, slice_width), grad_d_cols[:, None, :]], axis=1
    ).reshape(model_width, 3, 1, slice_width)
    returned = lax.all_to_all(
        local_grads.astype(jnp.bfloat16), ("grp", "seq"), split_axis=0, concat_axis=2, tiled=True
    ).astype(local_grads.dtype)
    grad_ffn = jnp.sum(
        returned.reshape(own_rows, 3, grp_count, seq_count, slice_width), axis=2
    ).reshape(own_rows, 3 * ffn_width)
    d_middle_norm, d_gain_three = norm_three_back(d_normed_three)
    d_middle = grad_top + d_middle_norm
    sum_gu = grad_ffn[:, : 2 * ffn_width]
    sum_down = grad_ffn[:, 2 * ffn_width :]
    d_branch, d_gain_two = norm_two_back(d_middle)
    d_branch_low = d_branch.astype(jnp.bfloat16)
    grad_out = contract_rows(d_branch_low, mixed_low)
    d_mixed = jnp.dot(d_branch_low, w_o, preferred_element_type=jnp.float32)
    d_mixed_low = d_mixed.astype(jnp.bfloat16).reshape(
        micro_count, local_rows, KV_HEADS, share, HEAD
    )
    d_attention = jnp.einsum(
        "mtgrd,mkgd->mgrtk", d_mixed_low, group_values, preferred_element_type=jnp.float32
    )
    (d_raw,) = attention_back(d_attention)
    d_raw_low = d_raw.astype(jnp.bfloat16)
    d_query = (
        jnp.einsum(
            "mgrtk,mkgd->mtgrd", d_raw_low, group_key_rows, preferred_element_type=jnp.float32
        )
        * score_scale
    )
    d_group_keys = (
        jnp.einsum("mgrtk,mtgrd->mkgd", d_raw_low, query_low, preferred_element_type=jnp.float32)
        * score_scale
    )
    d_group_values = jnp.einsum(
        "mgrtk,mtgrd->mkgd", attention_low, d_mixed_low, preferred_element_type=jnp.float32
    )
    d_keys, d_values = (
        lax.psum_scatter(
            d_group_keys.reshape(micro_count, -1, kv_width).astype(jnp.bfloat16),
            "seq",
            scatter_dimension=1,
            tiled=True,
        ).astype(jnp.float32),
        lax.psum_scatter(
            d_group_values.reshape(micro_count, -1, kv_width).astype(jnp.bfloat16),
            "seq",
            scatter_dimension=1,
            tiled=True,
        ).astype(jnp.float32),
    )
    (d_query_raw,) = query_back(d_query.reshape(all_rows, HEADS, HEAD))
    (d_key_raw,) = key_back(d_keys.reshape(all_rows, KV_HEADS, HEAD))
    d_projected = jnp.concatenate(
        [
            d_query_raw.reshape(all_rows, query_width),
            d_key_raw.reshape(all_rows, kv_width),
            d_values.reshape(all_rows, kv_width),
        ],
        axis=1,
    ).astype(jnp.bfloat16)
    grad_qkv = contract_rows(normed_one, d_projected)
    d_normed_one = contract_cols(d_projected, w_qkv)
    d_input_norm, d_gain_one = norm_one_back(d_normed_one)
    layer_grad = (d_middle + d_input_norm).reshape(micro_count, local_rows, model_width)
    d_gains = jnp.stack([d_gain_one, d_gain_two, d_gain_three, d_gain_four])
    part_qkv, part_out, part_gain = (
        lax.psum_scatter(
            grad_qkv.astype(jnp.bfloat16), "grp", scatter_dimension=0, tiled=True
        ).astype(jnp.float32),
        lax.psum_scatter(
            grad_out.astype(jnp.bfloat16), "grp", scatter_dimension=0, tiled=True
        ).astype(jnp.float32),
        lax.psum_scatter(
            d_gains.astype(jnp.bfloat16), "grp", scatter_dimension=1, tiled=True
        ).astype(jnp.float32),
    )
    sum_qkv, sum_out, sum_gain = (
        lax.psum_scatter(
            part_qkv.astype(jnp.bfloat16), "seq", scatter_dimension=0, tiled=True
        ).astype(jnp.float32),
        lax.psum_scatter(
            part_out.astype(jnp.bfloat16), "seq", scatter_dimension=0, tiled=True
        ).astype(jnp.float32),
        lax.psum_scatter(
            part_gain.astype(jnp.bfloat16), "seq", scatter_dimension=1, tiled=True
        ).astype(jnp.float32),
    )
    token_total = micro_count * local_rows * lax.axis_size(("grp", "seq"))
    rate_mat = weight_rate * token_total ** (-0.5)
    rate_gain = gain_rate * token_total ** (-0.5)
    qkv_new, qkv_mom, qkv_avg, qkv_copy = renew(
        attn_in, attn_in_mom, attn_in_avg, sum_qkv, rate_mat
    )
    out_new, out_mom, out_avg, out_copy = renew(
        attn_out, attn_out_mom, attn_out_avg, sum_out, rate_mat
    )
    gu_new, gu_mom, gu_avg, gu_copy = renew(ffn_in, ffn_in_mom, ffn_in_avg, sum_gu, rate_mat)
    down_new, down_mom, down_avg, down_copy = renew(
        ffn_out, ffn_out_mom, ffn_out_avg, sum_down, rate_mat
    )
    gain_new, gain_mom, gain_avg, gain_copy = renew(
        gains, gains_mom, gains_avg, sum_gain, rate_gain
    )
    return (
        layer_out,
        layer_grad,
        qkv_new,
        qkv_mom,
        qkv_avg,
        qkv_copy,
        out_new,
        out_mom,
        out_avg,
        out_copy,
        gu_new,
        gu_mom,
        gu_avg,
        gu_copy,
        down_new,
        down_mom,
        down_avg,
        down_copy,
        gain_new,
        gain_mom,
        gain_avg,
        gain_copy,
    )


VMEM_LIMIT = 48 * 1024 * 1024


def permute(field, offset):
    count = lax.axis_size("seq")
    return lax.ppermute(field, "seq", [(i, i ^ offset) for i in range(count)])


def gather_near(field):
    return field, permute(field, 2), permute(field, 4)


def gather_mine(field, by_x, by_y):
    half = field.shape[0] // 2
    far = [permute(by_x[:half], 4), permute(by_y[half:], 2)]
    return jnp.concatenate([field, by_x, by_y] + far, axis=0)


def gather_far(field, by_x, by_y):
    mine = gather_mine(field, by_x, by_y)
    return [mine, permute(mine, 1)]


def gather_pieces(field):
    return gather_far(*gather_near(field))


def add_low(left, right):
    return (left.astype(jnp.float32) + right.astype(jnp.float32)).astype(jnp.bfloat16)


def sum_far(own, by_x, by_y, far):
    half = own.shape[0] // 2
    far_x = permute(far[:half], 2)
    far_y = permute(far[half:], 4)
    by_y = jnp.concatenate([add_low(by_y[:half], far_x), by_y[half:]], axis=0)
    by_x = jnp.concatenate([by_x[:half], add_low(by_x[half:], far_y)], axis=0)
    return own, by_x, by_y


def sum_near(own, by_x, by_y):
    return own.astype(jnp.float32) + by_x.astype(jnp.float32) + by_y.astype(jnp.float32)


def sum_pairs(*blocks):
    own, by_x, by_y = sum_far(*blocks)
    return sum_near(own, permute(by_x, 2), permute(by_y, 4))


def pair_products(mine, other, weight):
    rows = mine.shape[0] // 4
    start = 3 * rows
    far_other = low(contract_cols(other[start:], weight))
    later, far_other = lax.optimization_barrier((weight, far_other))
    far_moved = permute(far_other, 1)
    near_moved = permute(low(contract_cols(other[:start], later)), 1)
    far = add_low(low(contract_cols(mine[start:], weight)), far_moved)
    near = add_low(low(contract_cols(mine[:start], later)), near_moved)
    return near[:rows], near[rows : 2 * rows], near[2 * rows :], far


def pair_halves(mine, other, weight):
    moved = permute(low(contract_cols(other, weight)), 1)
    total = add_low(low(contract_cols(mine, weight)), moved)
    rows = total.shape[0] // 4
    return [total[at * rows : (at + 1) * rows] for at in range(4)]


def sum_products(mine, other, weight):
    return sum_pairs(*pair_products(mine, other, weight))


def piece_order(blocks):
    index = lax.axis_index("seq")
    count = blocks.shape[0]
    bits = count.bit_length() - 1
    split = blocks.reshape((2,) * bits + blocks.shape[1:])
    for bit in range(bits):
        axis = bits - 1 - bit
        split = jnp.where((index >> bit) & 1 == 1, jnp.flip(split, axis), split)
    return jnp.swapaxes(split.reshape((count // 2, 2) + blocks.shape[1:]), 0, 1).reshape(blocks.shape)


def qkv_columns(device):
    return [device, HEADS + (device % 2) * KV_HEADS + device // 2]


def out_columns(device):
    return [device]


def spread_kernel(count, blocks, field_ref, out_ref):
    parts = len(blocks(0))
    width = out_ref.shape[2] // parts
    for device in range(count):
        for part, block in enumerate(blocks(device)):
            out_ref[device, :, part * width : (part + 1) * width] = field_ref[
                :, block * width : (block + 1) * width
            ].astype(jnp.bfloat16)


def spread(field, count, blocks):
    rows, columns = field.shape
    return pl.pallas_call(
        functools.partial(spread_kernel, count, blocks),
        out_shape=jax.ShapeDtypeStruct((count, rows, columns // count), jnp.bfloat16),
        cost_estimate=pl.CostEstimate(flops=0, transcendentals=0, bytes_accessed=6 * field.size),
        compiler_params=pltpu.CompilerParams(vmem_limit_bytes=VMEM_LIMIT),
        name="spread",
    )(field)


def row_product(weight, gradient):
    used = weight.astype(jnp.bfloat16).astype(jnp.float32)
    return jnp.sum(used * gradient, axis=1, keepdims=True)


def renew_kernel(rate, w_ref, m_ref, a_ref, g_ref, w_out, m_out, a_out, c_out, product_out):
    gradient = g_ref[0].astype(jnp.float32)
    w_new, m_new, a_new, copy = renew(w_ref[...], m_ref[...], a_ref[...], gradient, rate)
    product_out[...] += row_product(w_ref[...], gradient)
    w_out[...] = w_new
    m_out[...] = m_new
    a_out[...] = a_new
    c_out[...] = copy


def renew_parts_kernel(rate, w_ref, m_ref, a_ref, *refs):
    g_refs, outs = refs[:-5], refs[-5:]

    @pl.when((pl.program_id(0) == 0) & (pl.program_id(1) == 0))
    def _():
        outs[-1][...] = jnp.zeros_like(outs[-1])

    for part, g_ref in enumerate(g_refs):

        @pl.when(pl.program_id(1) == part)
        def _(g_ref=g_ref):
            renew_kernel(rate, w_ref, m_ref, a_ref, g_ref, *outs)


def renew_wide(weight, moment, average, gradients, rate):
    rows, columns = weight.shape
    parts = len(gradients)
    count = gradients[0][0].shape[0]
    width = columns // (count * parts)
    own = pl.BlockSpec((rows, width), lambda d, p: (0, p * count + d))

    def of_block(block):
        return pl.BlockSpec((1, rows, width), lambda d, p: (d, 0, block))

    return pl.pallas_call(
        functools.partial(renew_parts_kernel, rate),
        grid=(count, parts),
        in_specs=[own, own, own] + [of_block(block) for _, block in gradients],
        out_specs=[own, own, own, own, pl.BlockSpec((rows, 1), lambda d, p: (0, 0))],
        out_shape=[jax.ShapeDtypeStruct((rows, columns), jnp.float32)] * 3
        + [
            jax.ShapeDtypeStruct((rows, columns), jnp.bfloat16),
            jax.ShapeDtypeStruct((rows, 1), jnp.float32),
        ],
        cost_estimate=pl.CostEstimate(
            flops=8 * weight.size, transcendentals=0, bytes_accessed=28 * weight.size
        ),
        compiler_params=pltpu.CompilerParams(vmem_limit_bytes=VMEM_LIMIT),
        name="renew",
    )(weight, moment, average, *(array for array, _ in gradients))


def renew_heads_kernel(rate, g_ref, *refs):
    product = jnp.zeros(refs[-1].shape, jnp.float32)
    for device in range(g_ref.shape[0]):
        blocks = [(0, block) for block in qkv_columns(device)] + [(1, device)]
        for part, (which, block) in enumerate(blocks):
            w_ref, m_ref, a_ref = refs[3 * which : 3 * which + 3]
            outs = refs[6 + 4 * which : 10 + 4 * which]
            here = (slice(None), slice(block * HEAD, (block + 1) * HEAD))
            gradient = g_ref[device, : w_ref.shape[0], part * HEAD : (part + 1) * HEAD].astype(
                jnp.float32
            )
            results = renew(w_ref[here], m_ref[here], a_ref[here], gradient, rate)
            for out, result in zip(outs, results):
                out[here] = result
            if which == 0:
                product += row_product(w_ref[here], gradient)
    refs[-1][...] = product


def renew_heads(gradient, attn_in, attn_out, rate):
    kinds = (jnp.float32, jnp.float32, jnp.float32, jnp.bfloat16)
    shapes = [
        jax.ShapeDtypeStruct(state[0].shape, kind) for state in (attn_in, attn_out) for kind in kinds
    ]
    size = attn_in[0].size + attn_out[0].size
    results = pl.pallas_call(
        functools.partial(renew_heads_kernel, rate),
        out_shape=shapes + [jax.ShapeDtypeStruct((attn_in[0].shape[0], 1), jnp.float32)],
        cost_estimate=pl.CostEstimate(flops=8 * size, transcendentals=0, bytes_accessed=28 * size),
        compiler_params=pltpu.CompilerParams(vmem_limit_bytes=VMEM_LIMIT),
        name="renew_heads",
    )(gradient, *attn_in, *attn_out)
    return results[:4], results[4:8], results[8]


def glu_kernel(rows_ref, w_ref, gate_up_ref, hidden_ref):
    width = hidden_ref.shape[1]
    gate_up = jnp.dot(rows_ref[...], w_ref[...], preferred_element_type=jnp.float32)
    gate_up_ref[...] = gate_up
    gate, upper = gate_up[:, :width], gate_up[:, width:]
    bent = jnp.tanh(GELU_SCALE * gate * (1.0 + 0.044715 * gate * gate))
    hidden_ref[...] = (0.5 * gate * (1.0 + bent) * upper).astype(jnp.bfloat16)


def glu_rows(field, weight):
    rows, depth = field.shape
    width = weight.shape[1] // 2
    tile = rows // 6
    return pl.pallas_call(
        glu_kernel,
        grid=(rows // tile,),
        in_specs=[
            pl.BlockSpec((tile, depth), lambda i: (i, 0)),
            pl.BlockSpec(weight.shape, lambda i: (0, 0)),
        ],
        out_specs=[
            pl.BlockSpec((tile, 2 * width), lambda i: (i, 0)),
            pl.BlockSpec((tile, width), lambda i: (i, 0)),
        ],
        out_shape=[
            jax.ShapeDtypeStruct((rows, 2 * width), jnp.float32),
            jax.ShapeDtypeStruct((rows, width), jnp.bfloat16),
        ],
        cost_estimate=pl.CostEstimate(
            flops=4 * rows * depth * width,
            transcendentals=rows * width,
            bytes_accessed=rows * (2 * depth + 10 * width) + 4 * depth * width,
        ),
        compiler_params=pltpu.CompilerParams(vmem_limit_bytes=VMEM_LIMIT),
        name="glu",
    )(field, weight)


def glu_back_kernel(left0_ref, left1_ref, w0_ref, w1_ref, gate_up_ref, out_ref):
    width = w0_ref.shape[1]
    d_hidden = jnp.dot(left0_ref[...], w0_ref[...], preferred_element_type=jnp.float32)
    d_hidden += jnp.dot(left1_ref[...], w1_ref[...], preferred_element_type=jnp.float32)
    gate = gate_up_ref[:, :width]
    upper = gate_up_ref[:, width:]
    square = gate * gate
    bent = jnp.tanh(GELU_SCALE * gate * (1.0 + 0.044715 * square))
    rise = 0.5 * (1.0 + bent)
    slope = rise + 0.5 * gate * (1.0 - bent * bent) * GELU_SCALE * (1.0 + 3 * 0.044715 * square)
    out_ref[:, :width] = (d_hidden * upper * slope).astype(jnp.bfloat16)
    out_ref[:, width:] = (d_hidden * gate * rise).astype(jnp.bfloat16)


def glu_back_rows(left0, left1, w0, w1, gate_up):
    rows = left0.shape[0]
    width = w0.shape[1]
    tile = rows // 6
    return pl.pallas_call(
        glu_back_kernel,
        grid=(rows // tile,),
        in_specs=[
            pl.BlockSpec((tile, left0.shape[1]), lambda i: (i, 0)),
            pl.BlockSpec((tile, left1.shape[1]), lambda i: (i, 0)),
            pl.BlockSpec(w0.shape, lambda i: (0, 0)),
            pl.BlockSpec(w1.shape, lambda i: (0, 0)),
            pl.BlockSpec((tile, 2 * width), lambda i: (i, 0)),
        ],
        out_specs=pl.BlockSpec((tile, 2 * width), lambda i: (i, 0)),
        out_shape=jax.ShapeDtypeStruct((rows, 2 * width), jnp.bfloat16),
        cost_estimate=pl.CostEstimate(
            flops=2 * rows * (w0.shape[0] + w1.shape[0]) * width,
            transcendentals=rows * width,
            bytes_accessed=rows * (2 * (left0.shape[1] + left1.shape[1]) + 12 * width),
        ),
        compiler_params=pltpu.CompilerParams(vmem_limit_bytes=VMEM_LIMIT),
        name="glu_back",
    )(left0, left1, w0, w1, gate_up)


def norm_tiles(rows, width, kinds):
    tile = rows // 3
    return [
        pl.BlockSpec((tile, width), lambda i: (i, 0))
        if kind
        else pl.BlockSpec((1, width), lambda i: (0, 0))
        for kind in kinds
    ]


def norm_call(kernel, name, rows, width, fields, gains, outs):
    specs = norm_tiles(rows, width, [1] * len(fields) + [0] * len(gains))
    return pl.pallas_call(
        kernel,
        grid=(3,),
        in_specs=specs,
        out_specs=norm_tiles(rows, width, [out is not None for out in outs]),
        out_shape=[
            jax.ShapeDtypeStruct((rows, width), out)
            if out is not None
            else jax.ShapeDtypeStruct((1, width), jnp.float32)
            for out in outs
        ],
        cost_estimate=pl.CostEstimate(
            flops=20 * rows * width, transcendentals=0, bytes_accessed=20 * rows * width
        ),
        compiler_params=pltpu.CompilerParams(vmem_limit_bytes=VMEM_LIMIT // 2),
        name=name,
    )(*fields, *gains)


def row_inverse(field):
    return lax.rsqrt(jnp.mean(field * field, axis=1, keepdims=True) + eps_norm)


def row_back(field, inverse, top):
    inner = jnp.mean(field * top, axis=1, keepdims=True)
    return inverse * top - field * (inverse * inverse * inverse * inner)


def read_sum(own_ref, by_x_ref, by_y_ref):
    return (
        own_ref[...].astype(jnp.float32)
        + by_x_ref[...].astype(jnp.float32)
        + by_y_ref[...].astype(jnp.float32)
    )


def middle_kernel(own_ref, by_x_ref, by_y_ref, token_ref, g1_ref, g2_ref, branch_ref, middle_ref, out_ref):
    branch = read_sum(own_ref, by_x_ref, by_y_ref)
    branch_ref[...] = branch
    middle = token_ref[...].astype(jnp.float32) + branch * row_inverse(branch) * g1_ref[...]
    middle_ref[...] = middle
    out_ref[...] = (middle * row_inverse(middle) * g2_ref[...]).astype(jnp.bfloat16)


def middle_back_kernel(
    own_ref,
    by_x_ref,
    by_y_ref,
    top_ref,
    branch_ref,
    middle_ref,
    g1_ref,
    g2_ref,
    d_middle_ref,
    d_branch_ref,
    d_gain_ref,
):
    middle, branch = middle_ref[...], branch_ref[...]
    d_normed = read_sum(own_ref, by_x_ref, by_y_ref)
    d_middle = top_ref[...].astype(jnp.float32) + row_back(
        middle, row_inverse(middle), g2_ref[...] * d_normed
    )
    d_middle_ref[...] = d_middle
    inverse = row_inverse(branch)
    d_branch_ref[...] = row_back(branch, inverse, g1_ref[...] * d_middle).astype(jnp.bfloat16)

    @pl.when(pl.program_id(0) == 0)
    def _():
        d_gain_ref[...] = jnp.zeros_like(d_gain_ref)

    d_gain_ref[...] += jnp.sum(d_middle * (branch * inverse), axis=0, keepdims=True)


def input_back_kernel(own_ref, by_x_ref, by_y_ref, token_ref, d_middle_ref, g0_ref, out_ref):
    token = token_ref[...].astype(jnp.float32)
    d_normed = read_sum(own_ref, by_x_ref, by_y_ref)
    out_ref[...] = d_middle_ref[...] + row_back(token, row_inverse(token), g0_ref[...] * d_normed)


def across(left, right):
    return lax.dot_general(
        left, right, (((1,), (1,)), ((), ())), preferred_element_type=jnp.float32
    )


def down(left, right):
    return lax.dot_general(
        left, right, (((0,), (0,)), ((), ())), preferred_element_type=jnp.float32
    )


def attend_kernel(q_ref, k_ref, v_ref, key_ref, query_ref, out_ref, weights_ref, slopes_ref):
    bent = jnp.tanh(across(k_ref[0], q_ref[0]) * (HEAD ** (-0.5) / soft_cap))
    key, query = key_ref[0][:, :1], query_ref[0]
    seg_k, seg_q = key & 15, query & 15
    seen = ((key >> 4) <= (query >> 4)) & ((seg_k == 0) | (seg_k == seg_q))
    capped = jnp.where(seen, soft_cap * bent, -1e30)
    top = jnp.max(capped, axis=0, keepdims=True)
    powers = jnp.exp(capped - top)
    weights = powers * (1.0 / jnp.sum(powers, axis=0, keepdims=True))
    weights_low = weights.astype(jnp.bfloat16)
    weights_ref[0] = weights_low
    slopes_ref[0] = (weights * (1.0 - bent * bent)).astype(jnp.bfloat16)
    out_ref[0] = down(weights_low, v_ref[0]).astype(jnp.bfloat16)


def attend_back_kernel(
    q_ref,
    k_ref,
    v_ref,
    weights_ref,
    slopes_ref,
    cosine_ref,
    sine_ref,
    core_ref,
    d_out_ref,
    dq_ref,
    keep_ref,
    send_ref,
    dk_sum,
    dv_sum,
):
    q, k, v, d_out = q_ref[0], k_ref[0], v_ref[0], d_out_ref[0]
    weights = weights_ref[0]
    d_weights = across(v, d_out)
    inner = jnp.sum(weights.astype(jnp.float32) * d_weights, axis=0, keepdims=True)
    d_raw = (slopes_ref[0].astype(jnp.float32) * (d_weights - inner)).astype(jnp.bfloat16)
    scale = HEAD ** (-0.5)

    @pl.when(pl.program_id(1) == 0)
    def _():
        dk_sum[...] = jnp.zeros_like(dk_sum)
        dv_sum[...] = jnp.zeros_like(dv_sum)

    dq = down(d_raw, k) * scale
    half = HEAD // 2
    cosine, sine = cosine_ref[0], sine_ref[0]
    first, second = dq[:, :half], dq[:, half:]
    dq_ref[0, :, :half] = (first * cosine + second * sine).astype(jnp.bfloat16)
    dq_ref[0, :, half:] = (second * cosine - first * sine).astype(jnp.bfloat16)
    dk_sum[...] += jnp.dot(d_raw, q, preferred_element_type=jnp.float32)
    dv_sum[...] += jnp.dot(weights, d_out, preferred_element_type=jnp.float32)

    @pl.when(pl.program_id(1) == pl.num_programs(1) - 1)
    def _():
        holds_keys = core_ref[:, :1] == 0
        dk, dv = dk_sum[...] * scale, dv_sum[...]
        keep_ref[0] = jnp.where(holds_keys, dk, dv)
        send_ref[0] = jnp.where(holds_keys, dv, dk).astype(jnp.bfloat16)


def attention_cost(micros, rows, products):
    return pl.CostEstimate(
        flops=2 * products * micros * rows * rows * HEAD,
        transcendentals=2 * micros * rows * rows,
        bytes_accessed=4 * products * micros * rows * HEAD,
    )


def attention_specs(rows, tile):
    moving = pl.BlockSpec((1, tile, HEAD), lambda m, i: (m, i, 0))
    whole = pl.BlockSpec((1, rows, HEAD), lambda m, i: (m, 0, 0))
    scores = pl.BlockSpec((1, rows, tile), lambda m, i: (m, 0, i))
    return moving, whole, scores


def attend(q, k, v, places):
    micros, rows, _ = q.shape
    tile = rows // 3
    moving, whole, scores = attention_specs(rows, tile)
    return pl.pallas_call(
        attend_kernel,
        grid=(micros, rows // tile),
        in_specs=[
            moving,
            whole,
            whole,
            pl.BlockSpec((1, rows, 128), lambda m, i: (m, 0, 0)),
            pl.BlockSpec((1, 1, tile), lambda m, i: (m, 0, i)),
        ],
        out_specs=[moving, scores, scores],
        out_shape=[jax.ShapeDtypeStruct(q.shape, jnp.bfloat16)]
        + [jax.ShapeDtypeStruct((micros, rows, rows), jnp.bfloat16)] * 2,
        cost_estimate=attention_cost(micros, rows, 2),
        compiler_params=pltpu.CompilerParams(vmem_limit_bytes=VMEM_LIMIT),
        name="attend",
    )(q, k, v, *places)


def attend_back(q, k, v, weights, slopes, tables, core, d_out):
    micros, rows, _ = q.shape
    tile = rows // 3
    moving, whole, scores = attention_specs(rows, tile)
    turning = pl.BlockSpec((1, tile, HEAD // 2), lambda m, i: (m, i, 0))
    return pl.pallas_call(
        attend_back_kernel,
        grid=(micros, rows // tile),
        in_specs=[moving, whole, whole, scores, scores, turning, turning]
        + [pl.BlockSpec((1, 128), lambda m, i: (0, 0)), moving],
        out_specs=[moving, whole, whole],
        out_shape=[
            jax.ShapeDtypeStruct(q.shape, jnp.bfloat16),
            jax.ShapeDtypeStruct(q.shape, jnp.float32),
            jax.ShapeDtypeStruct(q.shape, jnp.bfloat16),
        ],
        scratch_shapes=[pltpu.VMEM((rows, HEAD), jnp.float32)] * 2,
        cost_estimate=attention_cost(micros, rows, 4),
        compiler_params=pltpu.CompilerParams(vmem_limit_bytes=VMEM_LIMIT),
        name="attend_back",
    )(q, k, v, weights, slopes, *tables, core, d_out)


def exchange(field):
    return lax.all_to_all(field, "seq", split_axis=0, concat_axis=0, tiled=True)


def in_order(step, *operands):
    zeros = jax.eval_shape(step, *operands)
    return lax.cond(
        lax.optimization_barrier(jnp.bool_(True)),
        step,
        lambda *_: jax.tree.map(lambda leaf: jnp.zeros(leaf.shape, leaf.dtype), zeros),
        *operands,
    )


def gather_planes(field):
    return lax.all_gather(field, "grp", axis=0, tiled=True)


def sum_planes(field):
    return lax.psum_scatter(field, "grp", scatter_dimension=0, tiled=True)


def turn(field, cosine, sine):
    half = field.shape[-1] // 2
    first, second = field[..., :half], field[..., half:]
    return jnp.concatenate([first * cosine - second * sine, second * cosine + first * sine], axis=-1)


def low(field):
    return field.astype(jnp.bfloat16)


def dot(left, right):
    return jnp.dot(left, right, preferred_element_type=jnp.float32)


def over_rows(lefts, rights):
    return low(contract_rows(lefts[0], rights[0]) + contract_rows(lefts[1], rights[1]))


def by_heads(
    tokens,
    cotangent,
    segments,
    attn_in,
    attn_out,
    ffn_in,
    ffn_out,
    gains,
    attn_in_mom,
    attn_out_mom,
    ffn_in_mom,
    ffn_out_mom,
    gains_mom,
    attn_in_avg,
    attn_out_avg,
    ffn_in_avg,
    ffn_out_avg,
    gains_avg,
):
    tie = lax.optimization_barrier
    micro_count, local_rows, model_width = tokens.shape
    all_rows = micro_count * local_rows
    seq_count = lax.axis_size("seq")
    grp_count = lax.axis_size("grp")
    device_count = seq_count * grp_count
    group_rows = segments.shape[1]
    own_rows = ffn_in.shape[0]
    plane_rows = own_rows * seq_count
    cut = own_rows * 2 // 3
    slice_width = ffn_out.shape[1] // seq_count
    index = lax.axis_index("seq")
    key_core = index % 2 == 0
    token_total = micro_count * local_rows * device_count
    rate_mat = weight_rate * token_total ** (-0.5)
    rate_gain = gain_rate * token_total ** (-0.5)

    def ffn_columns(device):
        return [device, seq_count + device]

    def by_device(part):
        return exchange(part.reshape(seq_count, own_rows, -1))

    def to_parts(field):
        split = field.reshape(-1, device_count, own_rows)
        return [
            split[:, :, :cut].reshape(field.shape[0], -1),
            split[:, :, cut:].reshape(field.shape[0], -1),
        ]

    def from_parts(parts):
        split = [part.reshape(part.shape[0], device_count, -1) for part in parts]
        return jnp.concatenate(split, axis=2).reshape(-1, model_width)

    def to_groups(field):
        return (
            field.reshape(seq_count, micro_count, local_rows, -1)
            .transpose(1, 0, 2, 3)
            .reshape(micro_count, group_rows, -1)
        )

    def from_groups(field):
        return (
            field.reshape(micro_count, seq_count, local_rows, -1)
            .transpose(1, 0, 2, 3)
            .reshape(seq_count * all_rows, -1)
        )

    def in_two(field):
        return [field[: field.shape[0] // 2], field[field.shape[0] // 2 :]]

    def swap_cores(field):
        first, second = in_two(permute(field, 1))
        return jnp.concatenate([second, first], axis=0)

    heads_moved = exchange(
        jnp.concatenate(
            [spread(attn_in, seq_count, qkv_columns), spread(attn_out, seq_count, out_columns)], axis=2
        )
    ).reshape(plane_rows, 3 * HEAD)
    later_tokens, gains_low, heads_moved = tie((tokens, low(gains), heads_moved))
    w_heads = gather_planes(heads_moved)
    all_gains = lax.all_to_all(
        jnp.broadcast_to(gains_low[None], (device_count,) + gains.shape),
        ("grp", "seq"),
        split_axis=0,
        concat_axis=0,
        tiled=True,
    )
    gain_vals = all_gains.transpose(1, 0, 2).reshape(4, model_width).astype(jnp.float32)
    own_rows_low, by_x, by_y = gather_near(later_tokens.reshape(all_rows, model_width))
    true_rows = jnp.arange(group_rows, dtype=jnp.int32)
    positions = jax.vmap(lambda seg: place_tokens(seg, seg, true_rows))(segments)

    def to_pieces(field):
        return piece_order(field.reshape(micro_count, seq_count, local_rows).transpose(1, 0, 2))

    place = to_pieces(positions).reshape(-1).astype(jnp.float32)
    seg = to_pieces(segments).transpose(1, 0, 2).reshape(micro_count, group_rows)
    row = piece_order(true_rows.reshape(seq_count, local_rows)).reshape(-1)
    freqs = rope_base ** (-jnp.arange(HEAD // 2, dtype=jnp.float32) * 2.0 / HEAD)
    angles = place[:, None] * freqs[None, :]
    cosine, sine = jnp.cos(angles), jnp.sin(angles)
    cosine, sine, kv_cosine, kv_sine, *places = tie(
        (
            cosine,
            sine,
            jnp.where(key_core, cosine, 1.0),
            jnp.where(key_core, sine, 0.0),
            jnp.broadcast_to((16 * row + seg)[:, :, None], seg.shape + (128,)),
            (16 * row + seg)[:, None, :],
        )
    )

    by_x, by_y, later_ffn_in, gain_vals, cosine = tie((by_x, by_y, ffn_in, gain_vals, cosine))
    gu_moved = exchange(spread(later_ffn_in, seq_count, ffn_columns))
    token_rows = gather_far(own_rows_low, by_x, by_y)
    w_gu = gather_planes(gu_moved.reshape(plane_rows, 2 * slice_width))
    down_low = spread(ffn_out, seq_count, out_columns)

    def normed_token_rows(token_rows, inverses):
        return [
            low(part.astype(jnp.float32) * inverse[:, None] * gain_vals[0])
            for part, inverse in zip(token_rows, inverses)
        ]

    def attention(token_rows, w_heads, down_low):
        w_qkv = w_heads[:, : 2 * HEAD]
        down_moved = exchange(down_low)
        inverses = [
            lax.rsqrt(jnp.mean(jnp.square(part.astype(jnp.float32)), axis=1) + eps_norm)
            for part in token_rows
        ]
        projected = jnp.concatenate(
            [dot(part, w_qkv) for part in normed_token_rows(token_rows, inverses)], axis=0
        )
        kv_own = low(turn(projected[:, HEAD:], kv_cosine, kv_sine))
        kv_other = swap_cores(kv_own)
        queries = to_groups(low(turn(projected[:, :HEAD], cosine, sine)))
        keys = to_groups(jnp.where(key_core, kv_own, kv_other))
        values = to_groups(jnp.where(key_core, kv_other, kv_own))
        mixed, weights, slopes = attend(queries, keys, values, places)
        mixed, down_moved = tie((mixed, down_moved))
        mixed_rows = in_two(from_groups(mixed))
        down_rows = [
            part.reshape(-1, slice_width) for part in (down_moved[:, :cut], down_moved[:, cut:])
        ]
        turn_tables = [to_groups(cosine), to_groups(sine)]
        state = (queries, keys, values, weights, slopes)
        return down_rows, inverses, state, mixed_rows, turn_tables

    down_rows, inverses, state, mixed_rows, turn_tables = in_order(
        attention, token_rows, w_heads, down_low
    )
    w_down0, w_down1 = gather_planes(down_rows[0]), gather_planes(down_rows[1])

    def attention_out(mixed_rows, w_heads, tokens, cotangent):
        w_o = w_heads[:, 2 * HEAD :]
        grad_parts = to_parts(cotangent.reshape(all_rows, model_width))
        own, by_x, by_y = sum_far(*pair_products(*mixed_rows, w_o))
        by_x, by_y, *grad_parts = tie((permute(by_x, 2), permute(by_y, 4), *grad_parts))
        branch, middle, normed_three = norm_call(
            middle_kernel,
            "middle",
            all_rows,
            model_width,
            [own, by_x, by_y, tokens.reshape(all_rows, model_width)],
            [gain_vals[1:2], gain_vals[2:3]],
            [jnp.float32, jnp.float32, jnp.bfloat16],
        )
        norm_rows = jnp.concatenate(gather_pieces(normed_three), axis=0)
        return branch, middle, norm_rows, grad_parts

    branch, middle, norm_rows, grad_parts = in_order(
        attention_out, mixed_rows, w_heads, tokens, cotangent
    )
    queries, keys, values, weights, slopes = state

    def feed_up(norm_rows, w_gu):
        return glu_rows(norm_rows, w_gu)

    gate_up, hidden = in_order(feed_up, norm_rows, w_gu)

    def feed_down(hidden, w_down0):
        return sum_products(*in_two(hidden), w_down0)

    ffn0 = in_order(feed_down, hidden, w_down0)
    gain_parts = to_parts(gain_vals[3:])

    def feed_end(hidden, w_down1, ffn0, grad_parts):
        ffn1 = sum_products(*in_two(hidden), w_down1)
        ffns = [ffn0, ffn1]
        squares = sum(jnp.sum(part * part, axis=1, keepdims=True) for part in ffns)
        inverse = lax.rsqrt(squares / model_width + eps_norm)
        tops = [part.astype(jnp.float32) for part in grad_parts]
        scaled_tops = [top * gain for top, gain in zip(tops, gain_parts)]
        inner = sum(
            jnp.sum(top * part, axis=1, keepdims=True) for top, part in zip(scaled_tops, ffns)
        )
        pull = inverse * inverse * inverse * (inner / model_width)
        d_ffns = [low(top * inverse - part * pull) for top, part in zip(scaled_tops, ffns)]
        first = jnp.concatenate(gather_pieces(d_ffns[1]), axis=0)
        return ffn1, inverse, gather_near(d_ffns[0]), first, low(contract_rows(first, hidden))

    ffn1, inverse, second_near, first, grad_down1 = in_order(feed_end, hidden, w_down1, ffn0, grad_parts)

    down_part1 = sum_planes(grad_down1)

    def feed_back(second_near, hidden):
        second = jnp.concatenate(gather_far(*second_near), axis=0)
        return second, low(contract_rows(second, hidden))

    second, grad_down0 = in_order(feed_back, second_near, hidden)
    down_part0 = sum_planes(grad_down0)

    def feed_back_rows(second, first, gate_up, norm_rows, w_down0, w_down1, w_gu, down_part1):
        second, down_part1 = tie((second, down_part1))
        d_gate_up = glu_back_rows(second, first, w_down0, w_down1, gate_up)
        moved = permute(low(contract_cols(d_gate_up[d_gate_up.shape[0] // 2 :], w_gu)), 1)
        grad_gate = low(contract_rows(norm_rows, d_gate_up[:, :slice_width]))
        return d_gate_up, moved, with_layout_constraint(grad_gate, Layout((0, 1))), down_part1

    d_gate_up, d_norm_moved, grad_gate, down_part1 = in_order(
        feed_back_rows, second, first, gate_up, norm_rows, w_down0, w_down1, w_gu, down_part1
    )
    gate_part = sum_planes(grad_gate)

    def middle_back(
        d_norm_moved,
        d_gate_up,
        norm_rows,
        cotangent,
        branch,
        middle,
        w_heads,
        w_gu,
    ):
        w_qkv = w_heads[:, : 2 * HEAD]
        w_pair = jnp.concatenate([w_qkv, permute(w_qkv, 1)], axis=1)
        total = add_low(
            low(contract_cols(d_gate_up[: d_gate_up.shape[0] // 2], w_gu)), d_norm_moved
        )
        rows = total.shape[0] // 4
        own, by_x, by_y = sum_far(*(total[at * rows : (at + 1) * rows] for at in range(4)))
        by_x, by_y, norm_rows = tie((by_x, by_y, norm_rows))
        by_x, by_y = permute(by_x, 2), permute(by_y, 4)
        grad_upper = low(contract_rows(norm_rows, d_gate_up[:, slice_width:]))
        by_x, by_y, grad_upper, w_pair = tie((by_x, by_y, grad_upper, w_pair))
        d_middle, d_branch, d_gain_two = norm_call(
            middle_back_kernel,
            "middle_back",
            all_rows,
            model_width,
            [own, by_x, by_y, cotangent.reshape(all_rows, model_width), branch, middle],
            [gain_vals[1:2], gain_vals[2:3]],
            [jnp.float32, jnp.bfloat16, None],
        )
        return grad_upper, d_middle, d_branch, d_gain_two[0], w_pair

    grad_upper, d_middle, d_branch, d_gain_two, w_pair = in_order(
        middle_back,
        d_norm_moved,
        d_gate_up,
        norm_rows,
        cotangent,
        branch,
        middle,
        w_heads,
        w_gu,
    )
    upper_part = sum_planes(grad_upper)

    core_row = jnp.broadcast_to(index % 2, (1, 128)).astype(jnp.int32)

    def output_rows(d_branch, d_gain_two, middle, ffns, inverse, grad_parts):
        own, by_x, by_y = gather_near(d_branch)
        normeds = [part * inverse for part in ffns]
        d_gain_four = from_parts(
            [
                jnp.sum(top.astype(jnp.float32) * part, axis=0)[None]
                for top, part in zip(grad_parts, normeds)
            ]
        )[0]
        normed_four = from_parts([part * gain for part, gain in zip(normeds, gain_parts)])
        layer_out = low(middle + normed_four).reshape(tokens.shape)
        gain_rows = jnp.concatenate(
            [low(gain).reshape(grp_count, seq_count, own_rows) for gain in (d_gain_two, d_gain_four)],
            axis=2,
        )
        gain_rows = jnp.pad(gain_rows, ((0, 0), (0, 0), (0, 3 * HEAD - 2 * own_rows)))
        by_x, by_y, layer_out, gain_rows = tie((by_x, by_y, layer_out, gain_rows))
        return gather_mine(own, by_x, by_y), gain_rows, layer_out

    d_branch_mine, gain_rows, layer_out = in_order(
        output_rows, d_branch, d_gain_two, middle, [ffn0, ffn1], inverse, grad_parts
    )

    def attention_back(
        d_branch_mine,
        mixed_rows,
        w_heads,
        gate_part,
        down_parts,
        gain_rows,
        token_rows,
        inverses,
        queries,
        keys,
        values,
        weights,
        slopes,
    ):
        gate_grad = by_device(gate_part)
        d_branch_rows = [d_branch_mine, permute(d_branch_mine, 1)]
        d_mixed = to_groups(
            jnp.concatenate([low(dot(part, w_heads[:, 2 * HEAD :])) for part in d_branch_rows], axis=0)
        )
        d_query, keep, send = attend_back(
            queries, keys, values, weights, slopes, turn_tables, core_row, d_mixed
        )
        d_query, keep, send, gate_grad = tie((d_query, keep, send, gate_grad))
        d_kv = from_groups(keep) + swap_cores(from_groups(send)).astype(jnp.float32)
        d_projected = in_two(
            jnp.concatenate(
                [from_groups(d_query), low(turn(d_kv, kv_cosine, -kv_sine))], axis=1
            )
        )
        moved = permute(d_projected[1], 1)
        down_grad = exchange(
            jnp.concatenate(
                [part.reshape(seq_count, -1, slice_width) for part in down_parts], axis=1
            )
        )
        grad_out = over_rows(d_branch_rows, mixed_rows)
        grad_qkv = over_rows(normed_token_rows(token_rows, inverses), d_projected)
        grad_heads = jnp.concatenate(
            [with_layout_constraint(grad, Layout((0, 1))) for grad in (grad_qkv, grad_out)], axis=1
        )
        grad_heads = jnp.concatenate(
            [grad_heads.reshape(grp_count, plane_rows, 3 * HEAD), gain_rows], axis=1
        ).reshape(-1, 3 * HEAD)
        return d_projected[0], moved, grad_heads, gate_grad, down_grad

    d_projected, moved, grad_heads, gate_grad, down_grad = in_order(
        attention_back,
        d_branch_mine,
        mixed_rows,
        w_heads,
        gate_part,
        [down_part0, down_part1],
        gain_rows,
        token_rows,
        inverses,
        queries,
        keys,
        values,
        weights,
        slopes,
    )
    heads_part = sum_planes(grad_heads)

    def update_start(d_projected, moved, w_pair, upper_part):
        upper_grad = by_device(upper_part)
        total = low(contract_cols(jnp.concatenate([d_projected, moved], axis=1), w_pair))
        total, upper_grad = tie((total, upper_grad))
        rows = total.shape[0] // 4
        return sum_far(*(total[at * rows : (at + 1) * rows] for at in range(4))), upper_grad

    (own, by_x, by_y), upper_grad = in_order(
        update_start, d_projected, moved, w_pair, upper_part
    )
    by_x, by_y = permute(by_x, 2), permute(by_y, 4)
    gu_all = renew_wide(
        ffn_in, ffn_in_mom, ffn_in_avg, [(gate_grad, 0), (upper_grad, 0)], rate_mat
    )
    down_all = renew_wide(ffn_out, ffn_out_mom, ffn_out_avg, [(down_grad, 0)], rate_mat)
    gu_all, heads_part = tie((gu_all, heads_part))
    heads_grad = exchange(
        jnp.concatenate(
            [
                heads_part[:plane_rows].reshape(seq_count, own_rows, 3 * HEAD),
                jnp.pad(heads_part[plane_rows:, None], ((0, 0), (0, 7), (0, 0))),
            ],
            axis=1,
        )
    )
    sum_gains = jnp.sum(heads_grad[:, own_rows, : 2 * own_rows].astype(jnp.float32), axis=0)
    sum_gains = sum_gains.reshape(2, own_rows)
    (layer_grad,) = norm_call(
        input_back_kernel,
        "input_back",
        all_rows,
        model_width,
        [own, by_x, by_y, tokens.reshape(all_rows, model_width), d_middle],
        [gain_vals[:1]],
        [jnp.float32],
    )
    layer_grad = layer_grad.reshape(tokens.shape)
    qkv_all, out_all, qkv_product = renew_heads(
        heads_grad,
        (attn_in, attn_in_mom, attn_in_avg),
        (attn_out, attn_out_mom, attn_out_avg),
        rate_mat,
    )
    gu_new, gu_mom, gu_avg, gu_copy, gu_product = gu_all
    down_new, down_mom, down_avg, down_copy, _ = down_all
    out_new, out_mom, out_avg, out_copy = out_all
    qkv_new, qkv_mom, qkv_avg, qkv_copy = qkv_all
    own_gains = low(gains).astype(jnp.float32)
    sum_gain = jnp.stack(
        [
            qkv_product[:, 0] / own_gains[0],
            sum_gains[0],
            gu_product[:, 0] / own_gains[2],
            sum_gains[1],
        ]
    )
    gain_new, gain_mom, gain_avg, gain_copy = renew(
        gains, gains_mom, gains_avg, sum_gain, rate_gain
    )
    return (
        layer_out,
        layer_grad,
        qkv_new,
        qkv_mom,
        qkv_avg,
        qkv_copy,
        out_new,
        out_mom,
        out_avg,
        out_copy,
        gu_new,
        gu_mom,
        gu_avg,
        gu_copy,
        down_new,
        down_mom,
        down_avg,
        down_copy,
        gain_new,
        gain_mom,
        gain_avg,
        gain_copy,
    )


def solution(mesh):
    placed = (
        P(None, ("grp", "seq"), None),
        P(None, ("grp", "seq"), None),
        P(None, "grp"),
        P(("grp", "seq"), None),
        P(("grp", "seq"), None),
        P(("grp", "seq"), None),
        P(("grp", "seq"), None),
        P(None, ("grp", "seq")),
        P(("grp", "seq"), None),
        P(("grp", "seq"), None),
        P(("grp", "seq"), None),
        P(("grp", "seq"), None),
        P(None, ("grp", "seq")),
        P(("grp", "seq"), None),
        P(("grp", "seq"), None),
        P(("grp", "seq"), None),
        P(("grp", "seq"), None),
        P(None, ("grp", "seq")),
    )
    heads_fit = mesh.shape["seq"] == HEADS
    return jax.shard_map(
        by_heads if heads_fit else by_rows,
        mesh=mesh,
        in_specs=placed,
        out_specs=(
            P(None, ("grp", "seq"), None),
            P(None, ("grp", "seq"), None),
            P(("grp", "seq"), None),
            P(("grp", "seq"), None),
            P(("grp", "seq"), None),
            P(("grp", "seq"), None),
            P(("grp", "seq"), None),
            P(("grp", "seq"), None),
            P(("grp", "seq"), None),
            P(("grp", "seq"), None),
            P(("grp", "seq"), None),
            P(("grp", "seq"), None),
            P(("grp", "seq"), None),
            P(("grp", "seq"), None),
            P(("grp", "seq"), None),
            P(("grp", "seq"), None),
            P(("grp", "seq"), None),
            P(("grp", "seq"), None),
            P(None, ("grp", "seq")),
            P(None, ("grp", "seq")),
            P(None, ("grp", "seq")),
            P(None, ("grp", "seq")),
        ),
        check_vma=False,
    )
```
